32 devices in a mesh: tm: 8 (over y, x, core), head: 4 (over z).
Axes of the slice: x: 2, y: 2, z: 4, core: 2. Of those that a mesh axis runs over, the one named last changes fastest.
Arguments:
- frames: bfloat16 [16, 512, 5120], P('tm', None, 'head'), may hold values from -8 to 8
- taps: float32 [3, 5120], P(None, 'head'), may hold values from -3 to 3
- w_query: bfloat16 [5120, 2560], P(None, 'head')
- w_key: bfloat16 [5120, 2560], P(None, 'head')
- w_value: bfloat16 [5120, 2560], P(None, 'head'), may hold values from -0.078125 to 0.078125
- q_gain: float32 [2560], P('head'), may hold values from 0.5 to 6
- k_gain: float32 [2560], P('head'), may hold values from 0.5 to 6
Outputs:
- attended: bfloat16 [16, 512, 2560], P('tm', None, 'head')
The draws below stay inside these ranges and needn't reach their ends.
All inputs are finite; a program needn't handle non-finite values.
Results may differ from the reference program's by a relative error of at most 0.0086.
Values may be sent and summed in bfloat16 or wider, within the bound.
No kernel may reach another device: no remote copies, remote signals or barrier semaphores. Data moves between devices by JAX's collectives and lax.ppermute only.
A program may use at most 192 MiB of HBM per device.

```python
import jax
import jax.numpy as jnp
from jax import lax

D = 5120
DH = 128
HEADS = 20
TOK = 512
FRAMES = 16


def shared_weight(key):
    base = jax.random.normal(jax.random.fold_in(key, 11), (D, HEADS * DH), jnp.float32)
    return jnp.clip(base, -4.0, 4.0) * D ** (-0.5)


def draw_w_key(key, part):
    return shared_weight(key).astype(jnp.bfloat16)


def draw_w_query(key, part):
    own_part = jnp.clip(jax.random.normal(jax.random.fold_in(key, 12), (D, HEADS * DH), jnp.float32), -4.0, 4.0) * D ** (-0.5)
    return own_part.astype(jnp.bfloat16)


def draw_frames(key, part):
    drawn = jax.random.normal(jax.random.fold_in(key, 24), (FRAMES, TOK, D), jnp.float32)
    return jnp.clip(drawn, -6.0, 6.0).astype(jnp.bfloat16)


def gain_draw(key, salt):
    return jax.random.uniform(jax.random.fold_in(key, salt), (HEADS * DH,), jnp.float32, 0.5, 1.5)


def draw_q_gain(key, part):
    return gain_draw(key, 31)


def draw_k_gain(key, part):
    return gain_draw(key, 32)


def levels(own_key, shape, split, low, high):
    factor_of = 1.0
    for position, parts in split:
        draws = jax.random.uniform(jax.random.fold_in(jax.random.fold_in(own_key, 6), position), (parts,), jnp.float32, low / len(split), high / len(split))
        factor_of = factor_of * jnp.repeat(jnp.exp(draws), shape[position] // parts).reshape((-1,) + (1,) * (len(shape) - 1 - position))
    return factor_of


def scatter_about(rng, extent, scale, reach, pieces=(), dtype=jnp.bfloat16):
    level = levels(rng, extent, pieces, -0.22, 0.18) if pieces else 1.0
    entries = jax.random.normal(rng, extent, jnp.float32) * scale * level
    return jnp.minimum(jnp.maximum(entries, -reach), reach).astype(dtype)


def setup_inputs(seed: int = 0) -> dict:
    splits = jax.random.split(jax.random.key(seed), 8)
    frames = draw_frames(jax.random.fold_in(splits[7], 71), 0)
    taps = scatter_about(splits[1], (3, D), 0.5, 3.0, ((1, 4),), jnp.float32)
    w_query = draw_w_query(jax.random.fold_in(splits[7], 71), 0)
    w_key = draw_w_key(jax.random.fold_in(splits[7], 71), 0)
    w_value = scatter_about(splits[4], (D, HEADS * DH), D ** -0.5, 0.078125, ((1, 4),))
    q_gain = draw_q_gain(jax.random.fold_in(splits[7], 71), 0)
    k_gain = draw_k_gain(jax.random.fold_in(splits[7], 71), 0)
    return dict(frames=frames, taps=taps, w_query=w_query, w_key=w_key, w_value=w_value, q_gain=q_gain, k_gain=k_gain)


def normalize(projected, gain):
    split_heads = projected.reshape(projected.shape[0], HEADS, DH)
    mean_sq = lax.optimization_barrier(jnp.mean(split_heads * split_heads, axis=-1, keepdims=True))
    scaled = split_heads * lax.rsqrt(mean_sq + 1e-06)
    return scaled.reshape(projected.shape[0], HEADS * DH) * gain

def reference(frames, taps, w_query, w_key, w_value, q_gain, k_gain):
    frame_f = frames.astype(jnp.float32)
    zero_frame = jnp.zeros_like(frame_f[:1])
    before = jnp.concatenate([zero_frame, frame_f[:-1]], axis=0)
    after = jnp.concatenate([frame_f[1:], zero_frame], axis=0)
    mixed = (frame_f + taps[0] * before + taps[1] * frame_f + taps[2] * after).astype(jnp.bfloat16)
    tok_rows = mixed.reshape(FRAMES * TOK, D)
    q_raw = jnp.dot(tok_rows, w_query, preferred_element_type=jnp.float32)
    k_raw = jnp.dot(tok_rows, w_key, preferred_element_type=jnp.float32)
    v_raw = jnp.dot(tok_rows, w_value, preferred_element_type=jnp.float32)
    query = normalize(q_raw, q_gain).astype(jnp.bfloat16).reshape(FRAMES, TOK, HEADS, DH)
    keys = normalize(k_raw, k_gain).astype(jnp.bfloat16).reshape(FRAMES, TOK, HEADS, DH)
    values = v_raw.astype(jnp.bfloat16).reshape(FRAMES, TOK, HEADS, DH)
    prev_keys = jnp.concatenate([keys[:1], keys[:-1]], axis=0)
    prev_values = jnp.concatenate([values[:1], values[:-1]], axis=0)
    anchor_k = keys[0]
    anchor_v = values[0]
    scale = 1.0 / DH ** 0.5

    def frame_attend(items):
        q_frame, k_prev, v_prev = items
        ctx_keys = jnp.concatenate([anchor_k, k_prev], axis=0)
        ctx_vals = jnp.concatenate([anchor_v, v_prev], axis=0)
        scores = jnp.einsum('qhd,khd->hqk', q_frame.astype(jnp.float32), ctx_keys.astype(jnp.float32)) * scale
        top = lax.optimization_barrier(jnp.max(scores, axis=-1, keepdims=True))
        expo = jnp.exp(scores - top)
        probs = (expo / lax.optimization_barrier(jnp.sum(expo, axis=-1, keepdims=True))).astype(jnp.bfloat16)
        out_frame = jnp.einsum('hqk,khd->qhd', probs.astype(jnp.float32), ctx_vals.astype(jnp.float32))
        return out_frame.astype(jnp.bfloat16).reshape(TOK, HEADS * DH)
    return lax.map(frame_attend, (query, prev_keys, prev_values))
```

```python
import functools

import jax
import jax.numpy as jnp
from jax import lax
from jax.experimental import pallas as pl
from jax.experimental.pallas import tpu as pltpu
from jax.sharding import PartitionSpec as P

DH = 128
BF16 = jnp.bfloat16
F32 = jnp.float32


def whole(shape):
    return pl.BlockSpec(shape, lambda *_: (0,) * len(shape))


def norm_heads(raw, gain, heads):
    cols = []
    for h in range(heads):
        part = raw[:, h * DH : (h + 1) * DH]
        mean_sq = jnp.mean(part * part, axis=-1, keepdims=True)
        scaled = part * lax.rsqrt(mean_sq + 1e-06)
        cols.append((scaled * gain[:, h * DH : (h + 1) * DH]).astype(BF16))
    return jnp.concatenate(cols, axis=1)


def project_body(count, halves, src_ref, *refs):
    xs = refs[:count]
    wq, wk, wv, qg, kg, q_out, kv_out, acc = refs[count:]
    step = pl.program_id(0)
    weight = jnp.concatenate([wq[...], wk[...], wv[...]], axis=1)
    for i in range(count):

        @pl.when(step // halves == i)
        def _(i=i):
            part = jnp.dot(xs[i][...], weight, preferred_element_type=F32)

            if i == 0:

                @pl.when(step == 0)
                def _():
                    acc[...] = part

                @pl.when(step != 0)
                def _():
                    acc[...] += part
            else:
                acc[...] += part

    @pl.when(step == count * halves - 1)
    def _():
        width = q_out.shape[1]
        heads = width // DH
        q_out[...] = norm_heads(acc[:, :width], qg[...], heads)
        kv_out[:, :width] = norm_heads(acc[:, width : 2 * width], kg[...], heads)
        kv_out[:, width:] = acc[:, 2 * width :].astype(BF16)


def project(xs, planes, w_query, w_key, w_value, q_gain, k_gain):
    count, halves = len(xs), 2
    rows, chans = xs[0].shape
    width = w_query.shape[1]
    depth = chans // halves
    x_specs = [
        pl.BlockSpec((rows, depth), lambda k, src, i=i: (0, jnp.clip(k - halves * i, 0, halves - 1)))
        for i in range(count)
    ]
    w_spec = pl.BlockSpec((depth, width), lambda k, src: (src[k // halves] * halves + k % halves, 0))
    g_spec = pl.BlockSpec((1, width), lambda k, src: (0, 0))
    return pl.pallas_call(
        functools.partial(project_body, count, halves),
        grid_spec=pltpu.PrefetchScalarGridSpec(
            num_scalar_prefetch=1,
            grid=(count * halves,),
            in_specs=x_specs + [w_spec] * 3 + [g_spec] * 2,
            out_specs=[
                pl.BlockSpec((rows, width), lambda k, src: (0, 0)),
                pl.BlockSpec((rows, 2 * width), lambda k, src: (0, 0)),
            ],
            scratch_shapes=[pltpu.VMEM((rows, 3 * width), F32)],
        ),
        out_shape=[
            jax.ShapeDtypeStruct((rows, width), BF16),
            jax.ShapeDtypeStruct((rows, 2 * width), BF16),
        ],
        compiler_params=pltpu.CompilerParams(vmem_limit_bytes=48 * 2**20),
        cost_estimate=pl.CostEstimate(
            flops=2 * rows * count * chans * 3 * width,
            bytes_accessed=2 * count * chans * (rows + 3 * width) + 6 * rows * width,
            transcendentals=0,
        ),
        name="project",
    )(jnp.stack(planes).astype(jnp.int32), *xs, w_query, w_key, w_value, q_gain[None], k_gain[None])


def attend_body(row_block, pos_ref, q1, q2, *refs):
    keys, values, out = refs[:5], refs[5:10], refs[10]
    pos = pos_ref[0]
    slot = pl.program_id(1)

    def pick(blocks):
        own1, own2, shift1, shift2 = (blocks[i][...] for i in range(1, 5))
        for_first = jnp.where(pos == 0, own1, own2)
        for_second = jnp.where(pos == 0, own1, jnp.where(pos == 1, shift2, shift1))
        return jnp.where(slot == 0, for_first, for_second)

    factor = 1.4426950408889634 / DH**0.5
    key = jnp.concatenate([keys[0][...], pick(keys)], axis=0)
    value = jnp.concatenate([values[0][...], pick(values)], axis=0)
    rows = q1.shape[0]
    for r in range(rows // row_block):
        span = pl.ds(r * row_block, row_block)
        query = jnp.where(slot == 0, q1[span, :], q2[span, :])
        scores = lax.dot_general(query, key, (((1,), (1,)), ((), ())), preferred_element_type=F32)
        top = jnp.max(scores, axis=-1, keepdims=True)
        expo = jnp.exp2((scores - top) * factor)
        total = jnp.sum(expo, axis=-1, keepdims=True)
        result = jnp.dot(expo.astype(BF16), value, preferred_element_type=F32)
        out[0, span, :] = (result / total).astype(BF16)


def attend(pos, q1, q2, anchor, own1, own2, shift1, shift2):
    rows, width = q1.shape
    heads = width // DH
    q_spec = pl.BlockSpec((rows, DH), lambda h, f, pos: (0, h))
    k_spec = pl.BlockSpec((rows, DH), lambda h, f, pos: (0, h))
    v_spec = pl.BlockSpec((rows, DH), lambda h, f, pos: (0, heads + h))
    kv = (anchor, own1, own2, shift1, shift2)
    return pl.pallas_call(
        functools.partial(attend_body, 256),
        grid_spec=pltpu.PrefetchScalarGridSpec(
            num_scalar_prefetch=1,
            grid=(heads, 2),
            in_specs=[q_spec] * 2 + [k_spec] * 5 + [v_spec] * 5,
            out_specs=pl.BlockSpec(
                (1, rows, DH), lambda h, f, pos: (jnp.where(pos[0] == 0, f, 1 - f), 0, h)
            ),
        ),
        out_shape=jax.ShapeDtypeStruct((2, rows, width), BF16),
        compiler_params=pltpu.CompilerParams(vmem_limit_bytes=48 * 2**20),
        cost_estimate=pl.CostEstimate(
            flops=16 * heads * rows * rows * DH,
            bytes_accessed=2 * rows * width * 14,
            transcendentals=4 * heads * rows * rows,
        ),
        name="attend",
    )(pos[None].astype(jnp.int32), q1, q2, *kv, *kv)


def broadcast_first(x, axis):
    count = lax.axis_size(axis)
    mine = lax.axis_index(axis)
    step = count // 2
    held = x
    while step:
        pairs = [(i, i + step) for i in range(0, count, 2 * step)]
        got = lax.ppermute(held, axis, pairs)
        held = jnp.where(mine % (2 * step) == step, got, held)
        step //= 2
    return held


def gather_line(x, axis):
    count = lax.axis_size(axis)
    z = lax.axis_index(axis)
    ups = [(i, i + 1) for i in range(count - 1)]
    downs = [(j, i) for i, j in ups]
    up, down = [x], [x]
    for _ in range(count - 1):
        up.append(lax.ppermute(up[-1], axis, ups))
        down.append(lax.ppermute(down[-1], axis, downs))
    return [x] + [jnp.where(z + k < count, down[k], up[count - k]) for k in range(1, count)]


def mix(before, centre, after, taps):
    before, centre, after = (v.astype(F32) for v in (before, centre, after))
    return (centre + taps[0] * before + taps[1] * centre + taps[2] * after).astype(BF16)


def per_device(frames, taps, w_query, w_key, w_value, q_gain, k_gain):
    count = lax.axis_size("tm")
    pos = lax.axis_index("tm")
    planes = lax.axis_size("head")
    z = lax.axis_index("head")
    first, last = frames[0], frames[1]
    ups = [(i, i + 1) for i in range(count - 1)]
    following = lax.ppermute(first, "tm", [(j, i) for i, j in ups])
    preceding = lax.ppermute(last, "tm", ups)
    start = pos == 0
    mixed1 = mix(
        jnp.where(start, jnp.zeros_like(first), first),
        jnp.where(start, first, last),
        jnp.where(start, last, following),
        taps,
    )
    mixed2 = mix(
        jnp.where(start, first, preceding),
        jnp.where(start, last, first),
        jnp.where(start, following, last),
        taps,
    )
    order = [(z + k) % planes for k in range(planes)]
    weights = (w_query, w_key, w_value, q_gain, k_gain)
    q1, kv1 = project(gather_line(mixed1, "head"), order, *weights)
    anchor = broadcast_first(kv1, "tm")
    shift1 = lax.ppermute(kv1, "tm", [(i, i + 1) for i in range(1, count - 1)])
    q2, kv2 = project(gather_line(mixed2, "head"), order, *weights)
    shift2 = lax.ppermute(kv2, "tm", [(0, 1)])
    return attend(pos, q1, q2, anchor, kv1, kv2, shift1, shift2)


def solution(mesh):
    placed = (
        P("tm", None, "head"),
        P(None, "head"),
        P(None, "head"),
        P(None, "head"),
        P(None, "head"),
        P("head"),
        P("head"),
    )
    return jax.shard_map(
        per_device, mesh=mesh, in_specs=placed, out_specs=P("tm", None, "head"), check_vma=False
    )
```

```python
import functools

import jax
import jax.numpy as jnp
from jax import lax
from jax.experimental import pallas as pl
from jax.experimental.pallas import tpu as pltpu
from jax.sharding import PartitionSpec as P

DH = 128
BF16 = jnp.bfloat16
F32 = jnp.float32
ANY = pl.BlockSpec(memory_space=pl.ANY)


def normalized(part, gain):
    square = part * part
    high = square.astype(BF16)
    low = (square - high.astype(F32)).astype(BF16)
    ones = jnp.ones((2 * DH, DH), BF16)
    total = jnp.dot(jnp.concatenate([high, low], axis=1), ones, preferred_element_type=F32)
    return (part * lax.rsqrt(total * (1.0 / DH) + 1e-06) * gain).astype(BF16)


def store_heads(acc, qg, kg, q_out, kv_out):
    heads = q_out.shape[0]

    def columns(group, h):
        return acc[:, (group * heads + h) * DH : (group * heads + h + 1) * DH]

    for h in range(heads):
        span = slice(h * DH, (h + 1) * DH)
        q_out[h] = normalized(columns(0, h), qg[:, span])
        kv_out[0, h] = normalized(columns(1, h), kg[:, span])
        kv_out[1, h] = columns(2, h).astype(BF16)


def project_body(pairs, has_acc, final, info, *refs):
    refs = list(refs)
    count = len(pairs)
    groups = [[refs.pop(0) for _ in range(n)] for n in pairs]
    weights = [refs.pop(0) for _ in range(3)]
    gains = [refs.pop(0) for _ in range(2)] if final else None
    start = refs.pop(0) if has_acc else None
    outs = [refs.pop(0) for _ in range(2)] if final else None
    acc, xbuf, sem = refs
    step = pl.program_id(0)

    @pl.when(step == 0)
    def _():
        for i, group in enumerate(groups):
            for j, source in enumerate(group):

                @pl.when((info[0] == j) | (len(group) == 1))
                def _(i=i, source=source):
                    pltpu.make_async_copy(source, xbuf.at[i], sem.at[i]).start()

    for i in range(count):

        @pl.when(step == i)
        def _(i=i):
            pltpu.make_async_copy(groups[i][0], xbuf.at[i], sem.at[i]).wait()
            weight = jnp.concatenate([w[...] for w in weights], axis=1)
            part = jnp.dot(xbuf[i], weight, preferred_element_type=F32)
            if i == 0:
                acc[...] = part + start[...] if has_acc else part
            else:
                acc[...] += part

    if final:

        @pl.when(step == count - 1)
        def _():
            store_heads(acc, gains[0][...], gains[1][...], *outs)


def project(sources, info, weights, gains=None, acc=None):
    pairs = [len(s) for s in sources]
    count = len(pairs)
    rows, chans = sources[0][0].shape
    width = weights[0].shape[1]
    heads = width // DH
    final = gains is not None
    a_spec = pl.BlockSpec((rows, 3 * width), lambda k, info: (0, 0))
    in_specs = [ANY] * sum(pairs) + [pl.BlockSpec((chans, width), lambda k, info: (info[1 + k], 0))] * 3
    args = [x for s in sources for x in s] + list(weights)
    scratch = [pltpu.VMEM((count, rows, chans), BF16), pltpu.SemaphoreType.DMA((count,))]
    raw = jax.ShapeDtypeStruct((rows, 3 * width), F32)
    if final:
        in_specs += [pl.BlockSpec((1, width), lambda k, info: (0, 0))] * 2
        args += [g[None] for g in gains]
        out_shape = [
            jax.ShapeDtypeStruct((heads, rows, DH), BF16),
            jax.ShapeDtypeStruct((2, heads, rows, DH), BF16),
        ]
        out_specs = [
            pl.BlockSpec((heads, rows, DH), lambda k, info: (0, 0, 0)),
            pl.BlockSpec((2, heads, rows, DH), lambda k, info: (0, 0, 0, 0)),
        ]
        scratch = [pltpu.VMEM(raw.shape, F32)] + scratch
    else:
        out_shape, out_specs = raw, a_spec
    if acc is not None:
        in_specs.append(a_spec)
        args.append(acc)
    return pl.pallas_call(
        functools.partial(project_body, pairs, acc is not None, final),
        grid_spec=pltpu.PrefetchScalarGridSpec(
            num_scalar_prefetch=1,
            grid=(count,),
            in_specs=in_specs,
            out_specs=out_specs,
            scratch_shapes=scratch,
        ),
        out_shape=out_shape,
        compiler_params=pltpu.CompilerParams(vmem_limit_bytes=48 * 2**20),
        cost_estimate=pl.CostEstimate(
            flops=2 * rows * count * chans * 3 * width,
            bytes_accessed=2 * count * chans * (rows + 3 * width) + 12 * rows * width,
            transcendentals=0,
        ),
        name="project" + ("_end" if final else "_raw"),
    )(info, *args)


def attend_body(row_block, pos_ref, q1, q2, anchor, own1, own2, shift1, shift2, out):
    pos = pos_ref[0]
    slot = pl.program_id(1)

    def pick(i):
        first = jnp.where(pos == 0, own1[i, 0], own2[i, 0])
        second = jnp.where(pos == 0, own1[i, 0], jnp.where(pos == 1, shift2[i, 0], shift1[i, 0]))
        return jnp.concatenate([anchor[i, 0], jnp.where(slot == 0, first, second)], axis=0)

    factor = 1.4426950408889634 / DH**0.5
    key, value = pick(0), pick(1)
    value = jnp.concatenate([value, jnp.ones_like(value)], axis=1)
    rows = q1.shape[1]
    for r in range(rows // row_block):
        span = pl.ds(r * row_block, row_block)
        query = jnp.where(slot == 0, q1[0, span, :], q2[0, span, :])
        scores = lax.dot_general(query, key, (((1,), (1,)), ((), ())), preferred_element_type=F32)
        tops = [scores[:, c : c + DH] for c in range(0, scores.shape[1], DH)]
        top = jnp.max(functools.reduce(jnp.maximum, tops), axis=-1, keepdims=True)
        expo = jnp.exp2((scores - top) * factor).astype(BF16)
        result = jnp.dot(expo, value, preferred_element_type=F32)
        out[0, span, :] = (result[:, :DH] / result[:, DH:]).astype(BF16)


def attend(pos, q1, q2, anchor, own1, own2, shift1, shift2):
    heads, rows, _ = q1.shape
    q_spec = pl.BlockSpec((1, rows, DH), lambda h, f, pos: (h, 0, 0))
    kv_spec = pl.BlockSpec((2, 1, rows, DH), lambda h, f, pos: (0, h, 0, 0))
    return pl.pallas_call(
        functools.partial(attend_body, 128),
        grid_spec=pltpu.PrefetchScalarGridSpec(
            num_scalar_prefetch=1,
            grid=(heads, 2),
            in_specs=[q_spec] * 2 + [kv_spec] * 5,
            out_specs=pl.BlockSpec(
                (1, rows, DH), lambda h, f, pos: (jnp.where(pos[0] == 0, f, 1 - f), 0, h)
            ),
        ),
        out_shape=jax.ShapeDtypeStruct((2, rows, heads * DH), BF16),
        compiler_params=pltpu.CompilerParams(vmem_limit_bytes=32 * 2**20),
        cost_estimate=pl.CostEstimate(
            flops=16 * heads * rows * rows * DH,
            bytes_accessed=2 * heads * rows * DH * 14,
            transcendentals=4 * heads * rows * rows,
        ),
        name="attend",
    )(pos[None].astype(jnp.int32), q1, q2, anchor, own1, own2, shift1, shift2)


def broadcast_first(x, axis):
    count = lax.axis_size(axis)
    mine = lax.axis_index(axis)
    step = count // 2
    held = x
    while step:
        pairs = [(i, i + step) for i in range(0, count, 2 * step)]
        got = lax.ppermute(held, axis, pairs)
        held = jnp.where(mine % (2 * step) == step, got, held)
        step //= 2
    return held


SWAP = [(0, 1), (1, 0), (2, 3), (3, 2)]
MIDDLE = [(1, 2), (2, 1)]
OUTWARD = [(1, 0), (2, 3)]


def mix(before, centre, after, taps):
    before, centre, after = (v.astype(F32) for v in (before, centre, after))
    return (centre + taps[0] * before + taps[1] * centre + taps[2] * after).astype(BF16)


def per_device(frames, taps, w_query, w_key, w_value, q_gain, k_gain):
    count = lax.axis_size("tm")
    pos = lax.axis_index("tm")
    z = lax.axis_index("head").astype(jnp.int32)
    outer = (z == 0) | (z == 3)
    near, far = (z + 2) % 4, 3 - z
    info = jnp.stack(
        [outer.astype(jnp.int32), z, z ^ 1, jnp.where(outer, near, far), jnp.where(outer, far, near)]
    )
    first, last = frames[0], frames[1]
    ups = [(i, i + 1) for i in range(count - 1)]
    following = lax.ppermute(first, "tm", [(j, i) for i, j in ups])
    preceding = lax.ppermute(last, "tm", ups)
    start = pos == 0
    mixed1 = mix(
        jnp.where(start, jnp.zeros_like(first), first),
        jnp.where(start, first, last),
        jnp.where(start, last, following),
        taps,
    )
    mixed2 = mix(
        jnp.where(start, first, preceding),
        jnp.where(start, last, first),
        jnp.where(start, following, last),
        taps,
    )
    weights = (w_query, w_key, w_value)
    gains = (q_gain, k_gain)

    def send(x, pairs):
        return lax.ppermute(x, "head", pairs)

    swap1, middle1 = send(mixed1, SWAP), send(mixed1, MIDDLE)
    mixed2, swap1 = lax.optimization_barrier((mixed2, swap1))
    cross1, second1 = send(swap1, MIDDLE), send(middle1, OUTWARD)
    swap2, middle2 = send(mixed2, SWAP), send(mixed2, MIDDLE)
    third1 = send(cross1, OUTWARD)
    cross2, second2 = send(swap2, MIDDLE), send(middle2, OUTWARD)
    third2 = send(cross2, OUTWARD)

    q1, kv1 = project([(mixed1,), (swap1,), (middle1, second1), (cross1, third1)], info, weights, gains)
    anchor = broadcast_first(kv1, "tm")
    shift1 = lax.ppermute(kv1, "tm", [(i, i + 1) for i in range(1, count - 1)])
    raw2 = project([(mixed2,), (swap2,), (middle2, second2)], info, weights)
    info_end = jnp.stack([info[0], info[4]])
    q2, kv2 = project([(cross2, third2)], info_end, weights, gains, raw2)
    shift2 = lax.ppermute(kv2, "tm", [(0, 1)])
    return attend(pos, q1, q2, anchor, kv1, kv2, shift1, shift2)


def solution(mesh):
    placed = (
        P("tm", None, "head"),
        P(None, "head"),
        P(None, "head"),
        P(None, "head"),
        P(None, "head"),
        P("head"),
        P("head"),
    )
    return jax.shard_map(
        per_device, mesh=mesh, in_specs=placed, out_specs=P("tm", None, "head"), check_vma=False
    )
```

```python
import functools

import jax
import jax.numpy as jnp
from jax import lax
from jax.experimental import pallas as pl
from jax.experimental.pallas import tpu as pltpu
from jax.sharding import PartitionSpec as P

DH = 128
BF16 = jnp.bfloat16
F32 = jnp.float32
ANY = pl.BlockSpec(memory_space=pl.ANY)


def normalized(part, gain):
    square = part * part
    high = square.astype(BF16)
    low = (square - high.astype(F32)).astype(BF16)
    ones = jnp.ones((2 * DH, DH), BF16)
    total = jnp.dot(jnp.concatenate([high, low], axis=1), ones, preferred_element_type=F32)
    return (part * lax.rsqrt(total * (1.0 / DH) + 1e-06) * gain).astype(BF16)


def store_heads(acc, qg, kg, q_out, kv_out):
    heads = q_out.shape[0]

    def columns(group, h):
        return acc[:, (group * heads + h) * DH : (group * heads + h + 1) * DH]

    for h in range(heads):
        span = slice(h * DH, (h + 1) * DH)
        q_out[h] = normalized(columns(0, h), qg[:, span])
        kv_out[0, h] = normalized(columns(1, h), kg[:, span])
        kv_out[1, h] = columns(2, h).astype(BF16)


def project_body(pairs, extra, has_acc, final, info, *refs):
    refs = list(refs)[extra:]
    count = len(pairs)
    groups = [[refs.pop(0) for _ in range(n)] for n in pairs]
    weights = [refs.pop(0) for _ in range(3)]
    gains = [refs.pop(0) for _ in range(2)] if final else None
    start = refs.pop(0) if has_acc else None
    outs = [refs.pop(0) for _ in range(2)] if final else None
    acc, xbuf, sem = refs
    step = pl.program_id(0)

    @pl.when(step == 0)
    def _():
        for i, group in enumerate(groups):
            for j, source in enumerate(group):

                @pl.when((info[0] == j) | (len(group) == 1))
                def _(i=i, source=source):
                    pltpu.make_async_copy(source, xbuf.at[i], sem.at[i]).start()

    for i in range(count):

        @pl.when(step == i)
        def _(i=i):
            pltpu.make_async_copy(groups[i][0], xbuf.at[i], sem.at[i]).wait()
            weight = jnp.concatenate([w[...] for w in weights], axis=1)
            part = jnp.dot(xbuf[i], weight, preferred_element_type=F32)
            if i == 0:
                acc[...] = part + start[...] if has_acc else part
            else:
                acc[...] += part

    if final:

        @pl.when(step == count - 1)
        def _():
            store_heads(acc, gains[0][...], gains[1][...], *outs)


def project(sources, info, weights, gains=None, acc=None, after=(), flops=1):
    pairs = [len(s) for s in sources]
    count = len(pairs)
    rows, chans = sources[0][0].shape
    width = weights[0].shape[1]
    heads = width // DH
    final = gains is not None
    a_spec = pl.BlockSpec((rows, 3 * width), lambda k, info: (0, 0))
    in_specs = [ANY] * (len(after) + sum(pairs)) + [pl.BlockSpec((chans, width), lambda k, info: (info[1 + k], 0))] * 3
    args = list(after) + [x for s in sources for x in s] + list(weights)
    scratch = [pltpu.VMEM((count, rows, chans), BF16), pltpu.SemaphoreType.DMA((count,))]
    raw = jax.ShapeDtypeStruct((rows, 3 * width), F32)
    if final:
        in_specs += [pl.BlockSpec((1, width), lambda k, info: (0, 0))] * 2
        args += [g[None] for g in gains]
        out_shape = [
            jax.ShapeDtypeStruct((heads, rows, DH), BF16),
            jax.ShapeDtypeStruct((2, heads, rows, DH), BF16),
        ]
        out_specs = [
            pl.BlockSpec((heads, rows, DH), lambda k, info: (0, 0, 0)),
            pl.BlockSpec((2, heads, rows, DH), lambda k, info: (0, 0, 0, 0)),
        ]
        scratch = [pltpu.VMEM(raw.shape, F32)] + scratch
    else:
        out_shape, out_specs = raw, a_spec
    if acc is not None:
        in_specs.append(a_spec)
        args.append(acc)
    return pl.pallas_call(
        functools.partial(project_body, pairs, len(after), acc is not None, final),
        grid_spec=pltpu.PrefetchScalarGridSpec(
            num_scalar_prefetch=1,
            grid=(count,),
            in_specs=in_specs,
            out_specs=out_specs,
            scratch_shapes=scratch,
        ),
        out_shape=out_shape,
        compiler_params=pltpu.CompilerParams(vmem_limit_bytes=48 * 2**20),
        cost_estimate=pl.CostEstimate(flops=flops, bytes_accessed=1, transcendentals=0),
        name="project" + ("_end" if final else "_raw"),
    )(info, *args)


def attend_body(row_block, choices, fresh, info, *refs):
    refs = list(refs)
    query = refs.pop(0)
    options = [[refs.pop(0) for _ in range(n)] for n in choices]
    if not fresh:
        refs.pop(0)
    out, held, sem = refs
    h = pl.program_id(0)

    def fetch(part, source, head):
        return pltpu.make_async_copy(source.at[:, head], held.at[part, :, head], sem.at[part, head])

    @pl.when(h == 0)
    def _():
        for head in range(held.shape[2]):
            for part in range(2):
                for j, source in enumerate(options[part]):

                    @pl.when(info[2 * part] == j)
                    def _(part=part, source=source, head=head):
                        fetch(part, source, head).start()

    for part in range(2):
        fetch(part, options[part][0], h).wait()
    factor = 1.4426950408889634 / DH**0.5
    key = jnp.concatenate([held[0, 0, h], held[1, 0, h]], axis=0)
    value = jnp.concatenate([held[0, 1, h], held[1, 1, h]], axis=0)
    value = jnp.concatenate([value, jnp.ones_like(value)], axis=1)
    rows = query.shape[1]
    for r in range(rows // row_block):
        span = pl.ds(r * row_block, row_block)
        scores = lax.dot_general(
            query[0, span, :], key, (((1,), (1,)), ((), ())), preferred_element_type=F32
        )
        tops = [scores[:, c : c + DH] for c in range(0, scores.shape[1], DH)]
        top = jnp.max(functools.reduce(jnp.maximum, tops), axis=-1, keepdims=True)
        expo = jnp.exp2((scores - top) * factor).astype(BF16)
        result = jnp.dot(expo, value, preferred_element_type=F32)
        out[0, span, :] = (result[:, :DH] / result[:, DH:]).astype(BF16)


def attend(query, anchors, anchor, options, choice, frame, partly=None):
    heads, rows, _ = query.shape
    in_specs = [pl.BlockSpec((1, rows, DH), lambda h, info: (h, 0, 0))]
    in_specs += [ANY] * (len(anchors) + len(options))
    args = [query, *anchors, *options]
    aliases = {}
    if partly is not None:
        in_specs.append(ANY)
        aliases = {1 + len(args): 0}
        args.append(partly)
    return pl.pallas_call(
        functools.partial(attend_body, 128, (len(anchors), len(options)), partly is None),
        grid_spec=pltpu.PrefetchScalarGridSpec(
            num_scalar_prefetch=1,
            grid=(heads,),
            in_specs=in_specs,
            out_specs=pl.BlockSpec((1, rows, DH), lambda h, info: (info[1], 0, h)),
            scratch_shapes=[
                pltpu.VMEM((2, 2, heads, rows, DH), BF16),
                pltpu.SemaphoreType.DMA((2, heads)),
            ],
        ),
        out_shape=jax.ShapeDtypeStruct((2, rows, heads * DH), BF16),
        input_output_aliases=aliases,
        compiler_params=pltpu.CompilerParams(vmem_limit_bytes=32 * 2**20),
        cost_estimate=pl.CostEstimate(
            flops=8 * heads * rows * rows * DH,
            bytes_accessed=2 * heads * rows * DH * 6,
            transcendentals=2 * heads * rows * rows,
        ),
        name="attend",
    )(jnp.stack([anchor, frame, choice]).astype(jnp.int32), *args)


def broadcast_first(x, axis):
    count = lax.axis_size(axis)
    mine = lax.axis_index(axis)
    held = x
    for to in range(2, count, 2):
        held = jnp.where(mine == to, lax.ppermute(x, axis, [(0, to)]), held)
    other = lax.ppermute(held, axis, [(i, i + 1) for i in range(0, count, 2)])
    return held, other


SWAP = [(0, 1), (1, 0), (2, 3), (3, 2)]
INWARD = [(0, 1), (3, 2)]
MIDDLE = [(1, 2), (2, 1)]
OUTWARD = [(1, 0), (2, 3)]


def mix(before, centre, after, taps):
    before, centre, after = (v.astype(F32) for v in (before, centre, after))
    return (centre + taps[0] * before + taps[1] * centre + taps[2] * after).astype(BF16)


def per_device(frames, taps, w_query, w_key, w_value, q_gain, k_gain):
    count = lax.axis_size("tm")
    pos = lax.axis_index("tm")
    z = lax.axis_index("head").astype(jnp.int32)
    outer = (z == 0) | (z == 3)
    near, far = (z + 2) % 4, 3 - z
    info = jnp.stack(
        [outer.astype(jnp.int32), z, z ^ 1, jnp.where(outer, near, far), jnp.where(outer, far, near)]
    )
    first, last = frames[0], frames[1]
    ups = [(i, i + 1) for i in range(count - 1)]
    start = pos == 0
    following = lax.ppermute(first, "tm", [(j, i) for i, j in ups])
    mixed1 = mix(
        jnp.where(start, jnp.zeros_like(first), first),
        jnp.where(start, first, last),
        jnp.where(start, last, following),
        taps,
    )
    _, held_last = lax.optimization_barrier((mixed1, last))
    preceding = lax.ppermute(held_last, "tm", ups)
    mixed2 = mix(
        jnp.where(start, first, preceding),
        jnp.where(start, last, first),
        jnp.where(start, following, last),
        taps,
    )
    weights = (w_query, w_key, w_value)
    gains = (q_gain, k_gain)

    def send(x, pairs):
        return lax.ppermute(x, "head", pairs)

    swap1, middle1 = send(mixed1, SWAP), send(mixed1, MIDDLE)
    swap1, middle1 = lax.optimization_barrier((swap1, middle1))
    cross1, second1 = send(swap1, MIDDLE), send(middle1, OUTWARD)
    mixed2, cross1, second1 = lax.optimization_barrier((mixed2, cross1, second1))
    third1, inward2, middle2 = send(cross1, OUTWARD), send(mixed2, INWARD), send(mixed2, MIDDLE)
    later2, inward2 = lax.optimization_barrier((mixed2, inward2))
    cross2, first2 = send(inward2, MIDDLE), send(later2, OUTWARD)
    second2, third2 = send(middle2, OUTWARD), send(cross2, OUTWARD)

    sources1 = [(mixed1,), (swap1,), (middle1, second1), (cross1, third1)]
    q1, kv1 = project(sources1, info, weights, gains, after=(inward2, middle2))
    kv1, first2 = lax.optimization_barrier((kv1, first2))
    anchor = broadcast_first(kv1, "tm")
    shift1 = lax.ppermute(kv1, "tm", [(i, i + 1) for i in range(1, count - 1)])
    raw2 = project([(mixed2,), (inward2, first2), (middle2, second2)], info, weights)
    info_end = jnp.stack([info[0], info[4]])
    q2, kv2 = project([(cross2, third2)], info_end, weights, gains, raw2)
    shift2 = lax.ppermute(kv2, "tm", [(0, 1)])
    late = jnp.where(start, 0, 1)
    odd = pos % 2
    result = attend(q1, anchor, odd, [kv1, kv2], late, late)
    choice = jnp.minimum(pos, 1) + (pos == 1)
    return attend(q2, anchor, odd, [kv1, shift1, shift2], choice, 1 - late, result)


def solution(mesh):
    placed = (
        P("tm", None, "head"),
        P(None, "head"),
        P(None, "head"),
        P(None, "head"),
        P(None, "head"),
        P("head"),
        P("head"),
    )
    return jax.shard_map(
        per_device, mesh=mesh, in_specs=placed, out_specs=P("tm", None, "head"), check_vma=False
    )
```

```python
import functools

import jax
import jax.numpy as jnp
from jax import lax
from jax.experimental import pallas as pl
from jax.experimental.pallas import tpu as pltpu
from jax.sharding import PartitionSpec as P

DH = 128
BF16 = jnp.bfloat16
F32 = jnp.float32
ANY = pl.BlockSpec(memory_space=pl.ANY)


def normalized(part, gain):
    square = part * part
    high = square.astype(BF16)
    low = (square - high.astype(F32)).astype(BF16)
    ones = jnp.ones((2 * DH, DH), BF16)
    total = jnp.dot(jnp.concatenate([high, low], axis=1), ones, preferred_element_type=F32)
    return (part * lax.rsqrt(total * (1.0 / DH) + 1e-06) * gain).astype(BF16)


def store_heads(acc, qg, kg, q_out, kv_out):
    heads = q_out.shape[0]

    def columns(group, h):
        return acc[:, (group * heads + h) * DH : (group * heads + h + 1) * DH]

    for h in range(heads):
        span = slice(h * DH, (h + 1) * DH)
        q_out[h] = normalized(columns(0, h), qg[:, span])
        kv_out[0, h] = normalized(columns(1, h), kg[:, span])
        kv_out[1, h] = columns(2, h).astype(BF16)


def project_body(pairs, extra, has_acc, final, info, *refs):
    refs = list(refs)[extra:]
    count = len(pairs)
    groups = [[refs.pop(0) for _ in range(n)] for n in pairs]
    weights = [refs.pop(0) for _ in range(3)]
    gains = [refs.pop(0) for _ in range(2)] if final else None
    start = refs.pop(0) if has_acc else None
    outs = [refs.pop(0) for _ in range(2)] if final else None
    acc, xbuf, sem = refs
    step = pl.program_id(0)

    @pl.when(step == 0)
    def _():
        for i, group in enumerate(groups):
            for j, source in enumerate(group):

                @pl.when((info[0] == j) | (len(group) == 1))
                def _(i=i, source=source):
                    pltpu.make_async_copy(source, xbuf.at[i], sem.at[i]).start()

    for i in range(count):

        @pl.when(step == i)
        def _(i=i):
            pltpu.make_async_copy(groups[i][0], xbuf.at[i], sem.at[i]).wait()
            weight = jnp.concatenate([w[...] for w in weights], axis=1)
            part = jnp.dot(xbuf[i], weight, preferred_element_type=F32)
            if i == 0:
                acc[...] = part + start[...] if has_acc else part
            else:
                acc[...] += part

    if final:

        @pl.when(step == count - 1)
        def _():
            store_heads(acc, gains[0][...], gains[1][...], *outs)


def project(sources, info, weights, gains=None, acc=None, after=(), flops=1):
    pairs = [len(s) for s in sources]
    count = len(pairs)
    rows, chans = sources[0][0].shape
    width = weights[0].shape[1]
    heads = width // DH
    final = gains is not None
    a_spec = pl.BlockSpec((rows, 3 * width), lambda k, info: (0, 0))
    in_specs = [ANY] * (len(after) + sum(pairs)) + [pl.BlockSpec((chans, width), lambda k, info: (info[1 + k], 0))] * 3
    args = list(after) + [x for s in sources for x in s] + list(weights)
    scratch = [pltpu.VMEM((count, rows, chans), BF16), pltpu.SemaphoreType.DMA((count,))]
    raw = jax.ShapeDtypeStruct((rows, 3 * width), F32)
    if final:
        in_specs += [pl.BlockSpec((1, width), lambda k, info: (0, 0))] * 2
        args += [g[None] for g in gains]
        out_shape = [
            jax.ShapeDtypeStruct((heads, rows, DH), BF16),
            jax.ShapeDtypeStruct((2, heads, rows, DH), BF16),
        ]
        out_specs = [
            pl.BlockSpec((heads, rows, DH), lambda k, info: (0, 0, 0)),
            pl.BlockSpec((2, heads, rows, DH), lambda k, info: (0, 0, 0, 0)),
        ]
        scratch = [pltpu.VMEM(raw.shape, F32)] + scratch
    else:
        out_shape, out_specs = raw, a_spec
    if acc is not None:
        in_specs.append(a_spec)
        args.append(acc)
    return pl.pallas_call(
        functools.partial(project_body, pairs, len(after), acc is not None, final),
        grid_spec=pltpu.PrefetchScalarGridSpec(
            num_scalar_prefetch=1,
            grid=(count,),
            in_specs=in_specs,
            out_specs=out_specs,
            scratch_shapes=scratch,
        ),
        out_shape=out_shape,
        compiler_params=pltpu.CompilerParams(vmem_limit_bytes=48 * 2**20),
        cost_estimate=pl.CostEstimate(flops=flops, bytes_accessed=1, transcendentals=0),
        name="project" + ("_end" if final else "_raw"),
    )(info, *args)


def attend_body(row_block, choices, fresh, info, *refs):
    refs = list(refs)
    query = refs.pop(0)
    options = [[refs.pop(0) for _ in range(n)] for n in choices]
    if not fresh:
        refs.pop(0)
    out, held, sem = refs
    h = pl.program_id(0)

    def fetch(part, source, head):
        return pltpu.make_async_copy(source.at[:, head], held.at[part, :, head], sem.at[part, head])

    @pl.when(h == 0)
    def _():
        for head in range(held.shape[2]):
            for part in range(2):
                for j, source in enumerate(options[part]):

                    @pl.when(info[2 * part] == j)
                    def _(part=part, source=source, head=head):
                        fetch(part, source, head).start()

    for part in range(2):
        fetch(part, options[part][0], h).wait()
    factor = 1.4426950408889634 / DH**0.5
    key = jnp.concatenate([held[0, 0, h], held[1, 0, h]], axis=0)
    value = jnp.concatenate([held[0, 1, h], held[1, 1, h]], axis=0)
    value = jnp.concatenate([value, jnp.ones_like(value)], axis=1)
    rows = query.shape[1]
    for r in range(rows // row_block):
        span = pl.ds(r * row_block, row_block)
        scores = lax.dot_general(
            query[0, span, :], key, (((1,), (1,)), ((), ())), preferred_element_type=F32
        )
        tops = [scores[:, c : c + DH] for c in range(0, scores.shape[1], DH)]
        top = jnp.max(functools.reduce(jnp.maximum, tops), axis=-1, keepdims=True)
        expo = jnp.exp2((scores - top) * factor).astype(BF16)
        result = jnp.dot(expo, value, preferred_element_type=F32)
        out[0, span, :] = (result[:, :DH] / result[:, DH:]).astype(BF16)


def attend(query, anchors, anchor, options, choice, frame, partly=None):
    heads, rows, _ = query.shape
    in_specs = [pl.BlockSpec((1, rows, DH), lambda h, info: (h, 0, 0))]
    in_specs += [ANY] * (len(anchors) + len(options))
    args = [query, *anchors, *options]
    aliases = {}
    if partly is not None:
        in_specs.append(ANY)
        aliases = {1 + len(args): 0}
        args.append(partly)
    return pl.pallas_call(
        functools.partial(attend_body, 128, (len(anchors), len(options)), partly is None),
        grid_spec=pltpu.PrefetchScalarGridSpec(
            num_scalar_prefetch=1,
            grid=(heads,),
            in_specs=in_specs,
            out_specs=pl.BlockSpec((1, rows, DH), lambda h, info: (info[1], 0, h)),
            scratch_shapes=[
                pltpu.VMEM((2, 2, heads, rows, DH), BF16),
                pltpu.SemaphoreType.DMA((2, heads)),
            ],
        ),
        out_shape=jax.ShapeDtypeStruct((2, rows, heads * DH), BF16),
        input_output_aliases=aliases,
        compiler_params=pltpu.CompilerParams(vmem_limit_bytes=32 * 2**20),
        cost_estimate=pl.CostEstimate(
            flops=8 * heads * rows * rows * DH,
            bytes_accessed=2 * heads * rows * DH * 6,
            transcendentals=2 * heads * rows * rows,
        ),
        name="attend",
    )(jnp.stack([anchor, frame, choice]).astype(jnp.int32), *args)


def broadcast_first(x, axis):
    count = lax.axis_size(axis)
    mine = lax.axis_index(axis)
    held = x
    for to in range(2, count, 2):
        held = jnp.where(mine == to, lax.ppermute(x, axis, [(0, to)]), held)
    other = lax.ppermute(held, axis, [(i, i + 1) for i in range(0, count, 2)])
    return held, other


SWAP = [(0, 1), (1, 0), (2, 3), (3, 2)]
INWARD = [(0, 1), (3, 2)]
MIDDLE = [(1, 2), (2, 1)]
OUTWARD = [(1, 0), (2, 3)]


def mix(before, centre, after, taps):
    before, centre, after = (v.astype(F32) for v in (before, centre, after))
    return (centre + taps[0] * before + taps[1] * centre + taps[2] * after).astype(BF16)


def per_device(frames, taps, w_query, w_key, w_value, q_gain, k_gain):
    count = lax.axis_size("tm")
    pos = lax.axis_index("tm")
    z = lax.axis_index("head").astype(jnp.int32)
    outer = (z == 0) | (z == 3)
    near, far = (z + 2) % 4, 3 - z
    side = outer.astype(jnp.int32)
    pair, second, third = z ^ 1, jnp.where(outer, near, far), jnp.where(outer, far, near)
    info = jnp.stack([side, z, pair, second, third])
    info_raw, info_end = jnp.stack([side, z, second, third]), jnp.stack([side, pair])
    first, last = frames[0], frames[1]
    ups = [(i, i + 1) for i in range(count - 1)]
    start = pos == 0
    following = lax.ppermute(first, "tm", [(j, i) for i, j in ups])
    mixed1 = mix(
        jnp.where(start, jnp.zeros_like(first), first),
        jnp.where(start, first, last),
        jnp.where(start, last, following),
        taps,
    )
    _, later = lax.optimization_barrier((mixed1, frames))
    preceding = lax.ppermute(later[1], "tm", ups)
    mixed2 = mix(
        jnp.where(start, first, preceding),
        jnp.where(start, last, first),
        jnp.where(start, following, last),
        taps,
    )
    weights = (w_query, w_key, w_value)
    gains = (q_gain, k_gain)

    def send(x, pairs):
        return lax.ppermute(x, "head", pairs)

    inward1, middle1, first1 = send(mixed1, INWARD), send(mixed1, MIDDLE), send(mixed1, OUTWARD)
    inward1, middle1, first1 = lax.optimization_barrier((inward1, middle1, first1))
    inward2, cross1, second1 = send(mixed2, INWARD), send(inward1, MIDDLE), send(middle1, OUTWARD)
    later2, cross1 = lax.optimization_barrier((mixed2, cross1))
    middle2 = send(later2, MIDDLE)
    cross1, second1 = lax.optimization_barrier((cross1, second1))
    third1 = send(cross1, OUTWARD)
    middle2, inward2 = lax.optimization_barrier((middle2, inward2))
    cross2, second2 = send(inward2, MIDDLE), send(middle2, OUTWARD)
    third2 = send(cross2, OUTWARD)
    later2, second2 = lax.optimization_barrier((mixed2, second2))
    first2 = send(later2, OUTWARD)

    sources1 = [(mixed1,), (inward1, first1), (middle1, second1), (cross1, third1)]
    q1, kv1 = project(sources1, info, weights, gains, after=(inward2, middle2), flops=10**10)
    anchor = broadcast_first(kv1, "tm")
    shift1 = lax.ppermute(kv1, "tm", [(i, i + 1) for i in range(1, count - 1)])
    raw2 = project([(mixed2,), (middle2, second2), (cross2, third2)], info_raw, weights, flops=10**10)
    q2, kv2 = project([(inward2, first2)], info_end, weights, gains, raw2, flops=10**10)
    shift2 = lax.ppermute(kv2, "tm", [(0, 1)])
    late = jnp.where(start, 0, 1)
    odd = pos % 2
    result = attend(q1, anchor, odd, [kv1, kv2], late, late)
    choice = jnp.minimum(pos, 1) + (pos == 1)
    return attend(q2, anchor, odd, [kv1, shift1, shift2], choice, 1 - late, result)


def solution(mesh):
    placed = (
        P("tm", None, "head"),
        P(None, "head"),
        P(None, "head"),
        P(None, "head"),
        P(None, "head"),
        P("head"),
        P("head"),
    )
    return jax.shard_map(
        per_device, mesh=mesh, in_specs=placed, out_specs=P("tm", None, "head"), check_vma=False
    )
```

```python
import functools

import jax
import jax.numpy as jnp
from jax import lax
from jax.experimental import pallas as pl
from jax.experimental.pallas import tpu as pltpu
from jax.sharding import PartitionSpec as P

DH = 128
BF16 = jnp.bfloat16
F32 = jnp.float32
ANY = pl.BlockSpec(memory_space=pl.ANY)


def normalized(part, gain):
    square = part * part
    high = square.astype(BF16)
    low = (square - high.astype(F32)).astype(BF16)
    ones = jnp.ones((2 * DH, DH), BF16)
    total = jnp.dot(jnp.concatenate([high, low], axis=1), ones, preferred_element_type=F32)
    return (part * lax.rsqrt(total * (1.0 / DH) + 1e-06) * gain).astype(BF16)


def store_heads(acc, qg, kg, q_out, kv_out):
    heads = q_out.shape[0]

    def columns(group, h):
        return acc[:, (group * heads + h) * DH : (group * heads + h + 1) * DH]

    for h in range(heads):
        span = slice(h * DH, (h + 1) * DH)
        q_out[h] = normalized(columns(0, h), qg[:, span])
        kv_out[0, h] = normalized(columns(1, h), kg[:, span])
        kv_out[1, h] = columns(2, h).astype(BF16)


def project_body(layout, extra, has_acc, final, info, *refs):
    refs = list(refs)[extra:]
    groups = [[[refs.pop(0) for _ in range(n)] for n in variants] for variants in layout]
    weights = [refs.pop(0) for _ in range(3)]
    gains = [refs.pop(0) for _ in range(2)] if final else None
    start = refs.pop(0) if has_acc else None
    outs = [refs.pop(0) for _ in range(2)] if final else None
    acc, xbuf, sem = refs
    step = pl.program_id(0)

    @pl.when(step == 0)
    def _():
        for i, group in enumerate(groups):
            for j, pieces in enumerate(group):

                @pl.when((info[0] == j) | (len(group) == 1))
                def _(i=i, pieces=pieces):
                    row = 0
                    for piece in pieces:
                        span = pl.ds(row, piece.shape[0])
                        pltpu.make_async_copy(piece, xbuf.at[i, span], sem.at[i]).start()
                        row += piece.shape[0]

    for i in range(len(groups)):

        @pl.when(step == i)
        def _(i=i):
            pltpu.make_async_copy(xbuf.at[i], xbuf.at[i], sem.at[i]).wait()
            weight = jnp.concatenate([w[...] for w in weights], axis=1)
            part = jnp.dot(xbuf[i], weight, preferred_element_type=F32)
            if i == 0:
                acc[...] = part + start[...] if has_acc else part
            else:
                acc[...] += part

    if final:

        @pl.when(step == len(groups) - 1)
        def _():
            store_heads(acc, gains[0][...], gains[1][...], *outs)


def project(sources, info, weights, gains=None, acc=None, after=(), flops=1):
    layout = [[len(variant) for variant in source] for source in sources]
    count = len(sources)
    rows = sum(piece.shape[0] for piece in sources[0][0])
    chans = sources[0][0][0].shape[1]
    width = weights[0].shape[1]
    heads = width // DH
    final = gains is not None
    a_spec = pl.BlockSpec((rows, 3 * width), lambda k, info: (0, 0))
    args = list(after) + [piece for source in sources for variant in source for piece in variant]
    in_specs = [ANY] * len(args) + [pl.BlockSpec((chans, width), lambda k, info: (info[1 + k], 0))] * 3
    args += list(weights)
    scratch = [pltpu.VMEM((count, rows, chans), BF16), pltpu.SemaphoreType.DMA((count,))]
    raw = jax.ShapeDtypeStruct((rows, 3 * width), F32)
    if final:
        in_specs += [pl.BlockSpec((1, width), lambda k, info: (0, 0))] * 2
        args += [g[None] for g in gains]
        out_shape = [
            jax.ShapeDtypeStruct((heads, rows, DH), BF16),
            jax.ShapeDtypeStruct((2, heads, rows, DH), BF16),
        ]
        out_specs = [
            pl.BlockSpec((heads, rows, DH), lambda k, info: (0, 0, 0)),
            pl.BlockSpec((2, heads, rows, DH), lambda k, info: (0, 0, 0, 0)),
        ]
        scratch = [pltpu.VMEM(raw.shape, F32)] + scratch
    else:
        out_shape, out_specs = raw, a_spec
    if acc is not None:
        in_specs.append(a_spec)
        args.append(acc)
    return pl.pallas_call(
        functools.partial(project_body, layout, len(after), acc is not None, final),
        grid_spec=pltpu.PrefetchScalarGridSpec(
            num_scalar_prefetch=1,
            grid=(count,),
            in_specs=in_specs,
            out_specs=out_specs,
            scratch_shapes=scratch,
        ),
        out_shape=out_shape,
        compiler_params=pltpu.CompilerParams(vmem_limit_bytes=48 * 2**20),
        cost_estimate=pl.CostEstimate(flops=flops, bytes_accessed=1, transcendentals=0),
        name="project" + ("_end" if final else "_raw"),
    )(info, *args)


def attend_body(row_block, choices, fresh, info, *refs):
    refs = list(refs)
    query = refs.pop(0)
    options = [[refs.pop(0) for _ in range(n)] for n in choices]
    if not fresh:
        refs.pop(0)
    out, held, sem = refs
    h = pl.program_id(0)

    def fetch(part, source, head):
        return pltpu.make_async_copy(source.at[:, head], held.at[part, :, head], sem.at[part, head])

    @pl.when(h == 0)
    def _():
        for head in range(held.shape[2]):
            for part in range(2):
                for j, source in enumerate(options[part]):

                    @pl.when(info[2 * part] == j)
                    def _(part=part, source=source, head=head):
                        fetch(part, source, head).start()

    for part in range(2):
        fetch(part, options[part][0], h).wait()
    factor = 1.4426950408889634 / DH**0.5
    key = jnp.concatenate([held[0, 0, h], held[1, 0, h]], axis=0)
    value = jnp.concatenate([held[0, 1, h], held[1, 1, h]], axis=0)
    value = jnp.concatenate([value, jnp.ones_like(value)], axis=1)
    rows = query.shape[1]
    for r in range(rows // row_block):
        span = pl.ds(r * row_block, row_block)
        scores = lax.dot_general(
            query[0, span, :], key, (((1,), (1,)), ((), ())), preferred_element_type=F32
        )
        tops = [scores[:, c : c + DH] for c in range(0, scores.shape[1], DH)]
        top = jnp.max(functools.reduce(jnp.maximum, tops), axis=-1, keepdims=True)
        expo = jnp.exp2((scores - top) * factor).astype(BF16)
        result = jnp.dot(expo, value, preferred_element_type=F32)
        out[0, span, :] = (result[:, :DH] / result[:, DH:]).astype(BF16)


def attend(query, anchors, anchor, options, choice, frame, partly=None):
    heads, rows, _ = query.shape
    in_specs = [pl.BlockSpec((1, rows, DH), lambda h, info: (h, 0, 0))]
    in_specs += [ANY] * (len(anchors) + len(options))
    args = [query, *anchors, *options]
    aliases = {}
    if partly is not None:
        in_specs.append(ANY)
        aliases = {1 + len(args): 0}
        args.append(partly)
    return pl.pallas_call(
        functools.partial(attend_body, 128, (len(anchors), len(options)), partly is None),
        grid_spec=pltpu.PrefetchScalarGridSpec(
            num_scalar_prefetch=1,
            grid=(heads,),
            in_specs=in_specs,
            out_specs=pl.BlockSpec((1, rows, DH), lambda h, info: (info[1], 0, h)),
            scratch_shapes=[
                pltpu.VMEM((2, 2, heads, rows, DH), BF16),
                pltpu.SemaphoreType.DMA((2, heads)),
            ],
        ),
        out_shape=jax.ShapeDtypeStruct((2, rows, heads * DH), BF16),
        input_output_aliases=aliases,
        compiler_params=pltpu.CompilerParams(vmem_limit_bytes=32 * 2**20),
        cost_estimate=pl.CostEstimate(
            flops=8 * heads * rows * rows * DH,
            bytes_accessed=2 * heads * rows * DH * 6,
            transcendentals=2 * heads * rows * rows,
        ),
        name="attend",
    )(jnp.stack([anchor, frame, choice]).astype(jnp.int32), *args)


def broadcast_first(x, axis):
    count = lax.axis_size(axis)
    mine = lax.axis_index(axis)
    held = x
    for to in range(2, count, 2):
        held = jnp.where(mine == to, lax.ppermute(x, axis, [(0, to)]), held)
    other = lax.ppermute(held, axis, [(i, i + 1) for i in range(0, count, 2)])
    return held, other


SWAP = [(0, 1), (1, 0), (2, 3), (3, 2)]
INWARD = [(0, 1), (3, 2)]
MIDDLE = [(1, 2), (2, 1)]
OUTWARD = [(1, 0), (2, 3)]


def mix(before, centre, after, taps):
    before, centre, after = (v.astype(F32) for v in (before, centre, after))
    return (centre + taps[0] * before + taps[1] * centre + taps[2] * after).astype(BF16)


def per_device(frames, taps, w_query, w_key, w_value, q_gain, k_gain):
    count = lax.axis_size("tm")
    pos = lax.axis_index("tm")
    z = lax.axis_index("head").astype(jnp.int32)
    outer = (z == 0) | (z == 3)
    near, far = (z + 2) % 4, 3 - z
    side = outer.astype(jnp.int32)
    pair, second, third = z ^ 1, jnp.where(outer, near, far), jnp.where(outer, far, near)
    info = jnp.stack([side, z, pair, second, third])
    info_raw, info_end = jnp.stack([side, z, second, third]), jnp.stack([side, pair])
    half = frames.shape[1] // 2
    ups = [(i, i + 1) for i in range(count - 1)]
    downs = [(j, i) for i, j in ups]
    start = pos == 0
    hold = lax.optimization_barrier
    weights = (w_query, w_key, w_value)
    gains = (q_gain, k_gain)

    def send(x, pairs):
        return lax.ppermute(x, "head", pairs)

    following, mixed1 = [], []
    held = frames
    for part in range(2):
        following.append(lax.ppermute(held[0, part * half : (part + 1) * half], "tm", downs))
        held, following[part] = hold((frames, following[part]))
    held = frames
    for part in range(2):
        rows = slice(part * half, (part + 1) * half)
        first, last = held[0, rows], held[1, rows]
        mixed1.append(
            mix(
                jnp.where(start, jnp.zeros_like(first), first),
                jnp.where(start, first, last),
                jnp.where(start, last, following[part]),
                taps,
            )
        )
        held, mixed1[part] = hold((held, mixed1[part]))
    inward1, middle1, first1, cross1, second1, third1 = ([None, None] for _ in range(6))
    for p in range(2):
        level = send(mixed1[p], INWARD), send(mixed1[p], MIDDLE), send(mixed1[p], OUTWARD)
        inward1[p], middle1[p], first1[p] = hold(level)
    _, later = hold((mixed1[1], frames))
    preceding = lax.ppermute(later[1], "tm", ups)
    after_first = jnp.concatenate(following, axis=0)
    mixed2 = mix(
        jnp.where(start, frames[0], preceding),
        jnp.where(start, frames[1], frames[0]),
        jnp.where(start, after_first, frames[1]),
        taps,
    )
    inward2 = send(mixed2, INWARD)
    for p in range(2):
        cross1[p], second1[p] = hold((send(inward1[p], MIDDLE), send(middle1[p], OUTWARD)))
        third1[p] = send(cross1[p], OUTWARD)
    later2, _ = hold((mixed2, cross1[0]))
    middle2 = send(later2, MIDDLE)
    later2, _ = hold((mixed2, cross1[1]))
    first2 = [send(later2[:half], OUTWARD)]
    middle2, inward2 = hold((middle2, inward2))
    cross2, second2 = send(inward2, MIDDLE), send(middle2, OUTWARD)
    later2, second2 = hold((mixed2, second2))
    first2.append(send(later2[half:], OUTWARD))

    sources1 = [[mixed1], [inward1, first1], [middle1, second1], [cross1, third1]]
    q1, kv1 = project(sources1, info, weights, gains, after=(inward2, middle2, first2[0]), flops=10**10)
    kv1, cross2 = hold((kv1, cross2))
    third2 = send(cross2, OUTWARD)
    anchor = broadcast_first(kv1, "tm")
    shift1 = lax.ppermute(kv1, "tm", [(i, i + 1) for i in range(1, count - 1)])
    sources2 = [[[mixed2]], [[middle2], [second2]], [[cross2], [third2]]]
    raw2 = project(sources2, info_raw, weights, flops=10**10)
    q2, kv2 = project([[[inward2], first2]], info_end, weights, gains, raw2, flops=10**10)
    shift2 = lax.ppermute(kv2, "tm", [(0, 1)])
    late = jnp.where(start, 0, 1)
    odd = pos % 2
    result = attend(q1, anchor, odd, [kv1, kv2], late, late)
    choice = jnp.minimum(pos, 1) + (pos == 1)
    return attend(q2, anchor, odd, [kv1, shift1, shift2], choice, 1 - late, result)


def solution(mesh):
    placed = (
        P("tm", None, "head"),
        P(None, "head"),
        P(None, "head"),
        P(None, "head"),
        P(None, "head"),
        P("head"),
        P("head"),
    )
    return jax.shard_map(
        per_device, mesh=mesh, in_specs=placed, out_specs=P("tm", None, "head"), check_vma=False
    )
```

```python
import functools

import jax
import jax.numpy as jnp
from jax import lax
from jax.experimental import pallas as pl
from jax.experimental.pallas import tpu as pltpu
from jax.sharding import PartitionSpec as P

DH = 128
BF16 = jnp.bfloat16
F32 = jnp.float32
ANY = pl.BlockSpec(memory_space=pl.ANY)


def normalized(part, gain):
    square = part * part
    high = square.astype(BF16)
    low = (square - high.astype(F32)).astype(BF16)
    ones = jnp.ones((2 * DH, DH), BF16)
    total = jnp.dot(jnp.concatenate([high, low], axis=1), ones, preferred_element_type=F32)
    return (part * lax.rsqrt(total * (1.0 / DH) + 1e-06) * gain).astype(BF16)


def store_heads(acc, qg, kg, q_out, kv_out):
    heads = q_out.shape[0]

    def columns(group, h):
        return acc[:, (group * heads + h) * DH : (group * heads + h + 1) * DH]

    for h in range(heads):
        span = slice(h * DH, (h + 1) * DH)
        q_out[h] = normalized(columns(0, h), qg[:, span])
        kv_out[0, h] = normalized(columns(1, h), kg[:, span])
        kv_out[1, h] = columns(2, h).astype(BF16)


def project_body(pairs, extra, has_acc, final, info, *refs):
    refs = list(refs)[extra:]
    count = len(pairs)
    groups = [[refs.pop(0) for _ in range(n)] for n in pairs]
    weights = [refs.pop(0) for _ in range(3)]
    gains = [refs.pop(0) for _ in range(2)] if final else None
    start = refs.pop(0) if has_acc else None
    outs = [refs.pop(0) for _ in range(2)] if final else None
    acc, xbuf, sem = refs
    step = pl.program_id(0)

    @pl.when(step == 0)
    def _():
        for i, group in enumerate(groups):
            for j, source in enumerate(group):

                @pl.when((info[0] == j) | (len(group) == 1))
                def _(i=i, source=source):
                    pltpu.make_async_copy(source, xbuf.at[i], sem.at[i]).start()

    for i in range(count):

        @pl.when(step == i)
        def _(i=i):
            pltpu.make_async_copy(groups[i][0], xbuf.at[i], sem.at[i]).wait()
            weight = jnp.concatenate([w[...] for w in weights], axis=1)
            part = jnp.dot(xbuf[i], weight, preferred_element_type=F32)
            if i == 0:
                acc[...] = part + start[...] if has_acc else part
            else:
                acc[...] += part

    if final:

        @pl.when(step == count - 1)
        def _():
            store_heads(acc, gains[0][...], gains[1][...], *outs)


def project(sources, info, weights, gains=None, acc=None, after=(), flops=1):
    pairs = [len(s) for s in sources]
    count = len(pairs)
    rows, chans = sources[0][0].shape
    width = weights[0].shape[1]
    heads = width // DH
    final = gains is not None
    a_spec = pl.BlockSpec((rows, 3 * width), lambda k, info: (0, 0))
    in_specs = [ANY] * (len(after) + sum(pairs)) + [pl.BlockSpec((chans, width), lambda k, info: (info[1 + k], 0))] * 3
    args = list(after) + [x for s in sources for x in s] + list(weights)
    scratch = [pltpu.VMEM((count, rows, chans), BF16), pltpu.SemaphoreType.DMA((count,))]
    raw = jax.ShapeDtypeStruct((rows, 3 * width), F32)
    if final:
        in_specs += [pl.BlockSpec((1, width), lambda k, info: (0, 0))] * 2
        args += [g[None] for g in gains]
        out_shape = [
            jax.ShapeDtypeStruct((heads, rows, DH), BF16),
            jax.ShapeDtypeStruct((2, heads, rows, DH), BF16),
        ]
        out_specs = [
            pl.BlockSpec((heads, rows, DH), lambda k, info: (0, 0, 0)),
            pl.BlockSpec((2, heads, rows, DH), lambda k, info: (0, 0, 0, 0)),
        ]
        scratch = [pltpu.VMEM(raw.shape, F32)] + scratch
    else:
        out_shape, out_specs = raw, a_spec
    if acc is not None:
        in_specs.append(a_spec)
        args.append(acc)
    return pl.pallas_call(
        functools.partial(project_body, pairs, len(after), acc is not None, final),
        grid_spec=pltpu.PrefetchScalarGridSpec(
            num_scalar_prefetch=1,
            grid=(count,),
            in_specs=in_specs,
            out_specs=out_specs,
            scratch_shapes=scratch,
        ),
        out_shape=out_shape,
        compiler_params=pltpu.CompilerParams(vmem_limit_bytes=48 * 2**20),
        cost_estimate=pl.CostEstimate(flops=flops, bytes_accessed=1, transcendentals=0),
        name="project" + ("_end" if final else "_raw"),
    )(info, *args)


def attend_body(row_block, choices, fresh, info, *refs):
    refs = list(refs)
    query = refs.pop(0)
    options = [[refs.pop(0) for _ in range(n)] for n in choices]
    if not fresh:
        refs.pop(0)
    out, held, sem = refs
    h = pl.program_id(0)

    def fetch(part, source, head):
        return pltpu.make_async_copy(source.at[:, head], held.at[part, :, head], sem.at[part, head])

    @pl.when(h == 0)
    def _():
        for head in range(held.shape[2]):
            for part in range(2):
                for j, source in enumerate(options[part]):

                    @pl.when(info[2 * part] == j)
                    def _(part=part, source=source, head=head):
                        fetch(part, source, head).start()

    for part in range(2):
        fetch(part, options[part][0], h).wait()
    factor = 1.4426950408889634 / DH**0.5
    key = jnp.concatenate([held[0, 0, h], held[1, 0, h]], axis=0)
    value = jnp.concatenate([held[0, 1, h], held[1, 1, h]], axis=0)
    value = jnp.concatenate([value, jnp.ones_like(value)], axis=1)
    rows = query.shape[1]
    for r in range(rows // row_block):
        span = pl.ds(r * row_block, row_block)
        scores = lax.dot_general(
            query[0, span, :], key, (((1,), (1,)), ((), ())), preferred_element_type=F32
        )
        tops = [scores[:, c : c + DH] for c in range(0, scores.shape[1], DH)]
        top = jnp.max(functools.reduce(jnp.maximum, tops), axis=-1, keepdims=True)
        expo = jnp.exp2((scores - top) * factor).astype(BF16)
        result = jnp.dot(expo, value, preferred_element_type=F32)
        out[0, span, :] = (result[:, :DH] / result[:, DH:]).astype(BF16)


def attend(query, anchors, anchor, options, choice, frame, partly=None):
    heads, rows, _ = query.shape
    in_specs = [pl.BlockSpec((1, rows, DH), lambda h, info: (h, 0, 0))]
    in_specs += [ANY] * (len(anchors) + len(options))
    args = [query, *anchors, *options]
    aliases = {}
    if partly is not None:
        in_specs.append(ANY)
        aliases = {1 + len(args): 0}
        args.append(partly)
    return pl.pallas_call(
        functools.partial(attend_body, 128, (len(anchors), len(options)), partly is None),
        grid_spec=pltpu.PrefetchScalarGridSpec(
            num_scalar_prefetch=1,
            grid=(heads,),
            in_specs=in_specs,
            out_specs=pl.BlockSpec((1, rows, DH), lambda h, info: (info[1], 0, h)),
            scratch_shapes=[
                pltpu.VMEM((2, 2, heads, rows, DH), BF16),
                pltpu.SemaphoreType.DMA((2, heads)),
            ],
        ),
        out_shape=jax.ShapeDtypeStruct((2, rows, heads * DH), BF16),
        input_output_aliases=aliases,
        compiler_params=pltpu.CompilerParams(vmem_limit_bytes=32 * 2**20),
        cost_estimate=pl.CostEstimate(
            flops=8 * heads * rows * rows * DH,
            bytes_accessed=2 * heads * rows * DH * 6,
            transcendentals=2 * heads * rows * rows,
        ),
        name="attend",
    )(jnp.stack([anchor, frame, choice]).astype(jnp.int32), *args)


def broadcast_first(x, axis):
    count = lax.axis_size(axis)
    mine = lax.axis_index(axis)
    held = x
    for to in range(2, count, 2):
        held = jnp.where(mine == to, lax.ppermute(x, axis, [(0, to)]), held)
    other = lax.ppermute(held, axis, [(i, i + 1) for i in range(0, count, 2)])
    return held, other


SWAP = [(0, 1), (1, 0), (2, 3), (3, 2)]
INWARD = [(0, 1), (3, 2)]
MIDDLE = [(1, 2), (2, 1)]
OUTWARD = [(1, 0), (2, 3)]


def mix(before, centre, after, taps):
    before, centre, after = (v.astype(F32) for v in (before, centre, after))
    return (centre + taps[0] * before + taps[1] * centre + taps[2] * after).astype(BF16)


def per_device(frames, taps, w_query, w_key, w_value, q_gain, k_gain):
    count = lax.axis_size("tm")
    pos = lax.axis_index("tm")
    z = lax.axis_index("head").astype(jnp.int32)
    outer = (z == 0) | (z == 3)
    near, far = (z + 2) % 4, 3 - z
    side = outer.astype(jnp.int32)
    pair, second, third = z ^ 1, jnp.where(outer, near, far), jnp.where(outer, far, near)
    info = jnp.stack([side, z, pair, second, third])
    info_raw, info_end = jnp.stack([side, z, pair, second]), jnp.stack([side, third])
    hold = lax.optimization_barrier
    weights = (w_query, w_key, w_value)
    gains = (q_gain, k_gain)
    ups = [(i, i + 1) for i in range(count - 1)]
    downs = [(j, i) for i, j in ups]
    start = pos == 0
    tokens = frames.shape[1]
    flat = frames.reshape(2 * tokens, frames.shape[2])
    cuts = [0, 3 * tokens // 4, 7 * tokens // 4, 2 * tokens]

    def send(x, pairs):
        return lax.ppermute(x, "head", pairs)

    def mix_first(first, last, following, scales):
        return mix(
            jnp.where(start, jnp.zeros_like(first), first),
            jnp.where(start, first, last),
            jnp.where(start, last, following),
            scales,
        )

    def mix_second(first, last, following, preceding, scales):
        return mix(
            jnp.where(start, first, preceding),
            jnp.where(start, last, first),
            jnp.where(start, following, last),
            scales,
        )

    raw = [send(flat[: cuts[1]], OUTWARD)]
    outer_taps = send(taps, OUTWARD)
    following = lax.ppermute(frames[0], "tm", downs)
    later, following, raw[0], outer_taps = hold((frames, following, raw[0], outer_taps))
    mixed1 = mix_first(frames[0], frames[1], following, taps)
    raw.append(send(later.reshape(flat.shape)[cuts[1] : cuts[2]], OUTWARD))
    inward1, middle1 = send(mixed1, INWARD), send(mixed1, MIDDLE)
    later, _ = hold((frames, mixed1))
    preceding = lax.ppermute(later[1], "tm", ups)
    mixed2 = mix_second(frames[0], frames[1], following, preceding, taps)
    inward1, middle1, raw[1], later = hold((inward1, middle1, raw[1], frames))
    raw.append(send(later.reshape(flat.shape)[cuts[2] :], OUTWARD))
    inward2, cross1, second1 = send(mixed2, INWARD), send(inward1, MIDDLE), send(middle1, OUTWARD)
    later2, cross1 = hold((mixed2, cross1))
    middle2 = send(later2, MIDDLE)
    cross1, second1 = hold((cross1, second1))
    third1 = send(cross1, OUTWARD)
    other_first = jnp.concatenate([raw[0], raw[1][: tokens - cuts[1]]], axis=0)
    other_last = jnp.concatenate([raw[1][tokens - cuts[1] :], raw[2]], axis=0)
    other_following = lax.ppermute(other_first, "tm", downs)
    other_preceding = lax.ppermute(other_last, "tm", ups)
    first1 = mix_first(other_first, other_last, other_following, outer_taps)
    first2 = mix_second(other_first, other_last, other_following, other_preceding, outer_taps)
    middle2, inward2 = hold((middle2, inward2))
    cross2, second2 = send(inward2, MIDDLE), send(middle2, OUTWARD)

    sources1 = [(mixed1,), (inward1, first1), (middle1, second1), (cross1, third1)]
    q1, kv1 = project(sources1, info, weights, gains, after=(inward2, middle2), flops=10**10)
    kv1, cross2 = hold((kv1, cross2))
    third2 = send(cross2, OUTWARD)
    anchor = broadcast_first(kv1, "tm")
    shift1 = lax.ppermute(kv1, "tm", [(i, i + 1) for i in range(1, count - 1)])
    raw2 = project([(mixed2,), (inward2, first2), (middle2, second2)], info_raw, weights, flops=10**10)
    q2, kv2 = project([(cross2, third2)], info_end, weights, gains, raw2, flops=10**10)
    shift2 = lax.ppermute(kv2, "tm", [(0, 1)])
    late = jnp.where(start, 0, 1)
    odd = pos % 2
    result = attend(q1, anchor, odd, [kv1, kv2], late, late)
    choice = jnp.minimum(pos, 1) + (pos == 1)
    return attend(q2, anchor, odd, [kv1, shift1, shift2], choice, 1 - late, result)


def solution(mesh):
    placed = (
        P("tm", None, "head"),
        P(None, "head"),
        P(None, "head"),
        P(None, "head"),
        P(None, "head"),
        P("head"),
        P("head"),
    )
    return jax.shard_map(
        per_device, mesh=mesh, in_specs=placed, out_specs=P("tm", None, "head"), check_vma=False
    )
```

```python
import functools

import jax
import jax.numpy as jnp
from jax import lax
from jax.experimental import pallas as pl
from jax.experimental.pallas import tpu as pltpu
from jax.sharding import PartitionSpec as P

DH = 128
BF16 = jnp.bfloat16
F32 = jnp.float32
ANY = pl.BlockSpec(memory_space=pl.ANY)


def normalized(part, gain):
    square = part * part
    high = square.astype(BF16)
    low = (square - high.astype(F32)).astype(BF16)
    ones = jnp.ones((2 * DH, DH), BF16)
    total = jnp.dot(jnp.concatenate([high, low], axis=1), ones, preferred_element_type=F32)
    return (part * lax.rsqrt(total * (1.0 / DH) + 1e-06) * gain).astype(BF16)


def store_heads(acc, qg, kg, q_out, kv_out):
    heads = q_out.shape[0]

    def columns(group, h):
        return acc[:, (group * heads + h) * DH : (group * heads + h + 1) * DH]

    for h in range(heads):
        span = slice(h * DH, (h + 1) * DH)
        q_out[h] = normalized(columns(0, h), qg[:, span])
        kv_out[0, h] = normalized(columns(1, h), kg[:, span])
        kv_out[1, h] = columns(2, h).astype(BF16)


def project_body(pairs, extra, has_acc, final, info, *refs):
    refs = list(refs)[extra:]
    count = len(pairs)
    groups = [[refs.pop(0) for _ in range(n)] for n in pairs]
    weights = [refs.pop(0) for _ in range(3)]
    gains = [refs.pop(0) for _ in range(2)] if final else None
    start = refs.pop(0) if has_acc else None
    outs = [refs.pop(0) for _ in range(2)] if final else None
    acc, xbuf, sem = refs
    step = pl.program_id(0)

    @pl.when(step == 0)
    def _():
        for i, group in enumerate(groups):
            for j, source in enumerate(group):

                @pl.when((info[0] == j) | (len(group) == 1))
                def _(i=i, source=source):
                    pltpu.make_async_copy(source, xbuf.at[i], sem.at[i]).start()

    for i in range(count):

        @pl.when(step == i)
        def _(i=i):
            pltpu.make_async_copy(groups[i][0], xbuf.at[i], sem.at[i]).wait()
            weight = jnp.concatenate([w[...] for w in weights], axis=1)
            part = jnp.dot(xbuf[i], weight, preferred_element_type=F32)
            if i == 0:
                acc[...] = part + start[...] if has_acc else part
            else:
                acc[...] += part

    if final:

        @pl.when(step == count - 1)
        def _():
            store_heads(acc, gains[0][...], gains[1][...], *outs)


def project(sources, info, weights, gains=None, acc=None, after=(), flops=1):
    pairs = [len(s) for s in sources]
    count = len(pairs)
    rows, chans = sources[0][0].shape
    width = weights[0].shape[1]
    heads = width // DH
    final = gains is not None
    a_spec = pl.BlockSpec((rows, 3 * width), lambda k, info: (0, 0))
    in_specs = [ANY] * (len(after) + sum(pairs)) + [pl.BlockSpec((chans, width), lambda k, info: (info[1 + k], 0))] * 3
    args = list(after) + [x for s in sources for x in s] + list(weights)
    scratch = [pltpu.VMEM((count, rows, chans), BF16), pltpu.SemaphoreType.DMA((count,))]
    raw = jax.ShapeDtypeStruct((rows, 3 * width), F32)
    if final:
        in_specs += [pl.BlockSpec((1, width), lambda k, info: (0, 0))] * 2
        args += [g[None] for g in gains]
        out_shape = [
            jax.ShapeDtypeStruct((heads, rows, DH), BF16),
            jax.ShapeDtypeStruct((2, heads, rows, DH), BF16),
        ]
        out_specs = [
            pl.BlockSpec((heads, rows, DH), lambda k, info: (0, 0, 0)),
            pl.BlockSpec((2, heads, rows, DH), lambda k, info: (0, 0, 0, 0)),
        ]
        scratch = [pltpu.VMEM(raw.shape, F32)] + scratch
    else:
        out_shape, out_specs = raw, a_spec
    if acc is not None:
        in_specs.append(a_spec)
        args.append(acc)
    return pl.pallas_call(
        functools.partial(project_body, pairs, len(after), acc is not None, final),
        grid_spec=pltpu.PrefetchScalarGridSpec(
            num_scalar_prefetch=1,
            grid=(count,),
            in_specs=in_specs,
            out_specs=out_specs,
            scratch_shapes=scratch,
        ),
        out_shape=out_shape,
        compiler_params=pltpu.CompilerParams(vmem_limit_bytes=48 * 2**20),
        cost_estimate=pl.CostEstimate(flops=flops, bytes_accessed=1, transcendentals=0),
        name="project" + ("_end" if final else "_raw"),
    )(info, *args)


def attend_body(row_block, choices, fresh, info, *refs):
    refs = list(refs)
    query = refs.pop(0)
    options = [[refs.pop(0) for _ in range(n)] for n in choices]
    if not fresh:
        refs.pop(0)
    out, held, sem = refs
    h = pl.program_id(0)

    def fetch(part, source, head):
        return pltpu.make_async_copy(source.at[:, head], held.at[part, :, head], sem.at[part, head])

    @pl.when(h == 0)
    def _():
        for head in range(held.shape[2]):
            for part in range(2):
                for j, source in enumerate(options[part]):

                    @pl.when(info[2 * part] == j)
                    def _(part=part, source=source, head=head):
                        fetch(part, source, head).start()

    for part in range(2):
        fetch(part, options[part][0], h).wait()
    factor = 1.4426950408889634 / DH**0.5
    key = jnp.concatenate([held[0, 0, h], held[1, 0, h]], axis=0)
    value = jnp.concatenate([held[0, 1, h], held[1, 1, h]], axis=0)
    value = jnp.concatenate([value, jnp.ones_like(value)], axis=1)
    rows = query.shape[1]
    for r in range(rows // row_block):
        span = pl.ds(r * row_block, row_block)
        scores = lax.dot_general(
            query[0, span, :], key, (((1,), (1,)), ((), ())), preferred_element_type=F32
        )
        tops = [scores[:, c : c + DH] for c in range(0, scores.shape[1], DH)]
        top = jnp.max(functools.reduce(jnp.maximum, tops), axis=-1, keepdims=True)
        expo = jnp.exp2((scores - top) * factor).astype(BF16)
        result = jnp.dot(expo, value, preferred_element_type=F32)
        out[0, span, :] = (result[:, :DH] / result[:, DH:]).astype(BF16)


def attend(query, anchors, anchor, options, choice, frame, partly=None):
    heads, rows, _ = query.shape
    in_specs = [pl.BlockSpec((1, rows, DH), lambda h, info: (h, 0, 0))]
    in_specs += [ANY] * (len(anchors) + len(options))
    args = [query, *anchors, *options]
    aliases = {}
    if partly is not None:
        in_specs.append(ANY)
        aliases = {1 + len(args): 0}
        args.append(partly)
    return pl.pallas_call(
        functools.partial(attend_body, 128, (len(anchors), len(options)), partly is None),
        grid_spec=pltpu.PrefetchScalarGridSpec(
            num_scalar_prefetch=1,
            grid=(heads,),
            in_specs=in_specs,
            out_specs=pl.BlockSpec((1, rows, DH), lambda h, info: (info[1], 0, h)),
            scratch_shapes=[
                pltpu.VMEM((2, 2, heads, rows, DH), BF16),
                pltpu.SemaphoreType.DMA((2, heads)),
            ],
        ),
        out_shape=jax.ShapeDtypeStruct((2, rows, heads * DH), BF16),
        input_output_aliases=aliases,
        compiler_params=pltpu.CompilerParams(vmem_limit_bytes=32 * 2**20),
        cost_estimate=pl.CostEstimate(
            flops=8 * heads * rows * rows * DH,
            bytes_accessed=2 * heads * rows * DH * 6,
            transcendentals=2 * heads * rows * rows,
        ),
        name="attend",
    )(jnp.stack([anchor, frame, choice]).astype(jnp.int32), *args)


def broadcast_first(x, axis, before):
    count = lax.axis_size(axis)
    mine = lax.axis_index(axis)
    held = x
    for to in range(2, count, 2):
        held = jnp.where(mine == to, lax.ppermute(x, axis, [(0, to)]), held)
    held, before = lax.optimization_barrier((held, before))
    other = lax.ppermute(held, axis, [(i, i + 1) for i in range(0, count, 2)])
    return (held, other), before


INWARD = [(0, 1), (3, 2)]
MIDDLE = [(1, 2), (2, 1)]
OUTWARD = [(1, 0), (2, 3)]


def mix(before, centre, after, taps):
    before, centre, after = (v.astype(F32) for v in (before, centre, after))
    return (centre + taps[0] * before + taps[1] * centre + taps[2] * after).astype(BF16)


def per_device(frames, taps, w_query, w_key, w_value, q_gain, k_gain):
    count = lax.axis_size("tm")
    pos = lax.axis_index("tm")
    z = lax.axis_index("head").astype(jnp.int32)
    outer = (z == 0) | (z == 3)
    near, far = (z + 2) % 4, 3 - z
    side = outer.astype(jnp.int32)
    pair, second, third = z ^ 1, jnp.where(outer, near, far), jnp.where(outer, far, near)
    info = jnp.stack([side, z, pair, second, third])
    info_raw, info_end = jnp.stack([side, z, pair, second]), jnp.stack([side, third])
    hold = lax.optimization_barrier
    weights = (w_query, w_key, w_value)
    gains = (q_gain, k_gain)
    ups = [(i, i + 1) for i in range(count - 1)]
    downs = [(j, i) for i, j in ups]
    start = pos == 0
    cut = 3 * frames.shape[1] // 4

    def send(x, pairs):
        return lax.ppermute(x, "head", pairs)

    def mix_first(first, last, following, scales):
        return mix(
            jnp.where(start, jnp.zeros_like(first), first),
            jnp.where(start, first, last),
            jnp.where(start, last, following),
            scales,
        )

    def mix_second(first, last, following, preceding, scales):
        return mix(
            jnp.where(start, first, preceding),
            jnp.where(start, last, first),
            jnp.where(start, following, last),
            scales,
        )

    raw = [send(frames[0], OUTWARD)]
    following = lax.ppermute(frames[0], "tm", downs)
    mixed1 = mix_first(frames[0], frames[1], following, taps)
    outer_taps = send(taps, OUTWARD)
    inward1, middle1 = send(mixed1, INWARD), send(mixed1, MIDDLE)
    later, raw[0], outer_taps, _ = hold((frames, raw[0], outer_taps, mixed1))
    preceding = lax.ppermute(later[1], "tm", ups)
    raw.append(send(later[1, :cut], OUTWARD))
    mixed2 = mix_second(frames[0], frames[1], following, preceding, taps)
    inward1, middle1, raw[1], later = hold((inward1, middle1, raw[1], frames))
    inward2, cross1, second1 = send(mixed2, INWARD), send(inward1, MIDDLE), send(middle1, OUTWARD)
    raw.append(send(later[1, cut:], OUTWARD))
    later2, cross1 = hold((mixed2, cross1))
    middle2 = send(later2, MIDDLE)
    cross1, second1 = hold((cross1, second1))
    third1 = send(cross1, OUTWARD)
    other_last = jnp.concatenate(raw[1:], axis=0)
    other_following = lax.ppermute(raw[0], "tm", downs)
    other_preceding = lax.ppermute(other_last, "tm", ups)
    first1 = mix_first(raw[0], other_last, other_following, outer_taps)
    first2 = mix_second(raw[0], other_last, other_following, other_preceding, outer_taps)
    middle2, inward2 = hold((middle2, inward2))
    cross2, second2 = send(inward2, MIDDLE), send(middle2, OUTWARD)

    sources1 = [(mixed1,), (inward1, first1), (middle1, second1), (cross1, third1)]
    q1, kv1 = project(sources1, info, weights, gains, after=(inward2, middle2), flops=10**10)
    kv1, cross2 = hold((kv1, cross2))
    third2 = send(cross2, OUTWARD)
    shift1 = lax.ppermute(kv1, "tm", [(i, i + 1) for i in range(1, count - 1)])
    anchor, shift1 = broadcast_first(kv1, "tm", shift1)
    raw2 = project([(mixed2,), (inward2, first2), (middle2, second2)], info_raw, weights, flops=10**10)
    q2, kv2 = project([(cross2, third2)], info_end, weights, gains, raw2, flops=10**10)
    shift2 = lax.ppermute(kv2, "tm", [(0, 1)])
    late = jnp.where(start, 0, 1)
    odd = pos % 2
    result = attend(q1, anchor, odd, [kv1, kv2], late, late)
    choice = jnp.minimum(pos, 1) + (pos == 1)
    return attend(q2, anchor, odd, [kv1, shift1, shift2], choice, 1 - late, result)


def solution(mesh):
    placed = (
        P("tm", None, "head"),
        P(None, "head"),
        P(None, "head"),
        P(None, "head"),
        P(None, "head"),
        P("head"),
        P("head"),
    )
    return jax.shard_map(
        per_device, mesh=mesh, in_specs=placed, out_specs=P("tm", None, "head"), check_vma=False
    )
```

```python
import functools

import jax
import jax.numpy as jnp
from jax import lax
from jax.experimental import pallas as pl
from jax.experimental.pallas import tpu as pltpu
from jax.sharding import PartitionSpec as P

DH = 128
BF16 = jnp.bfloat16
F32 = jnp.float32
ANY = pl.BlockSpec(memory_space=pl.ANY)


def normalized(part, gain):
    square = part * part
    high = square.astype(BF16)
    low = (square - high.astype(F32)).astype(BF16)
    ones = jnp.ones((2 * DH, DH), BF16)
    total = jnp.dot(jnp.concatenate([high, low], axis=1), ones, preferred_element_type=F32)
    return (part * lax.rsqrt(total * (1.0 / DH) + 1e-06) * gain).astype(BF16)


def store_heads(acc, qg, kg, q_out, kv_out):
    heads = q_out.shape[0]

    def columns(group, h):
        return acc[:, (group * heads + h) * DH : (group * heads + h + 1) * DH]

    for h in range(heads):
        span = slice(h * DH, (h + 1) * DH)
        q_out[h] = normalized(columns(0, h), qg[:, span])
        kv_out[0, h] = normalized(columns(1, h), kg[:, span])
        kv_out[1, h] = columns(2, h).astype(BF16)


def project_body(pairs, extra, has_acc, final, info, *refs):
    refs = list(refs)[extra:]
    count = len(pairs)
    groups = [[refs.pop(0) for _ in range(n)] for n in pairs]
    weights = [refs.pop(0) for _ in range(3)]
    gains = [refs.pop(0) for _ in range(2)] if final else None
    start = refs.pop(0) if has_acc else None
    outs = [refs.pop(0) for _ in range(2)] if final else None
    acc, xbuf, sem = refs
    step = pl.program_id(0)

    @pl.when(step == 0)
    def _():
        for i, group in enumerate(groups):
            for j, source in enumerate(group):

                @pl.when((info[0] == j) | (len(group) == 1))
                def _(i=i, source=source):
                    pltpu.make_async_copy(source, xbuf.at[i], sem.at[i]).start()

    for i in range(count):

        @pl.when(step == i)
        def _(i=i):
            pltpu.make_async_copy(groups[i][0], xbuf.at[i], sem.at[i]).wait()
            weight = jnp.concatenate([w[...] for w in weights], axis=1)
            part = jnp.dot(xbuf[i], weight, preferred_element_type=F32)
            if i == 0:
                acc[...] = part + start[...] if has_acc else part
            else:
                acc[...] += part

    if final:

        @pl.when(step == count - 1)
        def _():
            store_heads(acc, gains[0][...], gains[1][...], *outs)


def project(sources, info, weights, gains=None, acc=None, after=(), flops=1):
    pairs = [len(s) for s in sources]
    count = len(pairs)
    rows, chans = sources[0][0].shape
    width = weights[0].shape[1]
    heads = width // DH
    final = gains is not None
    a_spec = pl.BlockSpec((rows, 3 * width), lambda k, info: (0, 0))
    in_specs = [ANY] * (len(after) + sum(pairs)) + [pl.BlockSpec((chans, width), lambda k, info: (info[1 + k], 0))] * 3
    args = list(after) + [x for s in sources for x in s] + list(weights)
    scratch = [pltpu.VMEM((count, rows, chans), BF16), pltpu.SemaphoreType.DMA((count,))]
    raw = jax.ShapeDtypeStruct((rows, 3 * width), F32)
    if final:
        in_specs += [pl.BlockSpec((1, width), lambda k, info: (0, 0))] * 2
        args += [g[None] for g in gains]
        out_shape = [
            jax.ShapeDtypeStruct((heads, rows, DH), BF16),
            jax.ShapeDtypeStruct((2, heads, rows, DH), BF16),
        ]
        out_specs = [
            pl.BlockSpec((heads, rows, DH), lambda k, info: (0, 0, 0)),
            pl.BlockSpec((2, heads, rows, DH), lambda k, info: (0, 0, 0, 0)),
        ]
        scratch = [pltpu.VMEM(raw.shape, F32)] + scratch
    else:
        out_shape, out_specs = raw, a_spec
    if acc is not None:
        in_specs.append(a_spec)
        args.append(acc)
    return pl.pallas_call(
        functools.partial(project_body, pairs, len(after), acc is not None, final),
        grid_spec=pltpu.PrefetchScalarGridSpec(
            num_scalar_prefetch=1,
            grid=(count,),
            in_specs=in_specs,
            out_specs=out_specs,
            scratch_shapes=scratch,
        ),
        out_shape=out_shape,
        compiler_params=pltpu.CompilerParams(vmem_limit_bytes=48 * 2**20),
        cost_estimate=pl.CostEstimate(flops=flops, bytes_accessed=1, transcendentals=0),
        name="project" + ("_end" if final else "_raw"),
    )(info, *args)


def attend_body(row_block, choices, fresh, info, *refs):
    refs = list(refs)
    query = refs.pop(0)
    options = [[refs.pop(0) for _ in range(n)] for n in choices]
    if not fresh:
        refs.pop(0)
    out, held, sem = refs
    h = pl.program_id(0)

    def fetch(part, source, head):
        return pltpu.make_async_copy(source.at[:, head], held.at[part, :, head], sem.at[part, head])

    @pl.when(h == 0)
    def _():
        for head in range(held.shape[2]):
            for part in range(2):
                for j, source in enumerate(options[part]):

                    @pl.when(info[2 * part] == j)
                    def _(part=part, source=source, head=head):
                        fetch(part, source, head).start()

    for part in range(2):
        fetch(part, options[part][0], h).wait()
    factor = 1.4426950408889634 / DH**0.5
    key = jnp.concatenate([held[0, 0, h], held[1, 0, h]], axis=0)
    value = jnp.concatenate([held[0, 1, h], held[1, 1, h]], axis=0)
    value = jnp.concatenate([value, jnp.ones_like(value)], axis=1)
    rows = query.shape[1]
    for r in range(rows // row_block):
        span = pl.ds(r * row_block, row_block)
        scores = lax.dot_general(
            query[0, span, :], key, (((1,), (1,)), ((), ())), preferred_element_type=F32
        )
        tops = [scores[:, c : c + DH] for c in range(0, scores.shape[1], DH)]
        top = jnp.max(functools.reduce(jnp.maximum, tops), axis=-1, keepdims=True)
        expo = jnp.exp2((scores - top) * factor).astype(BF16)
        result = jnp.dot(expo, value, preferred_element_type=F32)
        out[0, span, :] = (result[:, :DH] / result[:, DH:]).astype(BF16)


def attend(query, anchors, anchor, options, choice, frame, partly=None):
    heads, rows, _ = query.shape
    in_specs = [pl.BlockSpec((1, rows, DH), lambda h, info: (h, 0, 0))]
    in_specs += [ANY] * (len(anchors) + len(options))
    args = [query, *anchors, *options]
    aliases = {}
    if partly is not None:
        in_specs.append(ANY)
        aliases = {1 + len(args): 0}
        args.append(partly)
    return pl.pallas_call(
        functools.partial(attend_body, 128, (len(anchors), len(options)), partly is None),
        grid_spec=pltpu.PrefetchScalarGridSpec(
            num_scalar_prefetch=1,
            grid=(heads,),
            in_specs=in_specs,
            out_specs=pl.BlockSpec((1, rows, DH), lambda h, info: (info[1], 0, h)),
            scratch_shapes=[
                pltpu.VMEM((2, 2, heads, rows, DH), BF16),
                pltpu.SemaphoreType.DMA((2, heads)),
            ],
        ),
        out_shape=jax.ShapeDtypeStruct((2, rows, heads * DH), BF16),
        input_output_aliases=aliases,
        compiler_params=pltpu.CompilerParams(vmem_limit_bytes=32 * 2**20),
        cost_estimate=pl.CostEstimate(
            flops=8 * heads * rows * rows * DH,
            bytes_accessed=2 * heads * rows * DH * 6,
            transcendentals=2 * heads * rows * rows,
        ),
        name="attend",
    )(jnp.stack([anchor, frame, choice]).astype(jnp.int32), *args)


def broadcast_first(x, axis):
    count = lax.axis_size(axis)
    mine = lax.axis_index(axis)
    held = x
    for to in range(2, count, 2):
        held = jnp.where(mine == to, lax.ppermute(x, axis, [(0, to)]), held)
    return held, lax.ppermute(held, axis, [(i, i + 1) for i in range(0, count, 2)])


INWARD = [(0, 1), (3, 2)]
MIDDLE = [(1, 2), (2, 1)]
OUTWARD = [(1, 0), (2, 3)]


def mix(before, centre, after, taps):
    before, centre, after = (v.astype(F32) for v in (before, centre, after))
    return (centre + taps[0] * before + taps[1] * centre + taps[2] * after).astype(BF16)


def per_device(frames, taps, w_query, w_key, w_value, q_gain, k_gain):
    count = lax.axis_size("tm")
    pos = lax.axis_index("tm")
    z = lax.axis_index("head").astype(jnp.int32)
    outer = (z == 0) | (z == 3)
    near, far = (z + 2) % 4, 3 - z
    side = outer.astype(jnp.int32)
    pair, second, third = z ^ 1, jnp.where(outer, near, far), jnp.where(outer, far, near)
    info = jnp.stack([side, z, pair, second, third])
    info_raw, info_end = jnp.stack([side, z, pair, second]), jnp.stack([side, third])
    hold = lax.optimization_barrier
    weights = (w_query, w_key, w_value)
    gains = (q_gain, k_gain)
    ups = [(i, i + 1) for i in range(count - 1)]
    downs = [(j, i) for i, j in ups]
    start = pos == 0
    cut = 3 * frames.shape[1] // 4

    def send(x, pairs):
        return lax.ppermute(x, "head", pairs)

    def mix_first(first, last, following, scales):
        return mix(
            jnp.where(start, jnp.zeros_like(first), first),
            jnp.where(start, first, last),
            jnp.where(start, last, following),
            scales,
        )

    def mix_second(first, last, following, preceding, scales):
        return mix(
            jnp.where(start, first, preceding),
            jnp.where(start, last, first),
            jnp.where(start, following, last),
            scales,
        )

    raw = [send(frames[0], OUTWARD)]
    following = lax.ppermute(frames[0], "tm", downs)
    mixed1 = mix_first(frames[0], frames[1], following, taps)
    outer_taps = send(taps, OUTWARD)
    inward1, middle1 = send(mixed1, INWARD), send(mixed1, MIDDLE)
    later, raw[0], outer_taps, _ = hold((frames, raw[0], outer_taps, mixed1))
    preceding = lax.ppermute(later[1], "tm", ups)
    raw.append(send(later[1, :cut], OUTWARD))
    mixed2 = mix_second(frames[0], frames[1], following, preceding, taps)
    inward1, middle1, raw[1], later = hold((inward1, middle1, raw[1], frames))
    cross1, second1 = send(inward1, MIDDLE), send(middle1, OUTWARD)
    raw.append(send(later[1, cut:], OUTWARD))
    later2, cross1, second1, raw[0] = hold((mixed2, cross1, second1, raw[0]))
    middle2, inward2 = send(later2, MIDDLE), send(later2, INWARD)
    third1 = send(cross1, OUTWARD)
    other_last = jnp.concatenate(raw[1:], axis=0)
    other_following = lax.ppermute(raw[0], "tm", downs)
    other_preceding = lax.ppermute(other_last, "tm", ups)
    first1 = mix_first(raw[0], other_last, other_following, outer_taps)
    first2 = mix_second(raw[0], other_last, other_following, other_preceding, outer_taps)
    middle2, inward2, first1, first2 = hold((middle2, inward2, first1, first2))
    cross2, second2 = send(inward2, MIDDLE), send(middle2, OUTWARD)

    sources1 = [(mixed1,), (inward1, first1), (middle1, second1), (cross1, third1)]
    q1, kv1 = project(sources1, info, weights, gains, after=(inward2, middle2), flops=10**10)
    kv1, cross2 = hold((kv1, cross2))
    third2 = send(cross2, OUTWARD)
    anchor = broadcast_first(kv1, "tm")
    later1, _ = hold((kv1, anchor[0]))
    shift1 = lax.ppermute(later1, "tm", [(i, i + 1) for i in range(1, count - 1)])
    raw2 = project([(mixed2,), (inward2, first2), (middle2, second2)], info_raw, weights, flops=10**10)
    q2, kv2 = project([(cross2, third2)], info_end, weights, gains, raw2, flops=10**10)
    shift2 = lax.ppermute(kv2, "tm", [(0, 1)])
    late = jnp.where(start, 0, 1)
    odd = pos % 2
    result = attend(q1, anchor, odd, [kv1, kv2], late, late)
    choice = jnp.minimum(pos, 1) + (pos == 1)
    return attend(q2, anchor, odd, [kv1, shift1, shift2], choice, 1 - late, result)


def solution(mesh):
    placed = (
        P("tm", None, "head"),
        P(None, "head"),
        P(None, "head"),
        P(None, "head"),
        P(None, "head"),
        P("head"),
        P("head"),
    )
    return jax.shard_map(
        per_device, mesh=mesh, in_specs=placed, out_specs=P("tm", None, "head"), check_vma=False
    )
```

```python
import functools

import jax
import jax.numpy as jnp
from jax import lax
from jax.experimental import pallas as pl
from jax.experimental.pallas import tpu as pltpu
from jax.sharding import PartitionSpec as P

DH = 128
BF16 = jnp.bfloat16
F32 = jnp.float32
ANY = pl.BlockSpec(memory_space=pl.ANY)


def normalized(part, gain):
    square = part * part
    high = square.astype(BF16)
    low = (square - high.astype(F32)).astype(BF16)
    ones = jnp.ones((2 * DH, DH), BF16)
    total = jnp.dot(jnp.concatenate([high, low], axis=1), ones, preferred_element_type=F32)
    return (part * lax.rsqrt(total * (1.0 / DH) + 1e-06) * gain).astype(BF16)


def store_heads(acc, qg, kg, q_out, kv_out):
    heads = q_out.shape[0]

    def columns(group, h):
        return acc[:, (group * heads + h) * DH : (group * heads + h + 1) * DH]

    for h in range(heads):
        span = slice(h * DH, (h + 1) * DH)
        q_out[h] = normalized(columns(0, h), qg[:, span])
        kv_out[0, h] = normalized(columns(1, h), kg[:, span])
        kv_out[1, h] = columns(2, h).astype(BF16)


def project_body(pairs, extra, has_acc, final, info, *refs):
    refs = list(refs)[extra:]
    count = len(pairs)
    groups = [[refs.pop(0) for _ in range(n)] for n in pairs]
    weights = [refs.pop(0) for _ in range(3)]
    gains = [refs.pop(0) for _ in range(2)] if final else None
    start = refs.pop(0) if has_acc else None
    outs = [refs.pop(0) for _ in range(2)] if final else None
    acc, xbuf, sem = refs
    step = pl.program_id(0)

    @pl.when(step == 0)
    def _():
        for i, group in enumerate(groups):
            for j, source in enumerate(group):

                @pl.when((info[0] == j) | (len(group) == 1))
                def _(i=i, source=source):
                    pltpu.make_async_copy(source, xbuf.at[i], sem.at[i]).start()

    for i in range(count):

        @pl.when(step == i)
        def _(i=i):
            pltpu.make_async_copy(groups[i][0], xbuf.at[i], sem.at[i]).wait()
            weight = jnp.concatenate([w[...] for w in weights], axis=1)
            part = jnp.dot(xbuf[i], weight, preferred_element_type=F32)
            if i == 0:
                acc[...] = part + start[...] if has_acc else part
            else:
                acc[...] += part

    if final:

        @pl.when(step == count - 1)
        def _():
            store_heads(acc, gains[0][...], gains[1][...], *outs)


def project(sources, info, weights, gains=None, acc=None, after=(), flops=1):
    pairs = [len(s) for s in sources]
    count = len(pairs)
    rows, chans = sources[0][0].shape
    width = weights[0].shape[1]
    heads = width // DH
    final = gains is not None
    a_spec = pl.BlockSpec((rows, 3 * width), lambda k, info: (0, 0))
    in_specs = [ANY] * (len(after) + sum(pairs)) + [pl.BlockSpec((chans, width), lambda k, info: (info[1 + k], 0))] * 3
    args = list(after) + [x for s in sources for x in s] + list(weights)
    scratch = [pltpu.VMEM((count, rows, chans), BF16), pltpu.SemaphoreType.DMA((count,))]
    raw = jax.ShapeDtypeStruct((rows, 3 * width), F32)
    if final:
        in_specs += [pl.BlockSpec((1, width), lambda k, info: (0, 0))] * 2
        args += [g[None] for g in gains]
        out_shape = [
            jax.ShapeDtypeStruct((heads, rows, DH), BF16),
            jax.ShapeDtypeStruct((2, heads, rows, DH), BF16),
        ]
        out_specs = [
            pl.BlockSpec((heads, rows, DH), lambda k, info: (0, 0, 0)),
            pl.BlockSpec((2, heads, rows, DH), lambda k, info: (0, 0, 0, 0)),
        ]
        scratch = [pltpu.VMEM(raw.shape, F32)] + scratch
    else:
        out_shape, out_specs = raw, a_spec
    if acc is not None:
        in_specs.append(a_spec)
        args.append(acc)
    return pl.pallas_call(
        functools.partial(project_body, pairs, len(after), acc is not None, final),
        grid_spec=pltpu.PrefetchScalarGridSpec(
            num_scalar_prefetch=1,
            grid=(count,),
            in_specs=in_specs,
            out_specs=out_specs,
            scratch_shapes=scratch,
        ),
        out_shape=out_shape,
        compiler_params=pltpu.CompilerParams(vmem_limit_bytes=48 * 2**20),
        cost_estimate=pl.CostEstimate(flops=flops, bytes_accessed=1, transcendentals=0),
        name="project" + ("_end" if final else "_raw"),
    )(info, *args)


def attend_body(row_block, choices, fresh, info, *refs):
    refs = list(refs)
    query = refs.pop(0)
    options = [[refs.pop(0) for _ in range(n)] for n in choices]
    if not fresh:
        refs.pop(0)
    out, held, sem = refs
    h = pl.program_id(0)

    def fetch(part, source, head):
        return pltpu.make_async_copy(source.at[:, head], held.at[part, :, head], sem.at[part, head])

    @pl.when(h == 0)
    def _():
        for head in range(held.shape[2]):
            for part in range(2):
                for j, source in enumerate(options[part]):

                    @pl.when(info[2 * part] == j)
                    def _(part=part, source=source, head=head):
                        fetch(part, source, head).start()

    for part in range(2):
        fetch(part, options[part][0], h).wait()
    factor = 1.4426950408889634 / DH**0.5
    key = jnp.concatenate([held[0, 0, h], held[1, 0, h]], axis=0)
    value = jnp.concatenate([held[0, 1, h], held[1, 1, h]], axis=0)
    value = jnp.concatenate([value, jnp.ones_like(value)], axis=1)
    rows = query.shape[1]
    for r in range(rows // row_block):
        span = pl.ds(r * row_block, row_block)
        scores = lax.dot_general(
            query[0, span, :], key, (((1,), (1,)), ((), ())), preferred_element_type=F32
        )
        tops = [scores[:, c : c + DH] for c in range(0, scores.shape[1], DH)]
        top = jnp.max(functools.reduce(jnp.maximum, tops), axis=-1, keepdims=True)
        expo = jnp.exp2((scores - top) * factor).astype(BF16)
        result = jnp.dot(expo, value, preferred_element_type=F32)
        out[0, span, :] = (result[:, :DH] / result[:, DH:]).astype(BF16)


def attend(query, anchors, anchor, options, choice, frame, partly=None):
    heads, rows, _ = query.shape
    in_specs = [pl.BlockSpec((1, rows, DH), lambda h, info: (h, 0, 0))]
    in_specs += [ANY] * (len(anchors) + len(options))
    args = [query, *anchors, *options]
    aliases = {}
    if partly is not None:
        in_specs.append(ANY)
        aliases = {1 + len(args): 0}
        args.append(partly)
    return pl.pallas_call(
        functools.partial(attend_body, 128, (len(anchors), len(options)), partly is None),
        grid_spec=pltpu.PrefetchScalarGridSpec(
            num_scalar_prefetch=1,
            grid=(heads,),
            in_specs=in_specs,
            out_specs=pl.BlockSpec((1, rows, DH), lambda h, info: (info[1], 0, h)),
            scratch_shapes=[
                pltpu.VMEM((2, 2, heads, rows, DH), BF16),
                pltpu.SemaphoreType.DMA((2, heads)),
            ],
        ),
        out_shape=jax.ShapeDtypeStruct((2, rows, heads * DH), BF16),
        input_output_aliases=aliases,
        compiler_params=pltpu.CompilerParams(vmem_limit_bytes=32 * 2**20),
        cost_estimate=pl.CostEstimate(
            flops=8 * heads * rows * rows * DH,
            bytes_accessed=2 * heads * rows * DH * 6,
            transcendentals=2 * heads * rows * rows,
        ),
        name="attend",
    )(jnp.stack([anchor, frame, choice]).astype(jnp.int32), *args)


def broadcast_first(x, axis):
    count = lax.axis_size(axis)
    mine = lax.axis_index(axis)
    held = x
    for to in range(2, count, 2):
        held = jnp.where(mine == to, lax.ppermute(x, axis, [(0, to)]), held)
    return held, lax.ppermute(held, axis, [(i, i + 1) for i in range(0, count, 2)])


INWARD = [(0, 1), (3, 2)]
MIDDLE = [(1, 2), (2, 1)]
OUTWARD = [(1, 0), (2, 3)]


def mix(before, centre, after, taps):
    before, centre, after = (v.astype(F32) for v in (before, centre, after))
    return (centre + taps[0] * before + taps[1] * centre + taps[2] * after).astype(BF16)


def per_device(frames, taps, w_query, w_key, w_value, q_gain, k_gain):
    count = lax.axis_size("tm")
    pos = lax.axis_index("tm")
    z = lax.axis_index("head").astype(jnp.int32)
    outer = (z == 0) | (z == 3)
    near, far = (z + 2) % 4, 3 - z
    side = outer.astype(jnp.int32)
    pair, second, third = z ^ 1, jnp.where(outer, near, far), jnp.where(outer, far, near)
    info = jnp.stack([side, z, pair, second, third])
    info_raw, info_end = jnp.stack([side, z, pair, second]), jnp.stack([side, third])
    hold = lax.optimization_barrier
    weights = (w_query, w_key, w_value)
    gains = (q_gain, k_gain)
    ups = [(i, i + 1) for i in range(count - 1)]
    downs = [(j, i) for i, j in ups]
    start = pos == 0

    def send(x, pairs):
        return lax.ppermute(x, "head", pairs)

    def mix_first(first, last, following, scales):
        return mix(
            jnp.where(start, jnp.zeros_like(first), first),
            jnp.where(start, first, last),
            jnp.where(start, last, following),
            scales,
        )

    def mix_second(first, last, following, preceding, scales):
        return mix(
            jnp.where(start, first, preceding),
            jnp.where(start, last, first),
            jnp.where(start, following, last),
            scales,
        )

    raw_first, raw_last = send(frames[0], OUTWARD), send(frames[1], OUTWARD)
    all_taps = lax.all_gather(taps, "head", axis=0)
    outer_taps = lax.dynamic_index_in_dim(all_taps, pair, axis=0, keepdims=False)
    following = lax.ppermute(frames[0], "tm", downs)
    mixed1 = mix_first(frames[0], frames[1], following, taps)
    inward1, middle1 = send(mixed1, INWARD), send(mixed1, MIDDLE)
    later, _ = hold((frames, mixed1))
    preceding = lax.ppermute(later[1], "tm", ups)
    mixed2 = mix_second(frames[0], frames[1], following, preceding, taps)
    raw_following = lax.ppermute(raw_first, "tm", downs)
    inward1, middle1, raw_last = hold((inward1, middle1, raw_last))
    cross1, second1 = send(inward1, MIDDLE), send(middle1, OUTWARD)
    raw_preceding = lax.ppermute(raw_last, "tm", ups)
    later2, cross1, second1, raw_following = hold((mixed2, cross1, second1, raw_following))
    middle2, inward2 = send(later2, MIDDLE), send(later2, INWARD)
    third1 = send(cross1, OUTWARD)
    first1 = mix_first(raw_first, raw_last, raw_following, outer_taps)
    first2 = mix_second(raw_first, raw_last, raw_following, raw_preceding, outer_taps)
    middle2, inward2, first1, first2 = hold((middle2, inward2, first1, first2))
    cross2, second2 = send(inward2, MIDDLE), send(middle2, OUTWARD)

    sources1 = [(mixed1,), (inward1, first1), (middle1, second1), (cross1, third1)]
    q1, kv1 = project(sources1, info, weights, gains, after=(inward2, middle2), flops=10**10)
    kv1, cross2 = hold((kv1, cross2))
    third2 = send(cross2, OUTWARD)
    anchor = broadcast_first(kv1, "tm")
    later1, _ = hold((kv1, anchor[0]))
    shift1 = lax.ppermute(later1, "tm", [(i, i + 1) for i in range(1, count - 1)])
    raw2 = project([(mixed2,), (inward2, first2), (middle2, second2)], info_raw, weights, flops=10**10)
    q2, kv2 = project([(cross2, third2)], info_end, weights, gains, raw2, flops=10**10)
    shift2 = lax.ppermute(kv2, "tm", [(0, 1)])
    late = jnp.where(start, 0, 1)
    odd = pos % 2
    result = attend(q1, anchor, odd, [kv1, kv2], late, late)
    choice = jnp.minimum(pos, 1) + (pos == 1)
    return attend(q2, anchor, odd, [kv1, shift1, shift2], choice, 1 - late, result)


def solution(mesh):
    placed = (
        P("tm", None, "head"),
        P(None, "head"),
        P(None, "head"),
        P(None, "head"),
        P(None, "head"),
        P("head"),
        P("head"),
    )
    return jax.shard_map(
        per_device, mesh=mesh, in_specs=placed, out_specs=P("tm", None, "head"), check_vma=False
    )
```

```python
import functools

import jax
import jax.numpy as jnp
from jax import lax
from jax.experimental import pallas as pl
from jax.experimental.pallas import tpu as pltpu
from jax.sharding import PartitionSpec as P

DH = 128
BF16 = jnp.bfloat16
F32 = jnp.float32
ANY = pl.BlockSpec(memory_space=pl.ANY)


def normalized(part, gain):
    square = part * part
    high = square.astype(BF16)
    low = (square - high.astype(F32)).astype(BF16)
    ones = jnp.ones((2 * DH, DH), BF16)
    total = jnp.dot(jnp.concatenate([high, low], axis=1), ones, preferred_element_type=F32)
    return (part * lax.rsqrt(total * (1.0 / DH) + 1e-06) * gain).astype(BF16)


def store_heads(acc, qg, kg, q_out, kv_out):
    heads = q_out.shape[0]

    def columns(group, h):
        return acc[:, (group * heads + h) * DH : (group * heads + h + 1) * DH]

    for h in range(heads):
        span = slice(h * DH, (h + 1) * DH)
        q_out[h] = normalized(columns(0, h), qg[:, span])
        kv_out[0, h] = normalized(columns(1, h), kg[:, span])
        kv_out[1, h] = columns(2, h).astype(BF16)


def project_body(pairs, extra, has_acc, final, info, *refs):
    refs = list(refs)[extra:]
    count = len(pairs)
    groups = [[refs.pop(0) for _ in range(n)] for n in pairs]
    weights = [refs.pop(0) for _ in range(3)]
    gains = [refs.pop(0) for _ in range(2)] if final else None
    start = refs.pop(0) if has_acc else None
    outs = [refs.pop(0) for _ in range(2)] if final else None
    acc, xbuf, sem = refs
    step = pl.program_id(0)

    @pl.when(step == 0)
    def _():
        for i, group in enumerate(groups):
            for j, source in enumerate(group):

                @pl.when((info[0] == j) | (len(group) == 1))
                def _(i=i, source=source):
                    pltpu.make_async_copy(source, xbuf.at[i], sem.at[i]).start()

    for i in range(count):

        @pl.when(step == i)
        def _(i=i):
            pltpu.make_async_copy(groups[i][0], xbuf.at[i], sem.at[i]).wait()
            weight = jnp.concatenate([w[...] for w in weights], axis=1)
            part = jnp.dot(xbuf[i], weight, preferred_element_type=F32)
            if i == 0:
                acc[...] = part + start[...] if has_acc else part
            else:
                acc[...] += part

    if final:

        @pl.when(step == count - 1)
        def _():
            store_heads(acc, gains[0][...], gains[1][...], *outs)


def project(sources, info, weights, gains=None, acc=None, after=(), flops=1):
    pairs = [len(s) for s in sources]
    count = len(pairs)
    rows, chans = sources[0][0].shape
    width = weights[0].shape[1]
    heads = width // DH
    final = gains is not None
    a_spec = pl.BlockSpec((rows, 3 * width), lambda k, info: (0, 0))
    in_specs = [ANY] * (len(after) + sum(pairs)) + [pl.BlockSpec((chans, width), lambda k, info: (info[1 + k], 0))] * 3
    args = list(after) + [x for s in sources for x in s] + list(weights)
    scratch = [pltpu.VMEM((count, rows, chans), BF16), pltpu.SemaphoreType.DMA((count,))]
    raw = jax.ShapeDtypeStruct((rows, 3 * width), F32)
    if final:
        in_specs += [pl.BlockSpec((1, width), lambda k, info: (0, 0))] * 2
        args += [g[None] for g in gains]
        out_shape = [
            jax.ShapeDtypeStruct((heads, rows, DH), BF16),
            jax.ShapeDtypeStruct((2, heads, rows, DH), BF16),
        ]
        out_specs = [
            pl.BlockSpec((heads, rows, DH), lambda k, info: (0, 0, 0)),
            pl.BlockSpec((2, heads, rows, DH), lambda k, info: (0, 0, 0, 0)),
        ]
        scratch = [pltpu.VMEM(raw.shape, F32)] + scratch
    else:
        out_shape, out_specs = raw, a_spec
    if acc is not None:
        in_specs.append(a_spec)
        args.append(acc)
    return pl.pallas_call(
        functools.partial(project_body, pairs, len(after), acc is not None, final),
        grid_spec=pltpu.PrefetchScalarGridSpec(
            num_scalar_prefetch=1,
            grid=(count,),
            in_specs=in_specs,
            out_specs=out_specs,
            scratch_shapes=scratch,
        ),
        out_shape=out_shape,
        compiler_params=pltpu.CompilerParams(vmem_limit_bytes=48 * 2**20),
        cost_estimate=pl.CostEstimate(flops=flops, bytes_accessed=1, transcendentals=0),
        name="project" + ("_end" if final else "_raw"),
    )(info, *args)


def attend_body(row_block, choices, fresh, info, *refs):
    refs = list(refs)
    query = refs.pop(0)
    options = [[refs.pop(0) for _ in range(n)] for n in choices]
    if not fresh:
        refs.pop(0)
    out, held, sem = refs
    h = pl.program_id(0)

    def fetch(part, source, head):
        return pltpu.make_async_copy(source.at[:, head], held.at[part, :, head], sem.at[part, head])

    @pl.when(h == 0)
    def _():
        for head in range(held.shape[2]):
            for part in range(2):
                for j, source in enumerate(options[part]):

                    @pl.when(info[2 * part] == j)
                    def _(part=part, source=source, head=head):
                        fetch(part, source, head).start()

    for part in range(2):
        fetch(part, options[part][0], h).wait()
    factor = 1.4426950408889634 / DH**0.5
    key = jnp.concatenate([held[0, 0, h], held[1, 0, h]], axis=0)
    value = jnp.concatenate([held[0, 1, h], held[1, 1, h]], axis=0)
    value = jnp.concatenate([value, jnp.ones_like(value)], axis=1)
    rows = query.shape[1]
    for r in range(rows // row_block):
        span = pl.ds(r * row_block, row_block)
        scores = lax.dot_general(
            query[0, span, :], key, (((1,), (1,)), ((), ())), preferred_element_type=F32
        )
        tops = [scores[:, c : c + DH] for c in range(0, scores.shape[1], DH)]
        top = jnp.max(functools.reduce(jnp.maximum, tops), axis=-1, keepdims=True)
        expo = jnp.exp2((scores - top) * factor).astype(BF16)
        result = jnp.dot(expo, value, preferred_element_type=F32)
        out[0, span, :] = (result[:, :DH] / result[:, DH:]).astype(BF16)


def attend(query, anchors, anchor, options, choice, frame, partly=None):
    heads, rows, _ = query.shape
    in_specs = [pl.BlockSpec((1, rows, DH), lambda h, info: (h, 0, 0))]
    in_specs += [ANY] * (len(anchors) + len(options))
    args = [query, *anchors, *options]
    aliases = {}
    if partly is not None:
        in_specs.append(ANY)
        aliases = {1 + len(args): 0}
        args.append(partly)
    return pl.pallas_call(
        functools.partial(attend_body, 128, (len(anchors), len(options)), partly is None),
        grid_spec=pltpu.PrefetchScalarGridSpec(
            num_scalar_prefetch=1,
            grid=(heads,),
            in_specs=in_specs,
            out_specs=pl.BlockSpec((1, rows, DH), lambda h, info: (info[1], 0, h)),
            scratch_shapes=[
                pltpu.VMEM((2, 2, heads, rows, DH), BF16),
                pltpu.SemaphoreType.DMA((2, heads)),
            ],
        ),
        out_shape=jax.ShapeDtypeStruct((2, rows, heads * DH), BF16),
        input_output_aliases=aliases,
        compiler_params=pltpu.CompilerParams(vmem_limit_bytes=32 * 2**20),
        cost_estimate=pl.CostEstimate(
            flops=8 * heads * rows * rows * DH,
            bytes_accessed=2 * heads * rows * DH * 6,
            transcendentals=2 * heads * rows * rows,
        ),
        name="attend",
    )(jnp.stack([anchor, frame, choice]).astype(jnp.int32), *args)


def broadcast_first(x, axis):
    count = lax.axis_size(axis)
    mine = lax.axis_index(axis)
    held = x
    for to in range(2, count, 2):
        held = jnp.where(mine == to, lax.ppermute(x, axis, [(0, to)]), held)
    return held, lax.ppermute(held, axis, [(i, i + 1) for i in range(0, count, 2)])


INWARD = [(0, 1), (3, 2)]
MIDDLE = [(1, 2), (2, 1)]
OUTWARD = [(1, 0), (2, 3)]


def mix(before, centre, after, taps):
    before, centre, after = (v.astype(F32) for v in (before, centre, after))
    return (centre + taps[0] * before + taps[1] * centre + taps[2] * after).astype(BF16)


def per_device(frames, taps, w_query, w_key, w_value, q_gain, k_gain):
    count = lax.axis_size("tm")
    pos = lax.axis_index("tm")
    z = lax.axis_index("head").astype(jnp.int32)
    outer = (z == 0) | (z == 3)
    near, far = (z + 2) % 4, 3 - z
    side = outer.astype(jnp.int32)
    pair, second, third = z ^ 1, jnp.where(outer, near, far), jnp.where(outer, far, near)
    info = jnp.stack([side, z, pair, second, third])
    info_raw, info_end = jnp.stack([side, z, pair, second]), jnp.stack([side, third])
    hold = lax.optimization_barrier
    weights = (w_query, w_key, w_value)
    gains = (q_gain, k_gain)
    ups = [(i, i + 1) for i in range(count - 1)]
    downs = [(j, i) for i, j in ups]
    start = pos == 0

    def send(x, pairs):
        return lax.ppermute(x, "head", pairs)

    def mix_first(first, last, following, scales):
        return mix(
            jnp.where(start, jnp.zeros_like(first), first),
            jnp.where(start, first, last),
            jnp.where(start, last, following),
            scales,
        )

    def mix_second(first, last, following, preceding, scales):
        return mix(
            jnp.where(start, first, preceding),
            jnp.where(start, last, first),
            jnp.where(start, following, last),
            scales,
        )

    first, last = frames[0], frames[1]
    following = lax.ppermute(first, "tm", downs)
    first, outer_taps = hold((first, send(taps, OUTWARD)))
    raw_first = send(first, OUTWARD)
    mixed1 = mix_first(frames[0], frames[1], following, taps)
    inward1, middle1 = send(mixed1, INWARD), send(mixed1, MIDDLE)
    last, _ = hold((last, mixed1))
    raw_last, preceding = send(last, OUTWARD), lax.ppermute(last, "tm", ups)
    mixed2 = mix_second(frames[0], frames[1], following, preceding, taps)
    raw_following = lax.ppermute(raw_first, "tm", downs)
    inward1, middle1, raw_last = hold((inward1, middle1, raw_last))
    cross1, second1 = send(inward1, MIDDLE), send(middle1, OUTWARD)
    raw_preceding = lax.ppermute(raw_last, "tm", ups)
    later2, cross1, second1, raw_following = hold((mixed2, cross1, second1, raw_following))
    middle2, inward2 = send(later2, MIDDLE), send(later2, INWARD)
    third1 = send(cross1, OUTWARD)
    first1 = mix_first(raw_first, raw_last, raw_following, outer_taps)
    first2 = mix_second(raw_first, raw_last, raw_following, raw_preceding, outer_taps)
    middle2, inward2, first1, first2 = hold((middle2, inward2, first1, first2))
    cross2, second2 = send(inward2, MIDDLE), send(middle2, OUTWARD)

    sources1 = [(mixed1,), (inward1, first1), (middle1, second1), (cross1, third1)]
    q1, kv1 = project(sources1, info, weights, gains, after=(inward2, middle2), flops=10**10)
    kv1, cross2 = hold((kv1, cross2))
    third2 = send(cross2, OUTWARD)
    anchor = broadcast_first(kv1, "tm")
    later1, _ = hold((kv1, anchor[0]))
    shift1 = lax.ppermute(later1, "tm", [(i, i + 1) for i in range(1, count - 1)])
    raw2 = project([(mixed2,), (inward2, first2), (middle2, second2)], info_raw, weights, flops=10**10)
    q2, kv2 = project([(cross2, third2)], info_end, weights, gains, raw2, flops=10**10)
    shift2 = lax.ppermute(kv2, "tm", [(0, 1)])
    late = jnp.where(start, 0, 1)
    odd = pos % 2
    result = attend(q1, anchor, odd, [kv1, kv2], late, late)
    choice = jnp.minimum(pos, 1) + (pos == 1)
    return attend(q2, anchor, odd, [kv1, shift1, shift2], choice, 1 - late, result)


def solution(mesh):
    placed = (
        P("tm", None, "head"),
        P(None, "head"),
        P(None, "head"),
        P(None, "head"),
        P(None, "head"),
        P("head"),
        P("head"),
    )
    return jax.shard_map(
        per_device, mesh=mesh, in_specs=placed, out_specs=P("tm", None, "head"), check_vma=False
    )
```

```python
import functools

import jax
import jax.numpy as jnp
from jax import lax
from jax.experimental import pallas as pl
from jax.experimental.pallas import tpu as pltpu
from jax.sharding import PartitionSpec as P

DH = 128
BF16 = jnp.bfloat16
F32 = jnp.float32
ANY = pl.BlockSpec(memory_space=pl.ANY)


def normalized(part, gain):
    square = part * part
    high = square.astype(BF16)
    low = (square - high.astype(F32)).astype(BF16)
    ones = jnp.ones((2 * DH, DH), BF16)
    total = jnp.dot(jnp.concatenate([high, low], axis=1), ones, preferred_element_type=F32)
    return (part * lax.rsqrt(total * (1.0 / DH) + 1e-06) * gain).astype(BF16)


def store_heads(acc, qg, kg, q_out, kv_out):
    heads = q_out.shape[0]

    def columns(group, h):
        return acc[:, (group * heads + h) * DH : (group * heads + h + 1) * DH]

    for h in range(heads):
        span = slice(h * DH, (h + 1) * DH)
        q_out[h] = normalized(columns(0, h), qg[:, span])
        kv_out[0, h] = normalized(columns(1, h), kg[:, span])
        kv_out[1, h] = columns(2, h).astype(BF16)


def project_body(pairs, extra, has_acc, final, info, *refs):
    refs = list(refs)[extra:]
    count = len(pairs)
    groups = [[refs.pop(0) for _ in range(n)] for n in pairs]
    weights = [refs.pop(0) for _ in range(3)]
    gains = [refs.pop(0) for _ in range(2)] if final else None
    start = refs.pop(0) if has_acc else None
    outs = [refs.pop(0) for _ in range(2)] if final else None
    acc, xbuf, sem = refs
    step = pl.program_id(0)

    @pl.when(step == 0)
    def _():
        for i, group in enumerate(groups):
            for j, source in enumerate(group):

                @pl.when((info[0] == j) | (len(group) == 1))
                def _(i=i, source=source):
                    pltpu.make_async_copy(source, xbuf.at[i], sem.at[i]).start()

    for i in range(count):

        @pl.when(step == i)
        def _(i=i):
            pltpu.make_async_copy(groups[i][0], xbuf.at[i], sem.at[i]).wait()
            weight = jnp.concatenate([w[...] for w in weights], axis=1)
            part = jnp.dot(xbuf[i], weight, preferred_element_type=F32)
            if i == 0:
                acc[...] = part + start[...] if has_acc else part
            else:
                acc[...] += part

    if final:

        @pl.when(step == count - 1)
        def _():
            store_heads(acc, gains[0][...], gains[1][...], *outs)


def project(sources, info, weights, gains=None, acc=None, after=(), flops=1):
    pairs = [len(s) for s in sources]
    count = len(pairs)
    rows, chans = sources[0][0].shape
    width = weights[0].shape[1]
    heads = width // DH
    final = gains is not None
    a_spec = pl.BlockSpec((rows, 3 * width), lambda k, info: (0, 0))
    in_specs = [ANY] * (len(after) + sum(pairs)) + [pl.BlockSpec((chans, width), lambda k, info: (info[1 + k], 0))] * 3
    args = list(after) + [x for s in sources for x in s] + list(weights)
    scratch = [pltpu.VMEM((count, rows, chans), BF16), pltpu.SemaphoreType.DMA((count,))]
    raw = jax.ShapeDtypeStruct((rows, 3 * width), F32)
    if final:
        in_specs += [pl.BlockSpec((1, width), lambda k, info: (0, 0))] * 2
        args += [g[None] for g in gains]
        out_shape = [
            jax.ShapeDtypeStruct((heads, rows, DH), BF16),
            jax.ShapeDtypeStruct((2, heads, rows, DH), BF16),
        ]
        out_specs = [
            pl.BlockSpec((heads, rows, DH), lambda k, info: (0, 0, 0)),
            pl.BlockSpec((2, heads, rows, DH), lambda k, info: (0, 0, 0, 0)),
        ]
        scratch = [pltpu.VMEM(raw.shape, F32)] + scratch
    else:
        out_shape, out_specs = raw, a_spec
    if acc is not None:
        in_specs.append(a_spec)
        args.append(acc)
    return pl.pallas_call(
        functools.partial(project_body, pairs, len(after), acc is not None, final),
        grid_spec=pltpu.PrefetchScalarGridSpec(
            num_scalar_prefetch=1,
            grid=(count,),
            in_specs=in_specs,
            out_specs=out_specs,
            scratch_shapes=scratch,
        ),
        out_shape=out_shape,
        compiler_params=pltpu.CompilerParams(vmem_limit_bytes=48 * 2**20),
        cost_estimate=pl.CostEstimate(flops=flops, bytes_accessed=1, transcendentals=0),
        name="project" + ("_end" if final else "_raw"),
    )(info, *args)


def attend_body(row_block, choices, fresh, info, *refs):
    refs = list(refs)
    query = refs.pop(0)
    options = [[refs.pop(0) for _ in range(n)] for n in choices]
    if not fresh:
        refs.pop(0)
    out, held, sem = refs
    h = pl.program_id(0)

    def fetch(part, source, head):
        return pltpu.make_async_copy(source.at[:, head], held.at[part, :, head], sem.at[part, head])

    @pl.when(h == 0)
    def _():
        for head in range(held.shape[2]):
            for part in range(2):
                for j, source in enumerate(options[part]):

                    @pl.when(info[2 * part] == j)
                    def _(part=part, source=source, head=head):
                        fetch(part, source, head).start()

    for part in range(2):
        fetch(part, options[part][0], h).wait()
    factor = 1.4426950408889634 / DH**0.5
    key = jnp.concatenate([held[0, 0, h], held[1, 0, h]], axis=0)
    value = jnp.concatenate([held[0, 1, h], held[1, 1, h]], axis=0)
    value = jnp.concatenate([value, jnp.ones_like(value)], axis=1)
    rows = query.shape[1]
    for r in range(rows // row_block):
        span = pl.ds(r * row_block, row_block)
        scores = lax.dot_general(
            query[0, span, :], key, (((1,), (1,)), ((), ())), preferred_element_type=F32
        )
        tops = [scores[:, c : c + DH] for c in range(0, scores.shape[1], DH)]
        top = jnp.max(functools.reduce(jnp.maximum, tops), axis=-1, keepdims=True)
        expo = jnp.exp2((scores - top) * factor).astype(BF16)
        result = jnp.dot(expo, value, preferred_element_type=F32)
        out[0, span, :] = (result[:, :DH] / result[:, DH:]).astype(BF16)


def attend(query, anchors, anchor, options, choice, frame, partly=None):
    heads, rows, _ = query.shape
    in_specs = [pl.BlockSpec((1, rows, DH), lambda h, info: (h, 0, 0))]
    in_specs += [ANY] * (len(anchors) + len(options))
    args = [query, *anchors, *options]
    aliases = {}
    if partly is not None:
        in_specs.append(ANY)
        aliases = {1 + len(args): 0}
        args.append(partly)
    return pl.pallas_call(
        functools.partial(attend_body, 128, (len(anchors), len(options)), partly is None),
        grid_spec=pltpu.PrefetchScalarGridSpec(
            num_scalar_prefetch=1,
            grid=(heads,),
            in_specs=in_specs,
            out_specs=pl.BlockSpec((1, rows, DH), lambda h, info: (info[1], 0, h)),
            scratch_shapes=[
                pltpu.VMEM((2, 2, heads, rows, DH), BF16),
                pltpu.SemaphoreType.DMA((2, heads)),
            ],
        ),
        out_shape=jax.ShapeDtypeStruct((2, rows, heads * DH), BF16),
        input_output_aliases=aliases,
        compiler_params=pltpu.CompilerParams(vmem_limit_bytes=32 * 2**20),
        cost_estimate=pl.CostEstimate(
            flops=8 * heads * rows * rows * DH,
            bytes_accessed=2 * heads * rows * DH * 6,
            transcendentals=2 * heads * rows * rows,
        ),
        name="attend",
    )(jnp.stack([anchor, frame, choice]).astype(jnp.int32), *args)


def broadcast_first(x, axis):
    count = lax.axis_size(axis)
    mine = lax.axis_index(axis)
    held = x
    for to in range(2, count, 2):
        held = jnp.where(mine == to, lax.ppermute(x, axis, [(0, to)]), held)
    return held, lax.ppermute(held, axis, [(i, i + 1) for i in range(0, count, 2)])


INWARD = [(0, 1), (3, 2)]
MIDDLE = [(1, 2), (2, 1)]
OUTWARD = [(1, 0), (2, 3)]


def mix(before, centre, after, taps):
    before, centre, after = (v.astype(F32) for v in (before, centre, after))
    return (centre + taps[0] * before + taps[1] * centre + taps[2] * after).astype(BF16)


def per_device(frames, taps, w_query, w_key, w_value, q_gain, k_gain):
    count = lax.axis_size("tm")
    pos = lax.axis_index("tm")
    z = lax.axis_index("head").astype(jnp.int32)
    outer = (z == 0) | (z == 3)
    near, far = (z + 2) % 4, 3 - z
    side = outer.astype(jnp.int32)
    pair, second, third = z ^ 1, jnp.where(outer, near, far), jnp.where(outer, far, near)
    info = jnp.stack([side, z, pair, second, third])
    info_raw, info_end = jnp.stack([side, z, pair, second]), jnp.stack([side, third])
    hold = lax.optimization_barrier
    weights = (w_query, w_key, w_value)
    gains = (q_gain, k_gain)
    ups = [(i, i + 1) for i in range(count - 1)]
    downs = [(j, i) for i, j in ups]
    start = pos == 0

    def send(x, pairs):
        return lax.ppermute(x, "head", pairs)

    def mix_first(first, last, following, scales):
        return mix(
            jnp.where(start, jnp.zeros_like(first), first),
            jnp.where(start, first, last),
            jnp.where(start, last, following),
            scales,
        )

    def mix_second(first, last, following, preceding, scales):
        return mix(
            jnp.where(start, first, preceding),
            jnp.where(start, last, first),
            jnp.where(start, following, last),
            scales,
        )

    first, last = frames[0], frames[1]
    following = lax.ppermute(first, "tm", downs)
    first, outer_taps = hold((first, send(taps, OUTWARD)))
    raw_first = send(first, OUTWARD)
    mixed1 = mix_first(frames[0], frames[1], following, taps)
    inward1, middle1 = send(mixed1, INWARD), send(mixed1, MIDDLE)
    last, _ = hold((last, mixed1))
    raw_last, preceding = send(last, OUTWARD), lax.ppermute(last, "tm", ups)
    mixed2 = mix_second(frames[0], frames[1], following, preceding, taps)
    raw_following = lax.ppermute(raw_first, "tm", downs)
    inward1, middle1, raw_last = hold((inward1, middle1, raw_last))
    cross1, second1 = send(inward1, MIDDLE), send(middle1, OUTWARD)
    raw_preceding = lax.ppermute(raw_last, "tm", ups)
    later2, cross1, second1, raw_following = hold((mixed2, cross1, second1, raw_following))
    middle2, inward2 = send(later2, MIDDLE), send(later2, INWARD)
    third1 = send(cross1, OUTWARD)
    first1 = mix_first(raw_first, raw_last, raw_following, outer_taps)
    first2 = mix_second(raw_first, raw_last, raw_following, raw_preceding, outer_taps)
    middle2, inward2, first1, first2 = hold((middle2, inward2, first1, first2))
    cross2, second2 = send(inward2, MIDDLE), send(middle2, OUTWARD)

    sources1 = [(mixed1,), (inward1, first1), (middle1, second1), (cross1, third1)]
    q1, kv1 = project(sources1, info, weights, gains, after=(inward2, middle2), flops=10**10)
    beside = lax.ppermute(middle2[:16], "tm", [(i, i ^ 1) for i in range(count)])
    kv1, beside = hold((kv1, beside))
    third2 = send(cross2, OUTWARD)
    anchor = broadcast_first(kv1, "tm")
    later1, _ = hold((kv1, anchor[0]))
    shift1 = lax.ppermute(later1, "tm", [(i, i + 1) for i in range(1, count - 1)])
    raw2 = project([(mixed2,), (inward2, first2), (middle2, second2)], info_raw, weights, after=(beside,), flops=10**10)
    q2, kv2 = project([(cross2, third2)], info_end, weights, gains, raw2, flops=10**10)
    shift2 = lax.ppermute(kv2, "tm", [(0, 1)])
    late = jnp.where(start, 0, 1)
    odd = pos % 2
    result = attend(q1, anchor, odd, [kv1, kv2], late, late)
    choice = jnp.minimum(pos, 1) + (pos == 1)
    return attend(q2, anchor, odd, [kv1, shift1, shift2], choice, 1 - late, result)


def solution(mesh):
    placed = (
        P("tm", None, "head"),
        P(None, "head"),
        P(None, "head"),
        P(None, "head"),
        P(None, "head"),
        P("head"),
        P("head"),
    )
    return jax.shard_map(
        per_device, mesh=mesh, in_specs=placed, out_specs=P("tm", None, "head"), check_vma=False
    )
```

```python
import functools

import jax
import jax.numpy as jnp
from jax import lax
from jax.experimental import pallas as pl
from jax.experimental.pallas import tpu as pltpu
from jax.sharding import PartitionSpec as P

DH = 128
BF16 = jnp.bfloat16
F32 = jnp.float32
ANY = pl.BlockSpec(memory_space=pl.ANY)


def normalized(part, gain):
    square = part * part
    high = square.astype(BF16)
    low = (square - high.astype(F32)).astype(BF16)
    ones = jnp.ones((2 * DH, DH), BF16)
    total = jnp.dot(jnp.concatenate([high, low], axis=1), ones, preferred_element_type=F32)
    return (part * lax.rsqrt(total * (1.0 / DH) + 1e-06) * gain).astype(BF16)


def store_head(raw, gains, q_out, kv_out, h):
    q_out[h] = normalized(raw[0], gains[0])
    kv_out[0, h] = normalized(raw[1], gains[1])
    kv_out[1, h] = raw[2].astype(BF16)


def project_body(pairs, extra, final, info, *refs):
    refs = list(refs)[extra:]
    count = len(pairs)
    groups = [[refs.pop(0) for _ in range(n)] for n in pairs]
    weights = [refs.pop(0) for _ in range(3)]
    gains = [refs.pop(0) for _ in range(2)] if final else None
    outs = [refs.pop(0) for _ in range(2)] if final else None
    acc, xbuf, sem = refs
    heads = weights[0].shape[1] // DH
    step = pl.program_id(0)

    @pl.when(step == 0)
    def _():
        for i, group in enumerate(groups):
            for j, source in enumerate(group):

                @pl.when((info[0] == j) | (len(group) == 1))
                def _(i=i, source=source):
                    pltpu.make_async_copy(source, xbuf.at[i], sem.at[i]).start()

    for i in range(count):

        @pl.when(step == i)
        def _(i=i):
            pltpu.make_async_copy(groups[i][0], xbuf.at[i], sem.at[i]).wait()
            weight = jnp.concatenate([w[...] for w in weights], axis=1)
            part = jnp.dot(xbuf[i], weight, preferred_element_type=F32)
            if final:
                acc[...] = part if i == 0 else acc[...] + part
            else:
                for group in range(3):
                    for h in range(heads):
                        columns = part[:, (group * heads + h) * DH : (group * heads + h + 1) * DH]
                        acc[group, h] = columns if i == 0 else acc[group, h] + columns

    if final:

        @pl.when(step == count - 1)
        def _():
            for h in range(heads):
                total = [acc[:, (group * heads + h) * DH : (group * heads + h + 1) * DH] for group in range(3)]
                store_head(total, [g[:, h * DH : (h + 1) * DH] for g in gains], *outs, h)


def project(sources, info, weights, gains=None, after=(), flops=1):
    pairs = [len(s) for s in sources]
    count = len(pairs)
    rows, chans = sources[0][0].shape
    width = weights[0].shape[1]
    heads = width // DH
    final = gains is not None
    a_spec = pl.BlockSpec((3, heads, rows, DH), lambda k, info: (0, 0, 0, 0))
    in_specs = [ANY] * (len(after) + sum(pairs)) + [pl.BlockSpec((chans, width), lambda k, info: (info[1 + k], 0))] * 3
    args = list(after) + [x for s in sources for x in s] + list(weights)
    scratch = [pltpu.VMEM((count, rows, chans), BF16), pltpu.SemaphoreType.DMA((count,))]
    raw = jax.ShapeDtypeStruct((3, heads, rows, DH), F32)
    if final:
        in_specs += [pl.BlockSpec((1, width), lambda k, info: (0, 0))] * 2
        args += [g[None] for g in gains]
        out_shape = [
            jax.ShapeDtypeStruct((heads, rows, DH), BF16),
            jax.ShapeDtypeStruct((2, heads, rows, DH), BF16),
        ]
        out_specs = [
            pl.BlockSpec((heads, rows, DH), lambda k, info: (0, 0, 0)),
            pl.BlockSpec((2, heads, rows, DH), lambda k, info: (0, 0, 0, 0)),
        ]
        scratch = [pltpu.VMEM((rows, 3 * width), F32)] + scratch
    else:
        out_shape, out_specs = raw, a_spec
    return pl.pallas_call(
        functools.partial(project_body, pairs, len(after), final),
        grid_spec=pltpu.PrefetchScalarGridSpec(
            num_scalar_prefetch=1,
            grid=(count,),
            in_specs=in_specs,
            out_specs=out_specs,
            scratch_shapes=scratch,
        ),
        out_shape=out_shape,
        compiler_params=pltpu.CompilerParams(vmem_limit_bytes=48 * 2**20),
        cost_estimate=pl.CostEstimate(flops=flops, bytes_accessed=1, transcendentals=0),
        name="project" + ("_end" if final else "_raw"),
    )(info, *args)


def finish_body(info, inner, outer, wq, wk, wv, qg, kg, raw, q_out, kv_out, rows, sem):
    @pl.when(pl.program_id(0) == 0)
    def _():
        for side, source in enumerate((inner, outer)):

            @pl.when(info[0] == side)
            def _(source=source):
                pltpu.make_async_copy(source, rows, sem).start()

        pltpu.make_async_copy(inner, rows, sem).wait()

    weight = jnp.concatenate([wq[...], wk[...], wv[...]], axis=1)
    part = jnp.dot(rows[...], weight, preferred_element_type=F32)
    total = [raw[group, 0] + part[:, group * DH : (group + 1) * DH] for group in range(3)]
    store_head(total, (qg[...], kg[...]), q_out, kv_out, 0)


def finish(raw, inner, outer, info, weights, gains, flops):
    rows, chans = inner.shape
    heads = raw.shape[1]
    w_spec = pl.BlockSpec((chans, DH), lambda h, info: (info[1], h))
    g_spec = pl.BlockSpec((1, DH), lambda h, info: (0, h))
    return pl.pallas_call(
        finish_body,
        grid_spec=pltpu.PrefetchScalarGridSpec(
            num_scalar_prefetch=1,
            grid=(heads,),
            in_specs=[ANY] * 2
            + [w_spec] * 3
            + [g_spec] * 2
            + [pl.BlockSpec((3, 1, rows, DH), lambda h, info: (0, h, 0, 0))],
            out_specs=[
                pl.BlockSpec((1, rows, DH), lambda h, info: (h, 0, 0)),
                pl.BlockSpec((2, 1, rows, DH), lambda h, info: (0, h, 0, 0)),
            ],
            scratch_shapes=[pltpu.VMEM((rows, chans), BF16), pltpu.SemaphoreType.DMA],
        ),
        out_shape=[
            jax.ShapeDtypeStruct((heads, rows, DH), BF16),
            jax.ShapeDtypeStruct((2, heads, rows, DH), BF16),
        ],
        compiler_params=pltpu.CompilerParams(vmem_limit_bytes=32 * 2**20),
        cost_estimate=pl.CostEstimate(flops=flops, bytes_accessed=1, transcendentals=0),
        name="finish",
    )(info, inner, outer, *weights, *(g[None] for g in gains), raw)


def attend_body(row_block, choices, fresh, info, *refs):
    refs = list(refs)
    query = refs.pop(0)
    options = [[refs.pop(0) for _ in range(n)] for n in choices]
    if not fresh:
        refs.pop(0)
    out, held, sem = refs
    h = pl.program_id(0)

    def fetch(part, source, head):
        return pltpu.make_async_copy(source.at[:, head], held.at[part, :, head], sem.at[part, head])

    @pl.when(h == 0)
    def _():
        for head in range(held.shape[2]):
            for part in range(2):
                for j, source in enumerate(options[part]):

                    @pl.when(info[2 * part] == j)
                    def _(part=part, source=source, head=head):
                        fetch(part, source, head).start()

    for part in range(2):
        fetch(part, options[part][0], h).wait()
    factor = 1.4426950408889634 / DH**0.5
    key = jnp.concatenate([held[0, 0, h], held[1, 0, h]], axis=0)
    value = jnp.concatenate([held[0, 1, h], held[1, 1, h]], axis=0)
    value = jnp.concatenate([value, jnp.ones_like(value)], axis=1)
    spans = [pl.ds(row, row_block) for row in range(0, query.shape[1], row_block)]

    def score(span):
        return lax.dot_general(
            query[0, span, :], key, (((1,), (1,)), ((), ())), preferred_element_type=F32
        )

    ahead = score(spans[0])
    for r, span in enumerate(spans):
        scores = ahead
        if r + 1 < len(spans):
            ahead = score(spans[r + 1])
        tops = [scores[:, c : c + DH] for c in range(0, scores.shape[1], DH)]
        top = jnp.max(functools.reduce(jnp.maximum, tops), axis=-1, keepdims=True)
        expo = jnp.exp2((scores - top) * factor).astype(BF16)
        result = jnp.dot(expo, value, preferred_element_type=F32)
        out[0, span, :] = (result[:, :DH] / result[:, DH:]).astype(BF16)


def attend(query, anchors, anchor, options, choice, frame, partly=None):
    heads, rows, _ = query.shape
    args = [query, *anchors, *options]
    aliases = {}
    if partly is not None:
        aliases = {1 + len(args): 0}
        args.append(partly)
    return pl.pallas_call(
        functools.partial(attend_body, 256, (len(anchors), len(options)), partly is None),
        grid_spec=pltpu.PrefetchScalarGridSpec(
            num_scalar_prefetch=1,
            grid=(heads,),
            in_specs=[pl.BlockSpec((1, rows, DH), lambda h, info: (h, 0, 0))] + [ANY] * (len(args) - 1),
            out_specs=pl.BlockSpec((1, rows, DH), lambda h, info: (info[1], 0, h)),
            scratch_shapes=[
                pltpu.VMEM((2, 2, heads, rows, DH), BF16),
                pltpu.SemaphoreType.DMA((2, heads)),
            ],
        ),
        out_shape=jax.ShapeDtypeStruct((2, rows, heads * DH), BF16),
        input_output_aliases=aliases,
        compiler_params=pltpu.CompilerParams(vmem_limit_bytes=32 * 2**20),
        cost_estimate=pl.CostEstimate(
            flops=8 * heads * rows * rows * DH,
            bytes_accessed=2 * heads * rows * DH * 6,
            transcendentals=2 * heads * rows * rows,
        ),
        name="attend",
    )(jnp.stack([anchor, frame, choice]).astype(jnp.int32), *args)


def broadcast_first(x, axis):
    count = lax.axis_size(axis)
    mine = lax.axis_index(axis)
    held = x
    for to in range(2, count, 2):
        held = jnp.where(mine == to, lax.ppermute(x, axis, [(0, to)]), held)
    return held, lax.ppermute(held, axis, [(i, i + 1) for i in range(0, count, 2)])


INWARD = [(0, 1), (3, 2)]
MIDDLE = [(1, 2), (2, 1)]
OUTWARD = [(1, 0), (2, 3)]


def mix(before, centre, after, taps):
    before, centre, after = (v.astype(F32) for v in (before, centre, after))
    return (centre + taps[0] * before + taps[1] * centre + taps[2] * after).astype(BF16)


def per_device(frames, taps, w_query, w_key, w_value, q_gain, k_gain):
    count = lax.axis_size("tm")
    pos = lax.axis_index("tm")
    z = lax.axis_index("head").astype(jnp.int32)
    outer = (z == 0) | (z == 3)
    near, far = (z + 2) % 4, 3 - z
    side = outer.astype(jnp.int32)
    pair, second, third = z ^ 1, jnp.where(outer, near, far), jnp.where(outer, far, near)
    info = jnp.stack([side, z, pair, second, third])
    info_raw, info_end = jnp.stack([side, z, pair, second]), jnp.stack([side, third])
    hold = lax.optimization_barrier
    weights = (w_query, w_key, w_value)
    gains = (q_gain, k_gain)
    ups = [(i, i + 1) for i in range(count - 1)]
    downs = [(j, i) for i, j in ups]
    start = pos == 0

    def send(x, pairs):
        return lax.ppermute(x, "head", pairs)

    def mix_first(first, last, following, scales):
        return mix(
            jnp.where(start, jnp.zeros_like(first), first),
            jnp.where(start, first, last),
            jnp.where(start, last, following),
            scales,
        )

    def mix_second(first, last, following, preceding, scales):
        return mix(
            jnp.where(start, first, preceding),
            jnp.where(start, last, first),
            jnp.where(start, following, last),
            scales,
        )

    first, last = frames[0], frames[1]
    following = lax.ppermute(first, "tm", downs)
    first, outer_taps = hold((first, send(taps, OUTWARD)))
    raw_first = send(first, OUTWARD)
    mixed1 = mix_first(frames[0], frames[1], following, taps)
    inward1, middle1 = send(mixed1, INWARD), send(mixed1, MIDDLE)
    last, _ = hold((last, mixed1))
    raw_last, preceding = send(last, OUTWARD), lax.ppermute(last, "tm", ups)
    mixed2 = mix_second(frames[0], frames[1], following, preceding, taps)
    raw_following = lax.ppermute(raw_first, "tm", downs)
    inward1, middle1 = hold((inward1, middle1))
    cross1, second1 = send(inward1, MIDDLE), send(middle1, OUTWARD)
    raw_preceding = lax.ppermute(raw_last, "tm", ups)
    level = (mixed2, cross1, second1, raw_following, raw_preceding)
    later2, cross1, second1, raw_following, raw_preceding = hold(level)
    middle2, inward2 = send(later2, MIDDLE), send(mixed2, INWARD)
    third1 = send(cross1, OUTWARD)
    first1 = mix_first(raw_first, raw_last, raw_following, outer_taps)
    first2 = mix_second(raw_first, raw_last, raw_following, raw_preceding, outer_taps)
    middle2, inward2, first1, first2 = hold((middle2, inward2, first1, first2))
    cross2, second2 = send(inward2, MIDDLE), send(middle2, OUTWARD)

    sources1 = [(mixed1,), (inward1, first1), (middle1, second1), (cross1, third1)]
    q1, kv1 = project(sources1, info, weights, gains, after=(inward2, middle2), flops=10**10)
    beside = lax.ppermute(inward2[:16], "tm", [(i, i ^ 1) for i in range(count)])
    kv1, beside = hold((kv1, beside))
    third2 = send(cross2, OUTWARD)
    anchor = broadcast_first(kv1, "tm")
    later1, _ = hold((kv1, anchor[0]))
    shift1 = lax.ppermute(later1, "tm", [(i, i + 1) for i in range(1, count - 1)])
    raw2 = project([(mixed2,), (inward2, first2), (middle2, second2)], info_raw, weights, after=(beside,), flops=10**10)
    q2, kv2 = finish(raw2, cross2, third2, info_end, weights, gains, 10**10)
    shift2 = lax.ppermute(kv2, "tm", [(0, 1)])
    late = jnp.where(start, 0, 1)
    odd = pos % 2
    result = attend(q1, anchor, odd, [kv1, kv2], late, late)
    choice = jnp.minimum(pos, 1) + (pos == 1)
    return attend(q2, anchor, odd, [kv1, shift1, shift2], choice, 1 - late, result)


def solution(mesh):
    placed = (
        P("tm", None, "head"),
        P(None, "head"),
        P(None, "head"),
        P(None, "head"),
        P(None, "head"),
        P("head"),
        P("head"),
    )
    return jax.shard_map(
        per_device, mesh=mesh, in_specs=placed, out_specs=P("tm", None, "head"), check_vma=False
    )
```

```python
import functools

import jax
import jax.numpy as jnp
from jax import lax
from jax.experimental import pallas as pl
from jax.experimental.pallas import tpu as pltpu
from jax.sharding import PartitionSpec as P

DH = 128
BF16 = jnp.bfloat16
F32 = jnp.float32
ANY = pl.BlockSpec(memory_space=pl.ANY)


def normalized(part, gain):
    square = part * part
    high = square.astype(BF16)
    low = (square - high.astype(F32)).astype(BF16)
    ones = jnp.ones((2 * DH, DH), BF16)
    total = jnp.dot(jnp.concatenate([high, low], axis=1), ones, preferred_element_type=F32)
    return (part * lax.rsqrt(total * (1.0 / DH) + 1e-06) * gain).astype(BF16)


def store_head(raw, gains, q_out, kv_out, h):
    q_out[h] = normalized(raw[0], gains[0])
    kv_out[0, h] = normalized(raw[1], gains[1])
    kv_out[1, h] = raw[2].astype(BF16)


def project_body(pairs, extra, final, info, *refs):
    refs = list(refs)[extra:]
    count = len(pairs)
    groups = [[refs.pop(0) for _ in range(n)] for n in pairs]
    weights = [refs.pop(0) for _ in range(3)]
    gains = [refs.pop(0) for _ in range(2)] if final else None
    outs = [refs.pop(0) for _ in range(2)] if final else None
    acc, xbuf, sem = refs
    heads = weights[0].shape[1] // DH
    step = pl.program_id(0)

    @pl.when(step == 0)
    def _():
        for i, group in enumerate(groups):
            for j, source in enumerate(group):

                @pl.when((info[0] == j) | (len(group) == 1))
                def _(i=i, source=source):
                    pltpu.make_async_copy(source, xbuf.at[i], sem.at[i]).start()

    for i in range(count):

        @pl.when(step == i)
        def _(i=i):
            pltpu.make_async_copy(groups[i][0], xbuf.at[i], sem.at[i]).wait()
            weight = jnp.concatenate([w[...] for w in weights], axis=1)
            part = jnp.dot(xbuf[i], weight, preferred_element_type=F32)
            if final:
                acc[...] = part if i == 0 else acc[...] + part
            else:
                for group in range(3):
                    for h in range(heads):
                        columns = part[:, (group * heads + h) * DH : (group * heads + h + 1) * DH]
                        acc[group, h] = columns if i == 0 else acc[group, h] + columns

    if final:

        @pl.when(step == count - 1)
        def _():
            for h in range(heads):
                total = [acc[:, (group * heads + h) * DH : (group * heads + h + 1) * DH] for group in range(3)]
                store_head(total, [g[:, h * DH : (h + 1) * DH] for g in gains], *outs, h)


def project(sources, info, weights, gains=None, after=(), flops=1):
    pairs = [len(s) for s in sources]
    count = len(pairs)
    rows, chans = sources[0][0].shape
    width = weights[0].shape[1]
    heads = width // DH
    final = gains is not None
    a_spec = pl.BlockSpec((3, heads, rows, DH), lambda k, info: (0, 0, 0, 0))
    in_specs = [ANY] * (len(after) + sum(pairs)) + [pl.BlockSpec((chans, width), lambda k, info: (info[1 + k], 0))] * 3
    args = list(after) + [x for s in sources for x in s] + list(weights)
    scratch = [pltpu.VMEM((count, rows, chans), BF16), pltpu.SemaphoreType.DMA((count,))]
    raw = jax.ShapeDtypeStruct((3, heads, rows, DH), F32)
    if final:
        in_specs += [pl.BlockSpec((1, width), lambda k, info: (0, 0))] * 2
        args += [g[None] for g in gains]
        out_shape = [
            jax.ShapeDtypeStruct((heads, rows, DH), BF16),
            jax.ShapeDtypeStruct((2, heads, rows, DH), BF16),
        ]
        out_specs = [
            pl.BlockSpec((heads, rows, DH), lambda k, info: (0, 0, 0)),
            pl.BlockSpec((2, heads, rows, DH), lambda k, info: (0, 0, 0, 0)),
        ]
        scratch = [pltpu.VMEM((rows, 3 * width), F32)] + scratch
    else:
        out_shape, out_specs = raw, a_spec
    return pl.pallas_call(
        functools.partial(project_body, pairs, len(after), final),
        grid_spec=pltpu.PrefetchScalarGridSpec(
            num_scalar_prefetch=1,
            grid=(count,),
            in_specs=in_specs,
            out_specs=out_specs,
            scratch_shapes=scratch,
        ),
        out_shape=out_shape,
        compiler_params=pltpu.CompilerParams(vmem_limit_bytes=48 * 2**20),
        cost_estimate=pl.CostEstimate(flops=flops, bytes_accessed=1, transcendentals=0),
        name="project" + ("_end" if final else "_raw"),
    )(info, *args)


def finish_body(info, inner, outer, wq, wk, wv, qg, kg, raw, q_out, kv_out, rows, sem):
    @pl.when(pl.program_id(0) == 0)
    def _():
        for side, source in enumerate((inner, outer)):

            @pl.when(info[0] == side)
            def _(source=source):
                pltpu.make_async_copy(source, rows, sem).start()

        pltpu.make_async_copy(inner, rows, sem).wait()

    weight = jnp.concatenate([wq[...], wk[...], wv[...]], axis=1)
    part = jnp.dot(rows[...], weight, preferred_element_type=F32)
    total = [raw[group, 0] + part[:, group * DH : (group + 1) * DH] for group in range(3)]
    store_head(total, (qg[...], kg[...]), q_out, kv_out, 0)


def finish(raw, inner, outer, info, weights, gains, flops):
    rows, chans = inner.shape
    heads = raw.shape[1]
    w_spec = pl.BlockSpec((chans, DH), lambda h, info: (info[1], h))
    g_spec = pl.BlockSpec((1, DH), lambda h, info: (0, h))
    return pl.pallas_call(
        finish_body,
        grid_spec=pltpu.PrefetchScalarGridSpec(
            num_scalar_prefetch=1,
            grid=(heads,),
            in_specs=[ANY] * 2
            + [w_spec] * 3
            + [g_spec] * 2
            + [pl.BlockSpec((3, 1, rows, DH), lambda h, info: (0, h, 0, 0))],
            out_specs=[
                pl.BlockSpec((1, rows, DH), lambda h, info: (h, 0, 0)),
                pl.BlockSpec((2, 1, rows, DH), lambda h, info: (0, h, 0, 0)),
            ],
            scratch_shapes=[pltpu.VMEM((rows, chans), BF16), pltpu.SemaphoreType.DMA],
        ),
        out_shape=[
            jax.ShapeDtypeStruct((heads, rows, DH), BF16),
            jax.ShapeDtypeStruct((2, heads, rows, DH), BF16),
        ],
        compiler_params=pltpu.CompilerParams(vmem_limit_bytes=48 * 2**20),
        cost_estimate=pl.CostEstimate(flops=flops, bytes_accessed=1, transcendentals=0),
        name="finish",
    )(info, inner, outer, *weights, *(g[None] for g in gains), raw)


def attend_body(row_block, choices, fresh, info, *refs):
    refs = list(refs)
    query = refs.pop(0)
    options = [[refs.pop(0) for _ in range(n)] for n in choices]
    if not fresh:
        refs.pop(0)
    out, held, sem = refs
    h = pl.program_id(0)

    def fetch(part, source, head):
        return pltpu.make_async_copy(source.at[:, head], held.at[part, :, head], sem.at[part, head])

    @pl.when(h == 0)
    def _():
        for head in range(held.shape[2]):
            for part in range(2):
                for j, source in enumerate(options[part]):

                    @pl.when(info[2 * part] == j)
                    def _(part=part, source=source, head=head):
                        fetch(part, source, head).start()

    for part in range(2):
        fetch(part, options[part][0], h).wait()
    factor = 1.4426950408889634 / DH**0.5
    key = jnp.concatenate([held[0, 0, h], held[1, 0, h]], axis=0)
    value = jnp.concatenate([held[0, 1, h], held[1, 1, h]], axis=0)
    value = jnp.concatenate([value, jnp.ones_like(value)], axis=1)
    spans = [pl.ds(row, row_block) for row in range(0, query.shape[1], row_block)]

    def score(span):
        return lax.dot_general(
            query[0, span, :], key, (((1,), (1,)), ((), ())), preferred_element_type=F32
        )

    ahead = score(spans[0])
    for r, span in enumerate(spans):
        scores = ahead
        if r + 1 < len(spans):
            ahead = score(spans[r + 1])
        tops = [scores[:, c : c + DH] for c in range(0, scores.shape[1], DH)]
        top = jnp.max(functools.reduce(jnp.maximum, tops), axis=-1, keepdims=True)
        expo = jnp.exp2((scores - top) * factor).astype(BF16)
        result = jnp.dot(expo, value, preferred_element_type=F32)
        out[0, span, :] = (result[:, :DH] / result[:, DH:]).astype(BF16)


def attend(query, anchors, anchor, options, choice, frame, partly=None):
    heads, rows, _ = query.shape
    args = [query, *anchors, *options]
    aliases = {}
    if partly is not None:
        aliases = {1 + len(args): 0}
        args.append(partly)
    return pl.pallas_call(
        functools.partial(attend_body, 256, (len(anchors), len(options)), partly is None),
        grid_spec=pltpu.PrefetchScalarGridSpec(
            num_scalar_prefetch=1,
            grid=(heads,),
            in_specs=[pl.BlockSpec((1, rows, DH), lambda h, info: (h, 0, 0))] + [ANY] * (len(args) - 1),
            out_specs=pl.BlockSpec((1, rows, DH), lambda h, info: (info[1], 0, h)),
            scratch_shapes=[
                pltpu.VMEM((2, 2, heads, rows, DH), BF16),
                pltpu.SemaphoreType.DMA((2, heads)),
            ],
        ),
        out_shape=jax.ShapeDtypeStruct((2, rows, heads * DH), BF16),
        input_output_aliases=aliases,
        compiler_params=pltpu.CompilerParams(vmem_limit_bytes=32 * 2**20),
        cost_estimate=pl.CostEstimate(
            flops=8 * heads * rows * rows * DH,
            bytes_accessed=2 * heads * rows * DH * 6,
            transcendentals=2 * heads * rows * rows,
        ),
        name="attend",
    )(jnp.stack([anchor, frame, choice]).astype(jnp.int32), *args)


def broadcast_first(x, axis):
    count = lax.axis_size(axis)
    mine = lax.axis_index(axis)
    held = x
    for to in range(2, count, 2):
        held = jnp.where(mine == to, lax.ppermute(x, axis, [(0, to)]), held)
    return held, lax.ppermute(held, axis, [(i, i + 1) for i in range(0, count, 2)])


INWARD = [(0, 1), (3, 2)]
MIDDLE = [(1, 2), (2, 1)]
OUTWARD = [(1, 0), (2, 3)]


def mix(before, centre, after, taps):
    before, centre, after = (v.astype(F32) for v in (before, centre, after))
    return (centre + taps[0] * before + taps[1] * centre + taps[2] * after).astype(BF16)


def split_rows(scales):
    parts, rest = [], scales
    for _ in range(3):
        part = lax.reduce_precision(rest, 8, 7)
        parts.append(part.astype(BF16))
        rest = rest - part
    rows = jnp.concatenate(parts, axis=0)
    return jnp.pad(rows, ((0, 16 - rows.shape[0]), (0, 0)))


def joined_rows(rows, count):
    high, middle, low = (rows[i * count : (i + 1) * count].astype(F32) for i in range(3))
    return high + middle + low


def per_device(frames, taps, w_query, w_key, w_value, q_gain, k_gain):
    count = lax.axis_size("tm")
    pos = lax.axis_index("tm")
    z = lax.axis_index("head").astype(jnp.int32)
    outer = (z == 0) | (z == 3)
    near, far = (z + 2) % 4, 3 - z
    side = outer.astype(jnp.int32)
    pair, second, third = z ^ 1, jnp.where(outer, near, far), jnp.where(outer, far, near)
    info = jnp.stack([side, z, pair, second, third])
    info_raw, info_end = jnp.stack([side, z, pair, second]), jnp.stack([side, third])
    hold = lax.optimization_barrier
    weights = (w_query, w_key, w_value)
    gains = (q_gain, k_gain)
    ups = [(i, i + 1) for i in range(count - 1)]
    downs = [(j, i) for i, j in ups]
    start = pos == 0

    def send(x, pairs):
        return lax.ppermute(x, "head", pairs)

    def mix_first(first, last, following, scales):
        return mix(
            jnp.where(start, jnp.zeros_like(first), first),
            jnp.where(start, first, last),
            jnp.where(start, last, following),
            scales,
        )

    def mix_second(first, last, following, preceding, scales):
        return mix(
            jnp.where(start, first, preceding),
            jnp.where(start, last, first),
            jnp.where(start, following, last),
            scales,
        )

    raw_first = send(frames[0], OUTWARD)
    following = lax.ppermute(frames[0], "tm", downs)
    mixed1 = mix_first(frames[0], frames[1], following, taps)
    last = jnp.concatenate([frames[1], split_rows(taps)], axis=0)
    later, last, mixed1 = hold((frames[1], last, mixed1))
    inward1, middle1 = send(mixed1, INWARD), send(mixed1, MIDDLE)
    raw_last = send(last, OUTWARD)
    later, raw_first = hold((later, raw_first))
    preceding = lax.ppermute(later, "tm", ups)
    mixed2 = mix_second(frames[0], frames[1], following, preceding, taps)
    raw_following = lax.ppermute(raw_first, "tm", downs)
    inward1, middle1 = hold((inward1, middle1))
    cross1, second1 = send(inward1, MIDDLE), send(middle1, OUTWARD)
    outer_taps = joined_rows(raw_last[later.shape[0] :], taps.shape[0])
    raw_last = raw_last[: later.shape[0]]
    raw_preceding = lax.ppermute(raw_last, "tm", ups)
    later2, cross1 = hold((mixed2, cross1))
    middle2, inward2 = send(later2, MIDDLE), send(mixed2, INWARD)
    level = (cross1, second1, raw_following, raw_preceding)
    cross1, second1, raw_following, raw_preceding = hold(level)
    third1 = send(cross1, OUTWARD)
    first1 = mix_first(raw_first, raw_last, raw_following, outer_taps)
    first2 = mix_second(raw_first, raw_last, raw_following, raw_preceding, outer_taps)
    middle2, inward2, first1, first2 = hold((middle2, inward2, first1, first2))
    cross2, second2 = send(inward2, MIDDLE), send(middle2, OUTWARD)

    sources1 = [(mixed1,), (inward1, first1), (middle1, second1), (cross1, third1)]
    q1, kv1 = project(sources1, info, weights, gains, after=(inward2, middle2), flops=10**10)
    beside = lax.ppermute(inward2[:16], "tm", [(i, i ^ 1) for i in range(count)])
    kv1, beside = hold((kv1, beside))
    third2 = send(cross2, OUTWARD)
    anchor = broadcast_first(kv1, "tm")
    later1, _ = hold((kv1, anchor[0]))
    shift1 = lax.ppermute(later1, "tm", [(i, i + 1) for i in range(1, count - 1)])
    raw2 = project([(mixed2,), (inward2, first2), (middle2, second2)], info_raw, weights, after=(beside,), flops=10**10)
    q2, kv2 = finish(raw2, cross2, third2, info_end, weights, gains, 10**10)
    shift2 = lax.ppermute(kv2, "tm", [(0, 1)])
    late = jnp.where(start, 0, 1)
    odd = pos % 2
    result = attend(q1, anchor, odd, [kv1, kv2], late, late)
    choice = jnp.minimum(pos, 1) + (pos == 1)
    return attend(q2, anchor, odd, [kv1, shift1, shift2], choice, 1 - late, result)


def solution(mesh):
    placed = (
        P("tm", None, "head"),
        P(None, "head"),
        P(None, "head"),
        P(None, "head"),
        P(None, "head"),
        P("head"),
        P("head"),
    )
    return jax.shard_map(
        per_device, mesh=mesh, in_specs=placed, out_specs=P("tm", None, "head"), check_vma=False
    )
```

```python
import functools

import jax
import jax.numpy as jnp
from jax import lax
from jax.experimental import pallas as pl
from jax.experimental.pallas import tpu as pltpu
from jax.sharding import PartitionSpec as P

DH = 128
BF16 = jnp.bfloat16
F32 = jnp.float32
ANY = pl.BlockSpec(memory_space=pl.ANY)


def normalized(part, gain):
    square = part * part
    high = square.astype(BF16)
    low = (square - high.astype(F32)).astype(BF16)
    ones = jnp.ones((2 * DH, DH), BF16)
    total = jnp.dot(jnp.concatenate([high, low], axis=1), ones, preferred_element_type=F32)
    return (part * lax.rsqrt(total * (1.0 / DH) + 1e-06) * gain).astype(BF16)


def store_head(raw, gains, q_out, kv_out, h):
    q_out[h] = normalized(raw[0], gains[0])
    kv_out[0, h] = normalized(raw[1], gains[1])
    kv_out[1, h] = raw[2].astype(BF16)


def project_body(pairs, extra, final, info, *refs):
    refs = list(refs)[extra:]
    count = len(pairs)
    groups = [[refs.pop(0) for _ in range(n)] for n in pairs]
    weights = [refs.pop(0) for _ in range(3)]
    gains = [refs.pop(0) for _ in range(2)] if final else None
    outs = [refs.pop(0) for _ in range(2)] if final else None
    acc, xbuf, sem = refs
    heads = weights[0].shape[1] // DH
    step = pl.program_id(0)

    @pl.when(step == 0)
    def _():
        for i, group in enumerate(groups):
            for j, source in enumerate(group):

                @pl.when((info[0] == j) | (len(group) == 1))
                def _(i=i, source=source):
                    pltpu.make_async_copy(source, xbuf.at[i], sem.at[i]).start()

    for i in range(count):

        @pl.when(step == i)
        def _(i=i):
            pltpu.make_async_copy(groups[i][0], xbuf.at[i], sem.at[i]).wait()
            weight = jnp.concatenate([w[...] for w in weights], axis=1)
            part = jnp.dot(xbuf[i], weight, preferred_element_type=F32)
            if final:
                acc[...] = part if i == 0 else acc[...] + part
            else:
                for group in range(3):
                    for h in range(heads):
                        columns = part[:, (group * heads + h) * DH : (group * heads + h + 1) * DH]
                        acc[group, h] = columns if i == 0 else acc[group, h] + columns

    if final:

        @pl.when(step == count - 1)
        def _():
            for h in range(heads):
                total = [acc[:, (group * heads + h) * DH : (group * heads + h + 1) * DH] for group in range(3)]
                store_head(total, [g[:, h * DH : (h + 1) * DH] for g in gains], *outs, h)


def project(sources, info, weights, gains=None, after=(), flops=1):
    pairs = [len(s) for s in sources]
    count = len(pairs)
    rows, chans = sources[0][0].shape
    width = weights[0].shape[1]
    heads = width // DH
    final = gains is not None
    a_spec = pl.BlockSpec((3, heads, rows, DH), lambda k, info: (0, 0, 0, 0))
    in_specs = [ANY] * (len(after) + sum(pairs)) + [pl.BlockSpec((chans, width), lambda k, info: (info[1 + k], 0))] * 3
    args = list(after) + [x for s in sources for x in s] + list(weights)
    scratch = [pltpu.VMEM((count, rows, chans), BF16), pltpu.SemaphoreType.DMA((count,))]
    raw = jax.ShapeDtypeStruct((3, heads, rows, DH), F32)
    if final:
        in_specs += [pl.BlockSpec((1, width), lambda k, info: (0, 0))] * 2
        args += [g[None] for g in gains]
        out_shape = [
            jax.ShapeDtypeStruct((heads, rows, DH), BF16),
            jax.ShapeDtypeStruct((2, heads, rows, DH), BF16),
        ]
        out_specs = [
            pl.BlockSpec((heads, rows, DH), lambda k, info: (0, 0, 0)),
            pl.BlockSpec((2, heads, rows, DH), lambda k, info: (0, 0, 0, 0)),
        ]
        scratch = [pltpu.VMEM((rows, 3 * width), F32)] + scratch
    else:
        out_shape, out_specs = raw, a_spec
    return pl.pallas_call(
        functools.partial(project_body, pairs, len(after), final),
        grid_spec=pltpu.PrefetchScalarGridSpec(
            num_scalar_prefetch=1,
            grid=(count,),
            in_specs=in_specs,
            out_specs=out_specs,
            scratch_shapes=scratch,
        ),
        out_shape=out_shape,
        compiler_params=pltpu.CompilerParams(vmem_limit_bytes=48 * 2**20),
        cost_estimate=pl.CostEstimate(flops=flops, bytes_accessed=1, transcendentals=0),
        name="project" + ("_end" if final else "_raw"),
    )(info, *args)


def finish_body(info, inner, outer, wq, wk, wv, qg, kg, raw, q_out, kv_out, rows, sem):
    @pl.when(pl.program_id(0) == 0)
    def _():
        for side, source in enumerate((inner, outer)):

            @pl.when(info[0] == side)
            def _(source=source):
                pltpu.make_async_copy(source, rows, sem).start()

        pltpu.make_async_copy(inner, rows, sem).wait()

    weight = jnp.concatenate([wq[...], wk[...], wv[...]], axis=1)
    part = jnp.dot(rows[...], weight, preferred_element_type=F32)
    total = [raw[group, 0] + part[:, group * DH : (group + 1) * DH] for group in range(3)]
    store_head(total, (qg[...], kg[...]), q_out, kv_out, 0)


def finish(raw, inner, outer, info, weights, gains, flops):
    rows, chans = inner.shape
    heads = raw.shape[1]
    w_spec = pl.BlockSpec((chans, DH), lambda h, info: (info[1], h))
    g_spec = pl.BlockSpec((1, DH), lambda h, info: (0, h))
    return pl.pallas_call(
        finish_body,
        grid_spec=pltpu.PrefetchScalarGridSpec(
            num_scalar_prefetch=1,
            grid=(heads,),
            in_specs=[ANY] * 2
            + [w_spec] * 3
            + [g_spec] * 2
            + [pl.BlockSpec((3, 1, rows, DH), lambda h, info: (0, h, 0, 0))],
            out_specs=[
                pl.BlockSpec((1, rows, DH), lambda h, info: (h, 0, 0)),
                pl.BlockSpec((2, 1, rows, DH), lambda h, info: (0, h, 0, 0)),
            ],
            scratch_shapes=[pltpu.VMEM((rows, chans), BF16), pltpu.SemaphoreType.DMA],
        ),
        out_shape=[
            jax.ShapeDtypeStruct((heads, rows, DH), BF16),
            jax.ShapeDtypeStruct((2, heads, rows, DH), BF16),
        ],
        compiler_params=pltpu.CompilerParams(vmem_limit_bytes=48 * 2**20),
        cost_estimate=pl.CostEstimate(flops=flops, bytes_accessed=1, transcendentals=0),
        name="finish",
    )(info, inner, outer, *weights, *(g[None] for g in gains), raw)


def attend_body(row_block, choices, fresh, info, *refs):
    refs = list(refs)
    query = refs.pop(0)
    options = [[refs.pop(0) for _ in range(n)] for n in choices]
    if not fresh:
        refs.pop(0)
    out, held, sem = refs
    h = pl.program_id(0)

    def fetch(part, source, head):
        return pltpu.make_async_copy(source.at[:, head], held.at[part, :, head], sem.at[part, head])

    @pl.when(h == 0)
    def _():
        for head in range(held.shape[2]):
            for part in range(2):
                for j, source in enumerate(options[part]):

                    @pl.when(info[2 * part] == j)
                    def _(part=part, source=source, head=head):
                        fetch(part, source, head).start()

    for part in range(2):
        fetch(part, options[part][0], h).wait()
    factor = 1.4426950408889634 / DH**0.5
    key = jnp.concatenate([held[0, 0, h], held[1, 0, h]], axis=0)
    value = jnp.concatenate([held[0, 1, h], held[1, 1, h]], axis=0)
    value = jnp.concatenate([value, jnp.ones_like(value)], axis=1)
    spans = [pl.ds(row, row_block) for row in range(0, query.shape[1], row_block)]

    def score(span):
        return lax.dot_general(
            query[0, span, :], key, (((1,), (1,)), ((), ())), preferred_element_type=F32
        )

    ahead = score(spans[0])
    for r, span in enumerate(spans):
        scores = ahead
        if r + 1 < len(spans):
            ahead = score(spans[r + 1])
        tops = [scores[:, c : c + DH] for c in range(0, scores.shape[1], DH)]
        top = jnp.max(functools.reduce(jnp.maximum, tops), axis=-1, keepdims=True)
        expo = jnp.exp2((scores - top) * factor).astype(BF16)
        result = jnp.dot(expo, value, preferred_element_type=F32)
        out[0, span, :] = (result[:, :DH] / result[:, DH:]).astype(BF16)


def attend(query, anchors, anchor, options, choice, frame, partly=None):
    heads, rows, _ = query.shape
    args = [query, *anchors, *options]
    aliases = {}
    if partly is not None:
        aliases = {1 + len(args): 0}
        args.append(partly)
    return pl.pallas_call(
        functools.partial(attend_body, 256, (len(anchors), len(options)), partly is None),
        grid_spec=pltpu.PrefetchScalarGridSpec(
            num_scalar_prefetch=1,
            grid=(heads,),
            in_specs=[pl.BlockSpec((1, rows, DH), lambda h, info: (h, 0, 0))] + [ANY] * (len(args) - 1),
            out_specs=pl.BlockSpec((1, rows, DH), lambda h, info: (info[1], 0, h)),
            scratch_shapes=[
                pltpu.VMEM((2, 2, heads, rows, DH), BF16),
                pltpu.SemaphoreType.DMA((2, heads)),
            ],
        ),
        out_shape=jax.ShapeDtypeStruct((2, rows, heads * DH), BF16),
        input_output_aliases=aliases,
        compiler_params=pltpu.CompilerParams(vmem_limit_bytes=32 * 2**20),
        cost_estimate=pl.CostEstimate(
            flops=8 * heads * rows * rows * DH,
            bytes_accessed=2 * heads * rows * DH * 6,
            transcendentals=2 * heads * rows * rows,
        ),
        name="attend",
    )(jnp.stack([anchor, frame, choice]).astype(jnp.int32), *args)


def broadcast_first(x, axis):
    count = lax.axis_size(axis)
    mine = lax.axis_index(axis)
    held = x
    for to in reversed(range(2, count, 2)):
        held = jnp.where(mine == to, lax.ppermute(x, axis, [(0, to)]), held)
    return held, lax.ppermute(held, axis, [(i, i + 1) for i in range(0, count, 2)])


INWARD = [(0, 1), (3, 2)]
MIDDLE = [(1, 2), (2, 1)]
OUTWARD = [(1, 0), (2, 3)]


def mix(before, centre, after, taps):
    before, centre, after = (v.astype(F32) for v in (before, centre, after))
    return (centre + taps[0] * before + taps[1] * centre + taps[2] * after).astype(BF16)


def split_rows(scales):
    parts, rest = [], scales
    for _ in range(3):
        part = lax.reduce_precision(rest, 8, 7)
        parts.append(part.astype(BF16))
        rest = rest - part
    rows = jnp.concatenate(parts, axis=0)
    return jnp.pad(rows, ((0, 16 - rows.shape[0]), (0, 0)))


def joined_rows(rows, count):
    high, middle, low = (rows[i * count : (i + 1) * count].astype(F32) for i in range(3))
    return high + middle + low


def per_device(frames, taps, w_query, w_key, w_value, q_gain, k_gain):
    count = lax.axis_size("tm")
    pos = lax.axis_index("tm")
    z = lax.axis_index("head").astype(jnp.int32)
    outer = (z == 0) | (z == 3)
    near, far = (z + 2) % 4, 3 - z
    side = outer.astype(jnp.int32)
    pair, second, third = z ^ 1, jnp.where(outer, near, far), jnp.where(outer, far, near)
    info = jnp.stack([side, z, pair, second, third])
    info_raw, info_end = jnp.stack([side, z, pair, second]), jnp.stack([side, third])
    hold = lax.optimization_barrier
    weights = (w_query, w_key, w_value)
    gains = (q_gain, k_gain)
    ups = [(i, i + 1) for i in range(count - 1)]
    downs = [(j, i) for i, j in ups]
    start = pos == 0

    def send(x, pairs):
        return lax.ppermute(x, "head", pairs)

    def mix_first(first, last, following, scales):
        return mix(
            jnp.where(start, jnp.zeros_like(first), first),
            jnp.where(start, first, last),
            jnp.where(start, last, following),
            scales,
        )

    def mix_second(first, last, following, preceding, scales):
        return mix(
            jnp.where(start, first, preceding),
            jnp.where(start, last, first),
            jnp.where(start, following, last),
            scales,
        )

    raw_first = send(frames[0], OUTWARD)
    following = lax.ppermute(frames[0], "tm", downs)
    mixed1 = mix_first(frames[0], frames[1], following, taps)
    last = jnp.concatenate([frames[1], split_rows(taps)], axis=0)
    later, last, mixed1 = hold((frames, last, mixed1))
    inward1, middle1 = send(mixed1, INWARD), send(mixed1, MIDDLE)
    raw_last = send(last, OUTWARD)
    later, raw_first = hold((later[1], raw_first))
    preceding = lax.ppermute(later, "tm", ups)
    mixed2 = mix_second(frames[0], frames[1], following, preceding, taps)
    raw_following = lax.ppermute(raw_first, "tm", downs)
    inward1, middle1 = hold((inward1, middle1))
    cross1, second1 = send(inward1, MIDDLE), send(middle1, OUTWARD)
    outer_taps = joined_rows(raw_last[later.shape[0] :], taps.shape[0])
    raw_last = raw_last[: later.shape[0]]
    raw_preceding = lax.ppermute(raw_last, "tm", ups)
    later2, cross1 = hold((mixed2, cross1))
    middle2, inward2 = send(later2, MIDDLE), send(mixed2, INWARD)
    level = (cross1, second1, raw_following, raw_preceding)
    cross1, second1, raw_following, raw_preceding = hold(level)
    third1 = send(cross1, OUTWARD)
    first1 = mix_first(raw_first, raw_last, raw_following, outer_taps)
    first2 = mix_second(raw_first, raw_last, raw_following, raw_preceding, outer_taps)
    middle2, inward2, first1, first2 = hold((middle2, inward2, first1, first2))
    cross2, second2 = send(inward2, MIDDLE), send(middle2, OUTWARD)

    sources1 = [(mixed1,), (inward1, first1), (middle1, second1), (cross1, third1)]
    q1, kv1 = project(sources1, info, weights, gains, after=(inward2, middle2), flops=10**10)
    beside = lax.ppermute(inward2[:16], "tm", [(i, i ^ 1) for i in range(count)])
    kv1, beside = hold((kv1, beside))
    third2 = send(cross2, OUTWARD)
    anchor = broadcast_first(kv1, "tm")
    later1, _ = hold((kv1, anchor[0]))
    shift1 = lax.ppermute(later1, "tm", [(i, i + 1) for i in range(1, count - 1)])
    raw2 = project([(mixed2,), (inward2, first2), (middle2, second2)], info_raw, weights, after=(beside,), flops=10**10)
    q2, kv2 = finish(raw2, cross2, third2, info_end, weights, gains, 10**10)
    shift2 = lax.ppermute(kv2, "tm", [(0, 1)])
    late = jnp.where(start, 0, 1)
    odd = pos % 2
    result = attend(q1, anchor, odd, [kv1, kv2], late, late)
    choice = jnp.minimum(pos, 1) + (pos == 1)
    return attend(q2, anchor, odd, [kv1, shift1, shift2], choice, 1 - late, result)


def solution(mesh):
    placed = (
        P("tm", None, "head"),
        P(None, "head"),
        P(None, "head"),
        P(None, "head"),
        P(None, "head"),
        P("head"),
        P("head"),
    )
    return jax.shard_map(
        per_device, mesh=mesh, in_specs=placed, out_specs=P("tm", None, "head"), check_vma=False
    )
```

```python
import functools

import jax
import jax.numpy as jnp
from jax import lax
from jax.experimental import pallas as pl
from jax.experimental.pallas import tpu as pltpu
from jax.sharding import PartitionSpec as P

DH = 128
BF16 = jnp.bfloat16
F32 = jnp.float32
ANY = pl.BlockSpec(memory_space=pl.ANY)


def normalized(part, gain):
    square = part * part
    high = square.astype(BF16)
    low = (square - high.astype(F32)).astype(BF16)
    ones = jnp.ones((2 * DH, DH), BF16)
    total = jnp.dot(jnp.concatenate([high, low], axis=1), ones, preferred_element_type=F32)
    return (part * lax.rsqrt(total * (1.0 / DH) + 1e-06) * gain).astype(BF16)


def store_head(raw, gains, q_out, kv_out, h):
    q_out[h] = normalized(raw[0], gains[0])
    kv_out[0, h] = normalized(raw[1], gains[1])
    kv_out[1, h] = raw[2].astype(BF16)


def project_body(pairs, extra, final, info, *refs):
    refs = list(refs)[extra:]
    count = len(pairs)
    groups = [[refs.pop(0) for _ in range(n)] for n in pairs]
    weights = [refs.pop(0) for _ in range(3)]
    gains = [refs.pop(0) for _ in range(2)] if final else None
    outs = [refs.pop(0) for _ in range(2)] if final else None
    acc, xbuf, sem = refs
    heads = weights[0].shape[1] // DH
    step = pl.program_id(0)

    @pl.when(step == 0)
    def _():
        for i, group in enumerate(groups):
            for j, source in enumerate(group):

                @pl.when((info[0] == j) | (len(group) == 1))
                def _(i=i, source=source):
                    pltpu.make_async_copy(source, xbuf.at[i], sem.at[i]).start()

    for i in range(count):

        @pl.when(step == i)
        def _(i=i):
            pltpu.make_async_copy(groups[i][0], xbuf.at[i], sem.at[i]).wait()
            weight = jnp.concatenate([w[...] for w in weights], axis=1)
            part = jnp.dot(xbuf[i], weight, preferred_element_type=F32)
            if final:
                acc[...] = part if i == 0 else acc[...] + part
            else:
                for group in range(3):
                    for h in range(heads):
                        columns = part[:, (group * heads + h) * DH : (group * heads + h + 1) * DH]
                        acc[group, h] = columns if i == 0 else acc[group, h] + columns

    if final:

        @pl.when(step == count - 1)
        def _():
            for h in range(heads):
                total = [acc[:, (group * heads + h) * DH : (group * heads + h + 1) * DH] for group in range(3)]
                store_head(total, [g[:, h * DH : (h + 1) * DH] for g in gains], *outs, h)


def project(sources, info, weights, gains=None, after=(), flops=1):
    pairs = [len(s) for s in sources]
    count = len(pairs)
    rows, chans = sources[0][0].shape
    width = weights[0].shape[1]
    heads = width // DH
    final = gains is not None
    a_spec = pl.BlockSpec((3, heads, rows, DH), lambda k, info: (0, 0, 0, 0))
    in_specs = [ANY] * (len(after) + sum(pairs)) + [pl.BlockSpec((chans, width), lambda k, info: (info[1 + k], 0))] * 3
    args = list(after) + [x for s in sources for x in s] + list(weights)
    scratch = [pltpu.VMEM((count, rows, chans), BF16), pltpu.SemaphoreType.DMA((count,))]
    raw = jax.ShapeDtypeStruct((3, heads, rows, DH), F32)
    if final:
        in_specs += [pl.BlockSpec((1, width), lambda k, info: (0, 0))] * 2
        args += [g[None] for g in gains]
        out_shape = [
            jax.ShapeDtypeStruct((heads, rows, DH), BF16),
            jax.ShapeDtypeStruct((2, heads, rows, DH), BF16),
        ]
        out_specs = [
            pl.BlockSpec((heads, rows, DH), lambda k, info: (0, 0, 0)),
            pl.BlockSpec((2, heads, rows, DH), lambda k, info: (0, 0, 0, 0)),
        ]
        scratch = [pltpu.VMEM((rows, 3 * width), F32)] + scratch
    else:
        out_shape, out_specs = raw, a_spec
    return pl.pallas_call(
        functools.partial(project_body, pairs, len(after), final),
        grid_spec=pltpu.PrefetchScalarGridSpec(
            num_scalar_prefetch=1,
            grid=(count,),
            in_specs=in_specs,
            out_specs=out_specs,
            scratch_shapes=scratch,
        ),
        out_shape=out_shape,
        compiler_params=pltpu.CompilerParams(vmem_limit_bytes=48 * 2**20),
        cost_estimate=pl.CostEstimate(flops=flops, bytes_accessed=1, transcendentals=0),
        name="project" + ("_end" if final else "_raw"),
    )(info, *args)


def finish_body(info, inner, outer, wq, wk, wv, qg, kg, raw, q_out, kv_out, rows, sem):
    @pl.when(pl.program_id(0) == 0)
    def _():
        for side, source in enumerate((inner, outer)):

            @pl.when(info[0] == side)
            def _(source=source):
                pltpu.make_async_copy(source, rows, sem).start()

        pltpu.make_async_copy(inner, rows, sem).wait()

    weight = jnp.concatenate([wq[...], wk[...], wv[...]], axis=1)
    part = jnp.dot(rows[...], weight, preferred_element_type=F32)
    total = [raw[group, 0] + part[:, group * DH : (group + 1) * DH] for group in range(3)]
    store_head(total, (qg[...], kg[...]), q_out, kv_out, 0)


def finish(raw, inner, outer, info, weights, gains, flops):
    rows, chans = inner.shape
    heads = raw.shape[1]
    w_spec = pl.BlockSpec((chans, DH), lambda h, info: (info[1], h))
    g_spec = pl.BlockSpec((1, DH), lambda h, info: (0, h))
    return pl.pallas_call(
        finish_body,
        grid_spec=pltpu.PrefetchScalarGridSpec(
            num_scalar_prefetch=1,
            grid=(heads,),
            in_specs=[ANY] * 2
            + [w_spec] * 3
            + [g_spec] * 2
            + [pl.BlockSpec((3, 1, rows, DH), lambda h, info: (0, h, 0, 0))],
            out_specs=[
                pl.BlockSpec((1, rows, DH), lambda h, info: (h, 0, 0)),
                pl.BlockSpec((2, 1, rows, DH), lambda h, info: (0, h, 0, 0)),
            ],
            scratch_shapes=[pltpu.VMEM((rows, chans), BF16), pltpu.SemaphoreType.DMA],
        ),
        out_shape=[
            jax.ShapeDtypeStruct((heads, rows, DH), BF16),
            jax.ShapeDtypeStruct((2, heads, rows, DH), BF16),
        ],
        compiler_params=pltpu.CompilerParams(vmem_limit_bytes=48 * 2**20),
        cost_estimate=pl.CostEstimate(flops=flops, bytes_accessed=1, transcendentals=0),
        name="finish",
    )(info, inner, outer, *weights, *(g[None] for g in gains), raw)


def attend_body(row_block, choices, fresh, info, *refs):
    refs = list(refs)
    query = refs.pop(0)
    options = [[refs.pop(0) for _ in range(n)] for n in choices]
    if not fresh:
        refs.pop(0)
    out, held, sem = refs
    h = pl.program_id(0)

    def fetch(part, source, head):
        return pltpu.make_async_copy(source.at[:, head], held.at[part, :, head], sem.at[part, head])

    @pl.when(h == 0)
    def _():
        for head in range(held.shape[2]):
            for part in range(2):
                for j, source in enumerate(options[part]):

                    @pl.when(info[2 * part] == j)
                    def _(part=part, source=source, head=head):
                        fetch(part, source, head).start()

    for part in range(2):
        fetch(part, options[part][0], h).wait()
    factor = 1.4426950408889634 / DH**0.5
    key = jnp.concatenate([held[0, 0, h], held[1, 0, h]], axis=0)
    value = jnp.concatenate([held[0, 1, h], held[1, 1, h]], axis=0)
    value = jnp.concatenate([value, jnp.ones_like(value)], axis=1)
    spans = [pl.ds(row, row_block) for row in range(0, query.shape[1], row_block)]

    def score(span):
        return lax.dot_general(
            query[0, span, :], key, (((1,), (1,)), ((), ())), preferred_element_type=F32
        )

    ahead = score(spans[0])
    for r, span in enumerate(spans):
        scores = ahead
        if r + 1 < len(spans):
            ahead = score(spans[r + 1])
        tops = [scores[:, c : c + DH] for c in range(0, scores.shape[1], DH)]
        top = jnp.max(functools.reduce(jnp.maximum, tops), axis=-1, keepdims=True)
        expo = jnp.exp2((scores - top) * factor).astype(BF16)
        result = jnp.dot(expo, value, preferred_element_type=F32)
        out[0, span, :] = (result[:, :DH] / result[:, DH:]).astype(BF16)


def attend(query, anchors, anchor, options, choice, frame, partly=None):
    heads, rows, _ = query.shape
    args = [query, *anchors, *options]
    aliases = {}
    if partly is not None:
        aliases = {1 + len(args): 0}
        args.append(partly)
    return pl.pallas_call(
        functools.partial(attend_body, 256, (len(anchors), len(options)), partly is None),
        grid_spec=pltpu.PrefetchScalarGridSpec(
            num_scalar_prefetch=1,
            grid=(heads,),
            in_specs=[pl.BlockSpec((1, rows, DH), lambda h, info: (h, 0, 0))] + [ANY] * (len(args) - 1),
            out_specs=pl.BlockSpec((1, rows, DH), lambda h, info: (info[1], 0, h)),
            scratch_shapes=[
                pltpu.VMEM((2, 2, heads, rows, DH), BF16),
                pltpu.SemaphoreType.DMA((2, heads)),
            ],
        ),
        out_shape=jax.ShapeDtypeStruct((2, rows, heads * DH), BF16),
        input_output_aliases=aliases,
        compiler_params=pltpu.CompilerParams(vmem_limit_bytes=32 * 2**20),
        cost_estimate=pl.CostEstimate(
            flops=8 * heads * rows * rows * DH,
            bytes_accessed=2 * heads * rows * DH * 6,
            transcendentals=2 * heads * rows * rows,
        ),
        name="attend",
    )(jnp.stack([anchor, frame, choice]).astype(jnp.int32), *args)


def broadcast_first(x, axis):
    count = lax.axis_size(axis)
    mine = lax.axis_index(axis)
    held = x
    for to in reversed(range(2, count, 2)):
        held = jnp.where(mine == to, lax.ppermute(x, axis, [(0, to)]), held)
    return held, lax.ppermute(held, axis, [(i, i + 1) for i in range(0, count, 2)])


INWARD = [(0, 1), (3, 2)]
MIDDLE = [(1, 2), (2, 1)]
OUTWARD = [(1, 0), (2, 3)]


def mix(before, centre, after, taps):
    before, centre, after = (v.astype(F32) for v in (before, centre, after))
    return (centre + taps[0] * before + taps[1] * centre + taps[2] * after).astype(BF16)


def split_rows(scales):
    parts, rest = [], scales
    for _ in range(3):
        part = lax.reduce_precision(rest, 8, 7)
        parts.append(part.astype(BF16))
        rest = rest - part
    rows = jnp.concatenate(parts, axis=0)
    return jnp.pad(rows, ((0, 16 - rows.shape[0]), (0, 0)))


def joined_rows(rows, count):
    high, middle, low = (rows[i * count : (i + 1) * count].astype(F32) for i in range(3))
    return high + middle + low


def per_device(frames, taps, w_query, w_key, w_value, q_gain, k_gain):
    count = lax.axis_size("tm")
    pos = lax.axis_index("tm")
    z = lax.axis_index("head").astype(jnp.int32)
    outer = (z == 0) | (z == 3)
    near, far = (z + 2) % 4, 3 - z
    side = outer.astype(jnp.int32)
    pair, second, third = z ^ 1, jnp.where(outer, near, far), jnp.where(outer, far, near)
    info = jnp.stack([side, z, pair, second, third])
    info_raw, info_end = jnp.stack([side, z, pair, second]), jnp.stack([side, third])
    hold = lax.optimization_barrier
    weights = (w_query, w_key, w_value)
    gains = (q_gain, k_gain)
    ups = [(i, i + 1) for i in range(count - 1)]
    downs = [(j, i) for i, j in ups]
    start = pos == 0

    def send(x, pairs):
        return lax.ppermute(x, "head", pairs)

    def mix_first(first, last, following, scales):
        return mix(
            jnp.where(start, jnp.zeros_like(first), first),
            jnp.where(start, first, last),
            jnp.where(start, last, following),
            scales,
        )

    def mix_second(first, last, following, preceding, scales):
        return mix(
            jnp.where(start, first, preceding),
            jnp.where(start, last, first),
            jnp.where(start, following, last),
            scales,
        )

    raw_first = send(frames[0], OUTWARD)
    following = lax.ppermute(frames[0], "tm", downs)
    mixed1 = mix_first(frames[0], frames[1], following, taps)
    last = jnp.concatenate([frames[1], split_rows(taps)], axis=0)
    later, last, mixed1 = hold((frames, last, mixed1))
    inward1, middle1 = send(mixed1, INWARD), send(mixed1, MIDDLE)
    raw_last = send(last, OUTWARD)
    later, raw_first = hold((later[1], raw_first))
    preceding = lax.ppermute(later, "tm", ups)
    mixed2 = mix_second(frames[0], frames[1], following, preceding, taps)
    raw_following = lax.ppermute(raw_first, "tm", downs)
    inward1, middle1 = hold((inward1, middle1))
    cross1, second1 = send(inward1, MIDDLE), send(middle1, OUTWARD)
    outer_taps = joined_rows(raw_last[later.shape[0] :], taps.shape[0])
    raw_last = raw_last[: later.shape[0]]
    raw_preceding = lax.ppermute(raw_last, "tm", ups)
    middle2, inward2 = send(mixed2, MIDDLE), send(mixed2, INWARD)
    level = (cross1, second1, raw_following, raw_preceding)
    cross1, second1, raw_following, raw_preceding = hold(level)
    third1 = send(cross1, OUTWARD)
    first1 = mix_first(raw_first, raw_last, raw_following, outer_taps)
    first2 = mix_second(raw_first, raw_last, raw_following, raw_preceding, outer_taps)
    middle2, first1, first2 = hold((middle2, first1, first2))
    cross2, second2 = send(inward2, MIDDLE), send(middle2, OUTWARD)

    sources1 = [(mixed1,), (inward1, first1), (middle1, second1), (cross1, third1)]
    q1, kv1 = project(sources1, info, weights, gains, after=(inward2, middle2), flops=10**10)
    beside = lax.ppermute(inward2[:16], "tm", [(i, i ^ 1) for i in range(count)])
    kv1, beside = hold((kv1, beside))
    third2 = send(cross2, OUTWARD)
    anchor = broadcast_first(kv1, "tm")
    later1, _ = hold((kv1, anchor[0]))
    shift1 = lax.ppermute(later1, "tm", [(i, i + 1) for i in range(1, count - 1)])
    raw2 = project([(mixed2,), (inward2, first2), (middle2, second2)], info_raw, weights, after=(beside,), flops=10**10)
    q2, kv2 = finish(raw2, cross2, third2, info_end, weights, gains, 10**10)
    shift2 = lax.ppermute(kv2, "tm", [(0, 1)])
    anchor, shift1 = hold((anchor, shift1))
    late = jnp.where(start, 0, 1)
    odd = pos % 2
    result = attend(q1, anchor, odd, [kv1, kv2], late, late)
    choice = jnp.minimum(pos, 1) + (pos == 1)
    return attend(q2, anchor, odd, [kv1, shift1, shift2], choice, 1 - late, result)


def solution(mesh):
    placed = (
        P("tm", None, "head"),
        P(None, "head"),
        P(None, "head"),
        P(None, "head"),
        P(None, "head"),
        P("head"),
        P("head"),
    )
    return jax.shard_map(
        per_device, mesh=mesh, in_specs=placed, out_specs=P("tm", None, "head"), check_vma=False
    )
```

```python
import functools

import jax
import jax.numpy as jnp
from jax import lax
from jax.experimental import pallas as pl
from jax.experimental.pallas import tpu as pltpu
from jax.sharding import PartitionSpec as P

DH = 128
BF16 = jnp.bfloat16
F32 = jnp.float32
ANY = pl.BlockSpec(memory_space=pl.ANY)


def normalized(part, gain):
    square = part * part
    high = square.astype(BF16)
    low = (square - high.astype(F32)).astype(BF16)
    ones = jnp.ones((2 * DH, DH), BF16)
    total = jnp.dot(jnp.concatenate([high, low], axis=1), ones, preferred_element_type=F32)
    return (part * lax.rsqrt(total * (1.0 / DH) + 1e-06) * gain).astype(BF16)


def store_head(raw, gains, q_out, kv_out, h):
    q_out[h] = normalized(raw[0], gains[0])
    kv_out[0, h] = normalized(raw[1], gains[1])
    kv_out[1, h] = raw[2].astype(BF16)


def project_body(pairs, extra, final, info, *refs):
    refs = list(refs)[extra:]
    count = len(pairs)
    groups = [[refs.pop(0) for _ in range(n)] for n in pairs]
    weights = [refs.pop(0) for _ in range(3)]
    gains = [refs.pop(0) for _ in range(2)] if final else None
    outs = [refs.pop(0) for _ in range(2)] if final else None
    acc, xbuf, sem = refs
    heads = weights[0].shape[1] // DH
    step = pl.program_id(0)

    @pl.when(step == 0)
    def _():
        for i, group in enumerate(groups):
            for j, source in enumerate(group):

                @pl.when((info[0] == j) | (len(group) == 1))
                def _(i=i, source=source):
                    pltpu.make_async_copy(source, xbuf.at[i], sem.at[i]).start()

    for i in range(count):

        @pl.when(step == i)
        def _(i=i):
            pltpu.make_async_copy(groups[i][0], xbuf.at[i], sem.at[i]).wait()
            weight = jnp.concatenate([w[...] for w in weights], axis=1)
            part = jnp.dot(xbuf[i], weight, preferred_element_type=F32)
            if final:
                acc[...] = part if i == 0 else acc[...] + part
            else:
                for group in range(3):
                    for h in range(heads):
                        columns = part[:, (group * heads + h) * DH : (group * heads + h + 1) * DH]
                        acc[group, h] = columns if i == 0 else acc[group, h] + columns

    if final:

        @pl.when(step == count - 1)
        def _():
            for h in range(heads):
                total = [acc[:, (group * heads + h) * DH : (group * heads + h + 1) * DH] for group in range(3)]
                store_head(total, [g[:, h * DH : (h + 1) * DH] for g in gains], *outs, h)


def project(sources, info, weights, gains=None, after=(), flops=1):
    pairs = [len(s) for s in sources]
    count = len(pairs)
    rows, chans = sources[0][0].shape
    width = weights[0].shape[1]
    heads = width // DH
    final = gains is not None
    a_spec = pl.BlockSpec((3, heads, rows, DH), lambda k, info: (0, 0, 0, 0))
    in_specs = [ANY] * (len(after) + sum(pairs)) + [pl.BlockSpec((chans, width), lambda k, info: (info[1 + k], 0))] * 3
    args = list(after) + [x for s in sources for x in s] + list(weights)
    scratch = [pltpu.VMEM((count, rows, chans), BF16), pltpu.SemaphoreType.DMA((count,))]
    raw = jax.ShapeDtypeStruct((3, heads, rows, DH), F32)
    if final:
        in_specs += [pl.BlockSpec((1, width), lambda k, info: (0, 0))] * 2
        args += [g[None] for g in gains]
        out_shape = [
            jax.ShapeDtypeStruct((heads, rows, DH), BF16),
            jax.ShapeDtypeStruct((2, heads, rows, DH), BF16),
        ]
        out_specs = [
            pl.BlockSpec((heads, rows, DH), lambda k, info: (0, 0, 0)),
            pl.BlockSpec((2, heads, rows, DH), lambda k, info: (0, 0, 0, 0)),
        ]
        scratch = [pltpu.VMEM((rows, 3 * width), F32)] + scratch
    else:
        out_shape, out_specs = raw, a_spec
    return pl.pallas_call(
        functools.partial(project_body, pairs, len(after), final),
        grid_spec=pltpu.PrefetchScalarGridSpec(
            num_scalar_prefetch=1,
            grid=(count,),
            in_specs=in_specs,
            out_specs=out_specs,
            scratch_shapes=scratch,
        ),
        out_shape=out_shape,
        compiler_params=pltpu.CompilerParams(vmem_limit_bytes=48 * 2**20),
        cost_estimate=pl.CostEstimate(flops=flops, bytes_accessed=1, transcendentals=0),
        name="project" + ("_end" if final else "_raw"),
    )(info, *args)


def finish_body(info, inner, outer, wq, wk, wv, qg, kg, raw, q_out, kv_out, rows, sem):
    @pl.when(pl.program_id(0) == 0)
    def _():
        for side, source in enumerate((inner, outer)):

            @pl.when(info[0] == side)
            def _(source=source):
                pltpu.make_async_copy(source, rows, sem).start()

        pltpu.make_async_copy(inner, rows, sem).wait()

    weight = jnp.concatenate([wq[...], wk[...], wv[...]], axis=1)
    part = jnp.dot(rows[...], weight, preferred_element_type=F32)
    total = [raw[group, 0] + part[:, group * DH : (group + 1) * DH] for group in range(3)]
    store_head(total, (qg[...], kg[...]), q_out, kv_out, 0)


def finish(raw, inner, outer, info, weights, gains, flops):
    rows, chans = inner.shape
    heads = raw.shape[1]
    w_spec = pl.BlockSpec((chans, DH), lambda h, info: (info[1], h))
    g_spec = pl.BlockSpec((1, DH), lambda h, info: (0, h))
    return pl.pallas_call(
        finish_body,
        grid_spec=pltpu.PrefetchScalarGridSpec(
            num_scalar_prefetch=1,
            grid=(heads,),
            in_specs=[ANY] * 2
            + [w_spec] * 3
            + [g_spec] * 2
            + [pl.BlockSpec((3, 1, rows, DH), lambda h, info: (0, h, 0, 0))],
            out_specs=[
                pl.BlockSpec((1, rows, DH), lambda h, info: (h, 0, 0)),
                pl.BlockSpec((2, 1, rows, DH), lambda h, info: (0, h, 0, 0)),
            ],
            scratch_shapes=[pltpu.VMEM((rows, chans), BF16), pltpu.SemaphoreType.DMA],
        ),
        out_shape=[
            jax.ShapeDtypeStruct((heads, rows, DH), BF16),
            jax.ShapeDtypeStruct((2, heads, rows, DH), BF16),
        ],
        compiler_params=pltpu.CompilerParams(vmem_limit_bytes=48 * 2**20),
        cost_estimate=pl.CostEstimate(flops=flops, bytes_accessed=1, transcendentals=0),
        name="finish",
    )(info, inner, outer, *weights, *(g[None] for g in gains), raw)


def attend_body(row_block, choices, fresh, info, *refs):
    refs = list(refs)
    query = refs.pop(0)
    options = [[refs.pop(0) for _ in range(n)] for n in choices]
    if not fresh:
        refs.pop(0)
    out, held, sem = refs
    h = pl.program_id(0)

    def fetch(part, source, head):
        return pltpu.make_async_copy(source.at[:, head], held.at[part, :, head], sem.at[part, head])

    @pl.when(h == 0)
    def _():
        for head in range(held.shape[2]):
            for part in range(2):
                for j, source in enumerate(options[part]):

                    @pl.when(info[2 * part] == j)
                    def _(part=part, source=source, head=head):
                        fetch(part, source, head).start()

    for part in range(2):
        fetch(part, options[part][0], h).wait()
    factor = 1.4426950408889634 / DH**0.5
    key = jnp.concatenate([held[0, 0, h], held[1, 0, h]], axis=0)
    value = jnp.concatenate([held[0, 1, h], held[1, 1, h]], axis=0)
    value = jnp.concatenate([value, jnp.ones_like(value)], axis=1)
    spans = [pl.ds(row, row_block) for row in range(0, query.shape[1], row_block)]

    def score(span):
        return lax.dot_general(
            query[0, span, :], key, (((1,), (1,)), ((), ())), preferred_element_type=F32
        )

    ahead = score(spans[0])
    for r, span in enumerate(spans):
        scores = ahead
        if r + 1 < len(spans):
            ahead = score(spans[r + 1])
        tops = [scores[:, c : c + DH] for c in range(0, scores.shape[1], DH)]
        top = jnp.max(functools.reduce(jnp.maximum, tops), axis=-1, keepdims=True)
        expo = jnp.exp2((scores - top) * factor).astype(BF16)
        result = jnp.dot(expo, value, preferred_element_type=F32)
        out[0, span, :] = (result[:, :DH] / result[:, DH:]).astype(BF16)


def attend(query, anchors, anchor, options, choice, frame, partly=None):
    heads, rows, _ = query.shape
    args = [query, *anchors, *options]
    aliases = {}
    if partly is not None:
        aliases = {1 + len(args): 0}
        args.append(partly)
    return pl.pallas_call(
        functools.partial(attend_body, 256, (len(anchors), len(options)), partly is None),
        grid_spec=pltpu.PrefetchScalarGridSpec(
            num_scalar_prefetch=1,
            grid=(heads,),
            in_specs=[pl.BlockSpec((1, rows, DH), lambda h, info: (h, 0, 0))] + [ANY] * (len(args) - 1),
            out_specs=pl.BlockSpec((1, rows, DH), lambda h, info: (info[1], 0, h)),
            scratch_shapes=[
                pltpu.VMEM((2, 2, heads, rows, DH), BF16),
                pltpu.SemaphoreType.DMA((2, heads)),
            ],
        ),
        out_shape=jax.ShapeDtypeStruct((2, rows, heads * DH), BF16),
        input_output_aliases=aliases,
        compiler_params=pltpu.CompilerParams(vmem_limit_bytes=32 * 2**20),
        cost_estimate=pl.CostEstimate(
            flops=8 * heads * rows * rows * DH,
            bytes_accessed=2 * heads * rows * DH * 6,
            transcendentals=2 * heads * rows * rows,
        ),
        name="attend",
    )(jnp.stack([anchor, frame, choice]).astype(jnp.int32), *args)


def broadcast_first(x, axis):
    count = lax.axis_size(axis)
    mine = lax.axis_index(axis)
    held = x
    for to in range(2, count, 2):
        held = jnp.where(mine == to, lax.ppermute(x, axis, [(0, to)]), held)
    return held, lax.ppermute(held, axis, [(i, i + 1) for i in range(0, count, 2)])


INWARD = [(0, 1), (3, 2)]
MIDDLE = [(1, 2), (2, 1)]
OUTWARD = [(1, 0), (2, 3)]


def mix(before, centre, after, taps):
    before, centre, after = (v.astype(F32) for v in (before, centre, after))
    return (centre + taps[0] * before + taps[1] * centre + taps[2] * after).astype(BF16)


def split_rows(scales):
    parts, rest = [], scales
    for _ in range(3):
        part = lax.reduce_precision(rest, 8, 7)
        parts.append(part.astype(BF16))
        rest = rest - part
    rows = jnp.concatenate(parts, axis=0)
    return jnp.pad(rows, ((0, 16 - rows.shape[0]), (0, 0)))


def joined_rows(rows, count):
    high, middle, low = (rows[i * count : (i + 1) * count].astype(F32) for i in range(3))
    return high + middle + low


def per_device(frames, taps, w_query, w_key, w_value, q_gain, k_gain):
    count = lax.axis_size("tm")
    pos = lax.axis_index("tm")
    z = lax.axis_index("head").astype(jnp.int32)
    outer = (z == 0) | (z == 3)
    near, far = (z + 2) % 4, 3 - z
    side = outer.astype(jnp.int32)
    pair, second, third = z ^ 1, jnp.where(outer, near, far), jnp.where(outer, far, near)
    info = jnp.stack([side, z, pair, second, third])
    info_raw, info_end = jnp.stack([side, z, pair, second]), jnp.stack([side, third])
    hold = lax.optimization_barrier
    weights = (w_query, w_key, w_value)
    gains = (q_gain, k_gain)
    ups = [(i, i + 1) for i in range(count - 1)]
    downs = [(j, i) for i, j in ups]
    start = pos == 0

    def send(x, pairs):
        return lax.ppermute(x, "head", pairs)

    def mix_first(first, last, following, scales):
        return mix(
            jnp.where(start, jnp.zeros_like(first), first),
            jnp.where(start, first, last),
            jnp.where(start, last, following),
            scales,
        )

    def mix_second(first, last, following, preceding, scales):
        return mix(
            jnp.where(start, first, preceding),
            jnp.where(start, last, first),
            jnp.where(start, following, last),
            scales,
        )

    raw_first = send(frames[0], OUTWARD)
    following = lax.ppermute(frames[0], "tm", downs)
    mixed1 = mix_first(frames[0], frames[1], following, taps)
    last = jnp.concatenate([frames[1], split_rows(taps)], axis=0)
    later, last, mixed1 = hold((frames, last, mixed1))
    inward1, middle1 = send(mixed1, INWARD), send(mixed1, MIDDLE)
    raw_last = send(last, OUTWARD)
    later, raw_first = hold((later[1], raw_first))
    preceding = lax.ppermute(later, "tm", ups)
    mixed2 = mix_second(frames[0], frames[1], following, preceding, taps)
    raw_following = lax.ppermute(raw_first, "tm", downs)
    inward1, middle1 = hold((inward1, middle1))
    cross1, second1 = send(inward1, MIDDLE), send(middle1, OUTWARD)
    outer_taps = joined_rows(raw_last[later.shape[0] :], taps.shape[0])
    raw_last = raw_last[: later.shape[0]]
    raw_preceding = lax.ppermute(raw_last, "tm", ups)
    middle2, inward2 = send(mixed2, MIDDLE), send(mixed2, INWARD)
    level = (cross1, second1, raw_following, raw_preceding)
    cross1, second1, raw_following, raw_preceding = hold(level)
    third1 = send(cross1, OUTWARD)
    first1 = mix_first(raw_first, raw_last, raw_following, outer_taps)
    first2 = mix_second(raw_first, raw_last, raw_following, raw_preceding, outer_taps)
    middle2, first1, first2 = hold((middle2, first1, first2))
    cross2, second2 = send(inward2, MIDDLE), send(middle2, OUTWARD)

    sources1 = [(mixed1,), (inward1, first1), (middle1, second1), (cross1, third1)]
    q1, kv1 = project(sources1, info, weights, gains, after=(inward2, middle2), flops=10**10)
    beside = lax.ppermute(inward2[:16], "tm", [(i, i ^ 1) for i in range(count)])
    kv1, beside = hold((kv1, beside))
    third2 = send(cross2, OUTWARD)
    anchor = broadcast_first(kv1, "tm")
    later1, _ = hold((kv1, anchor[0]))
    shift1 = lax.ppermute(later1, "tm", [(i, i + 1) for i in range(1, count - 1)])
    raw2 = project([(mixed2,), (inward2, first2), (middle2, second2)], info_raw, weights, after=(beside,), flops=10**10)
    q2, kv2 = finish(raw2, cross2, third2, info_end, weights, gains, 10**10)
    shift2 = lax.ppermute(kv2, "tm", [(0, 1)])
    anchor, shift1 = hold((anchor, shift1))
    late = jnp.where(start, 0, 1)
    odd = pos % 2
    result = attend(q1, anchor, odd, [kv1, kv2], late, late)
    choice = jnp.minimum(pos, 1) + (pos == 1)
    return attend(q2, anchor, odd, [kv1, shift1, shift2], choice, 1 - late, result)


def solution(mesh):
    placed = (
        P("tm", None, "head"),
        P(None, "head"),
        P(None, "head"),
        P(None, "head"),
        P(None, "head"),
        P("head"),
        P("head"),
    )
    return jax.shard_map(
        per_device, mesh=mesh, in_specs=placed, out_specs=P("tm", None, "head"), check_vma=False
    )
```

```python
import functools

import jax
import jax.numpy as jnp
from jax import lax
from jax.experimental import pallas as pl
from jax.experimental.pallas import tpu as pltpu
from jax.sharding import PartitionSpec as P

DH = 128
BF16 = jnp.bfloat16
F32 = jnp.float32
ANY = pl.BlockSpec(memory_space=pl.ANY)


def normalized(part, gain):
    square = part * part
    high = square.astype(BF16)
    low = (square - high.astype(F32)).astype(BF16)
    ones = jnp.ones((2 * DH, DH), BF16)
    total = jnp.dot(jnp.concatenate([high, low], axis=1), ones, preferred_element_type=F32)
    return (part * lax.rsqrt(total * (1.0 / DH) + 1e-06) * gain).astype(BF16)


def store_head(raw, gains, q_out, kv_out, h):
    q_out[h] = normalized(raw[0], gains[0])
    kv_out[0, h] = normalized(raw[1], gains[1])
    kv_out[1, h] = raw[2].astype(BF16)


def project_body(pairs, extra, final, info, *refs):
    refs = list(refs)[extra:]
    count = len(pairs)
    groups = [[refs.pop(0) for _ in range(n)] for n in pairs]
    weights = [refs.pop(0) for _ in range(3)]
    gains = [refs.pop(0) for _ in range(2)] if final else None
    outs = [refs.pop(0) for _ in range(2)] if final else None
    acc, xbuf, sem = refs
    heads = weights[0].shape[1] // DH
    step = pl.program_id(0)

    @pl.when(step == 0)
    def _():
        for i, group in enumerate(groups):
            for j, source in enumerate(group):

                @pl.when((info[0] == j) | (len(group) == 1))
                def _(i=i, source=source):
                    pltpu.make_async_copy(source, xbuf.at[i], sem.at[i]).start()

    for i in range(count):

        @pl.when(step == i)
        def _(i=i):
            pltpu.make_async_copy(groups[i][0], xbuf.at[i], sem.at[i]).wait()
            weight = jnp.concatenate([w[...] for w in weights], axis=1)
            part = jnp.dot(xbuf[i], weight, preferred_element_type=F32)
            if final:
                acc[...] = part if i == 0 else acc[...] + part
            else:
                for group in range(3):
                    for h in range(heads):
                        columns = part[:, (group * heads + h) * DH : (group * heads + h + 1) * DH]
                        acc[group, h] = columns if i == 0 else acc[group, h] + columns

    if final:

        @pl.when(step == count - 1)
        def _():
            for h in range(heads):
                total = [acc[:, (group * heads + h) * DH : (group * heads + h + 1) * DH] for group in range(3)]
                store_head(total, [g[:, h * DH : (h + 1) * DH] for g in gains], *outs, h)


def project(sources, info, weights, gains=None, after=(), flops=1):
    pairs = [len(s) for s in sources]
    count = len(pairs)
    rows, chans = sources[0][0].shape
    width = weights[0].shape[1]
    heads = width // DH
    final = gains is not None
    a_spec = pl.BlockSpec((3, heads, rows, DH), lambda k, info: (0, 0, 0, 0))
    in_specs = [ANY] * (len(after) + sum(pairs)) + [pl.BlockSpec((chans, width), lambda k, info: (info[1 + k], 0))] * 3
    args = list(after) + [x for s in sources for x in s] + list(weights)
    scratch = [pltpu.VMEM((count, rows, chans), BF16), pltpu.SemaphoreType.DMA((count,))]
    raw = jax.ShapeDtypeStruct((3, heads, rows, DH), F32)
    if final:
        in_specs += [pl.BlockSpec((1, width), lambda k, info: (0, 0))] * 2
        args += [g[None] for g in gains]
        out_shape = [
            jax.ShapeDtypeStruct((heads, rows, DH), BF16),
            jax.ShapeDtypeStruct((2, heads, rows, DH), BF16),
        ]
        out_specs = [
            pl.BlockSpec((heads, rows, DH), lambda k, info: (0, 0, 0)),
            pl.BlockSpec((2, heads, rows, DH), lambda k, info: (0, 0, 0, 0)),
        ]
        scratch = [pltpu.VMEM((rows, 3 * width), F32)] + scratch
    else:
        out_shape, out_specs = raw, a_spec
    return pl.pallas_call(
        functools.partial(project_body, pairs, len(after), final),
        grid_spec=pltpu.PrefetchScalarGridSpec(
            num_scalar_prefetch=1,
            grid=(count,),
            in_specs=in_specs,
            out_specs=out_specs,
            scratch_shapes=scratch,
        ),
        out_shape=out_shape,
        compiler_params=pltpu.CompilerParams(vmem_limit_bytes=48 * 2**20),
        cost_estimate=pl.CostEstimate(flops=flops, bytes_accessed=1, transcendentals=0),
        name="project" + ("_end" if final else "_raw"),
    )(info, *args)


def finish_body(info, inner, outer, wq, wk, wv, qg, kg, raw, q_out, kv_out, rows, sem):
    @pl.when(pl.program_id(0) == 0)
    def _():
        for side, source in enumerate((inner, outer)):

            @pl.when(info[0] == side)
            def _(source=source):
                pltpu.make_async_copy(source, rows, sem).start()

        pltpu.make_async_copy(inner, rows, sem).wait()

    weight = jnp.concatenate([wq[...], wk[...], wv[...]], axis=1)
    part = jnp.dot(rows[...], weight, preferred_element_type=F32)
    total = [raw[group, 0] + part[:, group * DH : (group + 1) * DH] for group in range(3)]
    store_head(total, (qg[...], kg[...]), q_out, kv_out, 0)


def finish(raw, inner, outer, info, weights, gains, flops):
    rows, chans = inner.shape
    heads = raw.shape[1]
    w_spec = pl.BlockSpec((chans, DH), lambda h, info: (info[1], h))
    g_spec = pl.BlockSpec((1, DH), lambda h, info: (0, h))
    return pl.pallas_call(
        finish_body,
        grid_spec=pltpu.PrefetchScalarGridSpec(
            num_scalar_prefetch=1,
            grid=(heads,),
            in_specs=[ANY] * 2
            + [w_spec] * 3
            + [g_spec] * 2
            + [pl.BlockSpec((3, 1, rows, DH), lambda h, info: (0, h, 0, 0))],
            out_specs=[
                pl.BlockSpec((1, rows, DH), lambda h, info: (h, 0, 0)),
                pl.BlockSpec((2, 1, rows, DH), lambda h, info: (0, h, 0, 0)),
            ],
            scratch_shapes=[pltpu.VMEM((rows, chans), BF16), pltpu.SemaphoreType.DMA],
        ),
        out_shape=[
            jax.ShapeDtypeStruct((heads, rows, DH), BF16),
            jax.ShapeDtypeStruct((2, heads, rows, DH), BF16),
        ],
        compiler_params=pltpu.CompilerParams(vmem_limit_bytes=48 * 2**20),
        cost_estimate=pl.CostEstimate(flops=flops, bytes_accessed=1, transcendentals=0),
        name="finish",
    )(info, inner, outer, *weights, *(g[None] for g in gains), raw)


def attend_body(row_block, choices, fresh, info, *refs):
    refs = list(refs)
    query = refs.pop(0)
    options = [[refs.pop(0) for _ in range(n)] for n in choices]
    if not fresh:
        refs.pop(0)
    out, held, sem = refs
    h = pl.program_id(0)

    def fetch(part, source, head):
        return pltpu.make_async_copy(source.at[:, head], held.at[part, :, head], sem.at[part, head])

    @pl.when(h == 0)
    def _():
        for head in range(held.shape[2]):
            for part in range(2):
                for j, source in enumerate(options[part]):

                    @pl.when(info[2 * part] == j)
                    def _(part=part, source=source, head=head):
                        fetch(part, source, head).start()

    for part in range(2):
        fetch(part, options[part][0], h).wait()
    factor = 1.4426950408889634 / DH**0.5
    key = jnp.concatenate([held[0, 0, h], held[1, 0, h]], axis=0)
    value = jnp.concatenate([held[0, 1, h], held[1, 1, h]], axis=0)
    value = jnp.concatenate([value, jnp.ones_like(value)], axis=1)
    spans = [pl.ds(row, row_block) for row in range(0, query.shape[1], row_block)]

    def score(span):
        return lax.dot_general(
            query[0, span, :], key, (((1,), (1,)), ((), ())), preferred_element_type=F32
        )

    ahead = score(spans[0])
    for r, span in enumerate(spans):
        scores = ahead
        if r + 1 < len(spans):
            ahead = score(spans[r + 1])
        tops = [scores[:, c : c + DH] for c in range(0, scores.shape[1], DH)]
        top = jnp.max(functools.reduce(jnp.maximum, tops), axis=-1, keepdims=True)
        expo = jnp.exp2((scores - top) * factor).astype(BF16)
        result = jnp.dot(expo, value, preferred_element_type=F32)
        out[0, span, :] = (result[:, :DH] / result[:, DH:]).astype(BF16)


def attend(query, anchors, anchor, options, choice, frame, partly=None):
    heads, rows, _ = query.shape
    args = [query, *anchors, *options]
    aliases = {}
    if partly is not None:
        aliases = {1 + len(args): 0}
        args.append(partly)
    return pl.pallas_call(
        functools.partial(attend_body, 256, (len(anchors), len(options)), partly is None),
        grid_spec=pltpu.PrefetchScalarGridSpec(
            num_scalar_prefetch=1,
            grid=(heads,),
            in_specs=[pl.BlockSpec((1, rows, DH), lambda h, info: (h, 0, 0))] + [ANY] * (len(args) - 1),
            out_specs=pl.BlockSpec((1, rows, DH), lambda h, info: (info[1], 0, h)),
            scratch_shapes=[
                pltpu.VMEM((2, 2, heads, rows, DH), BF16),
                pltpu.SemaphoreType.DMA((2, heads)),
            ],
        ),
        out_shape=jax.ShapeDtypeStruct((2, rows, heads * DH), BF16),
        input_output_aliases=aliases,
        compiler_params=pltpu.CompilerParams(vmem_limit_bytes=32 * 2**20),
        cost_estimate=pl.CostEstimate(
            flops=8 * heads * rows * rows * DH,
            bytes_accessed=2 * heads * rows * DH * 6,
            transcendentals=2 * heads * rows * rows,
        ),
        name="attend",
    )(jnp.stack([anchor, frame, choice]).astype(jnp.int32), *args)


def broadcast_first(x, axis):
    count = lax.axis_size(axis)
    mine = lax.axis_index(axis)
    held = x
    for to in range(2, count, 2):
        held = jnp.where(mine == to, lax.ppermute(x, axis, [(0, to)]), held)
    return held, lax.ppermute(held, axis, [(i, i + 1) for i in range(0, count, 2)])


INWARD = [(0, 1), (3, 2)]
MIDDLE = [(1, 2), (2, 1)]
OUTWARD = [(1, 0), (2, 3)]


def mix(before, centre, after, taps):
    before, centre, after = (v.astype(F32) for v in (before, centre, after))
    return (centre + taps[0] * before + taps[1] * centre + taps[2] * after).astype(BF16)


def split_rows(scales):
    parts, rest = [], scales
    for _ in range(3):
        part = lax.reduce_precision(rest, 8, 7)
        parts.append(part.astype(BF16))
        rest = rest - part
    rows = jnp.concatenate(parts, axis=0)
    return jnp.pad(rows, ((0, 16 - rows.shape[0]), (0, 0)))


def joined_rows(rows, count):
    high, middle, low = (rows[i * count : (i + 1) * count].astype(F32) for i in range(3))
    return high + middle + low


def per_device(frames, taps, w_query, w_key, w_value, q_gain, k_gain):
    count = lax.axis_size("tm")
    pos = lax.axis_index("tm")
    z = lax.axis_index("head").astype(jnp.int32)
    outer = (z == 0) | (z == 3)
    near, far = (z + 2) % 4, 3 - z
    side = outer.astype(jnp.int32)
    pair, second, third = z ^ 1, jnp.where(outer, near, far), jnp.where(outer, far, near)
    info = jnp.stack([side, z, pair, second, third])
    info_raw, info_end = jnp.stack([side, z, pair, second]), jnp.stack([side, third])
    hold = lax.optimization_barrier
    weights = (w_query, w_key, w_value)
    gains = (q_gain, k_gain)
    ups = [(i, i + 1) for i in range(count - 1)]
    downs = [(j, i) for i, j in ups]
    start = pos == 0

    def send(x, pairs):
        return lax.ppermute(x, "head", pairs)

    def mix_first(first, last, following, scales):
        return mix(
            jnp.where(start, jnp.zeros_like(first), first),
            jnp.where(start, first, last),
            jnp.where(start, last, following),
            scales,
        )

    def mix_second(first, last, following, preceding, scales):
        return mix(
            jnp.where(start, first, preceding),
            jnp.where(start, last, first),
            jnp.where(start, following, last),
            scales,
        )

    raw_first = send(frames[0], OUTWARD)
    following = lax.ppermute(frames[0], "tm", downs)
    mixed1 = mix_first(frames[0], frames[1], following, taps)
    last = jnp.concatenate([frames[1], split_rows(taps)], axis=0)
    later, last, mixed1 = hold((frames, last, mixed1))
    inward1, middle1 = send(mixed1, INWARD), send(mixed1, MIDDLE)
    raw_last = send(last, OUTWARD)
    later, raw_first = hold((later[1], raw_first))
    preceding = lax.ppermute(later, "tm", ups)
    mixed2 = mix_second(frames[0], frames[1], following, preceding, taps)
    raw_following = lax.ppermute(raw_first, "tm", downs)
    inward1, middle1 = hold((inward1, middle1))
    cross1, second1 = send(inward1, MIDDLE), send(middle1, OUTWARD)
    outer_taps = joined_rows(raw_last[later.shape[0] :], taps.shape[0])
    raw_last = raw_last[: later.shape[0]]
    raw_preceding = lax.ppermute(raw_last, "tm", ups)
    middle2, inward2 = send(mixed2, MIDDLE), send(mixed2, INWARD)
    level = (cross1, second1, raw_following, raw_preceding)
    cross1, second1, raw_following, raw_preceding = hold(level)
    third1 = send(cross1, OUTWARD)
    first1 = mix_first(raw_first, raw_last, raw_following, outer_taps)
    first2 = mix_second(raw_first, raw_last, raw_following, raw_preceding, outer_taps)
    middle2, first1, first2 = hold((middle2, first1, first2))
    cross2, second2 = send(inward2, MIDDLE), send(middle2, OUTWARD)

    sources1 = [(mixed1,), (inward1, first1), (middle1, second1), (cross1, third1)]
    q1, kv1 = project(sources1, info, weights, gains, after=(inward2, middle2), flops=10**10)
    beside = lax.ppermute(inward2[:16], "tm", [(i, i ^ 1) for i in range(count)])
    kv1, beside = hold((kv1, beside))
    third2 = send(cross2, OUTWARD)
    anchor = broadcast_first(kv1, "tm")
    shift1 = lax.ppermute(kv1, "tm", [(i, i + 1) for i in range(1, count - 1)])
    raw2 = project([(mixed2,), (inward2, first2), (middle2, second2)], info_raw, weights, after=(beside,), flops=10**10)
    q2, kv2 = finish(raw2, cross2, third2, info_end, weights, gains, 10**10)
    shift2 = lax.ppermute(kv2, "tm", [(0, 1)])
    anchor, shift1 = hold((anchor, shift1))
    late = jnp.where(start, 0, 1)
    odd = pos % 2
    result = attend(q1, anchor, odd, [kv1, kv2], late, late)
    choice = jnp.minimum(pos, 1) + (pos == 1)
    return attend(q2, anchor, odd, [kv1, shift1, shift2], choice, 1 - late, result)


def solution(mesh):
    placed = (
        P("tm", None, "head"),
        P(None, "head"),
        P(None, "head"),
        P(None, "head"),
        P(None, "head"),
        P("head"),
        P("head"),
    )
    return jax.shard_map(
        per_device, mesh=mesh, in_specs=placed, out_specs=P("tm", None, "head"), check_vma=False
    )
```

```python
import functools

import jax
import jax.numpy as jnp
from jax import lax
from jax.experimental import pallas as pl
from jax.experimental.pallas import tpu as pltpu
from jax.sharding import PartitionSpec as P

DH = 128
BF16 = jnp.bfloat16
F32 = jnp.float32
ANY = pl.BlockSpec(memory_space=pl.ANY)


def normalized(part, gain):
    square = part * part
    high = square.astype(BF16)
    low = (square - high.astype(F32)).astype(BF16)
    ones = jnp.ones((2 * DH, DH), BF16)
    total = jnp.dot(jnp.concatenate([high, low], axis=1), ones, preferred_element_type=F32)
    return (part * lax.rsqrt(total * (1.0 / DH) + 1e-06) * gain).astype(BF16)


def store_head(raw, gains, q_out, kv_out, h):
    q_out[h] = normalized(raw[0], gains[0])
    kv_out[0, h] = normalized(raw[1], gains[1])
    kv_out[1, h] = raw[2].astype(BF16)


def project_body(pairs, extra, final, info, *refs):
    refs = list(refs)[extra:]
    count = len(pairs)
    groups = [[refs.pop(0) for _ in range(n)] for n in pairs]
    weights = [refs.pop(0) for _ in range(3)]
    gains = [refs.pop(0) for _ in range(2)] if final else None
    outs = [refs.pop(0) for _ in range(2)] if final else None
    acc, xbuf, sem = refs
    heads = weights[0].shape[1] // DH
    step = pl.program_id(0)

    @pl.when(step == 0)
    def _():
        for i, group in enumerate(groups):
            for j, source in enumerate(group):

                @pl.when((info[0] == j) | (len(group) == 1))
                def _(i=i, source=source):
                    pltpu.make_async_copy(source, xbuf.at[i], sem.at[i]).start()

    for i in range(count):

        @pl.when(step == i)
        def _(i=i):
            pltpu.make_async_copy(groups[i][0], xbuf.at[i], sem.at[i]).wait()
            weight = jnp.concatenate([w[...] for w in weights], axis=1)
            part = jnp.dot(xbuf[i], weight, preferred_element_type=F32)
            if final:
                acc[...] = part if i == 0 else acc[...] + part
            else:
                for group in range(3):
                    for h in range(heads):
                        columns = part[:, (group * heads + h) * DH : (group * heads + h + 1) * DH]
                        acc[group, h] = columns if i == 0 else acc[group, h] + columns

    if final:

        @pl.when(step == count - 1)
        def _():
            for h in range(heads):
                total = [acc[:, (group * heads + h) * DH : (group * heads + h + 1) * DH] for group in range(3)]
                store_head(total, [g[:, h * DH : (h + 1) * DH] for g in gains], *outs, h)


def project(sources, info, weights, gains=None, after=(), flops=1):
    pairs = [len(s) for s in sources]
    count = len(pairs)
    rows, chans = sources[0][0].shape
    width = weights[0].shape[1]
    heads = width // DH
    final = gains is not None
    a_spec = pl.BlockSpec((3, heads, rows, DH), lambda k, info: (0, 0, 0, 0))
    in_specs = [ANY] * (len(after) + sum(pairs)) + [pl.BlockSpec((chans, width), lambda k, info: (info[1 + k], 0))] * 3
    args = list(after) + [x for s in sources for x in s] + list(weights)
    scratch = [pltpu.VMEM((count, rows, chans), BF16), pltpu.SemaphoreType.DMA((count,))]
    raw = jax.ShapeDtypeStruct((3, heads, rows, DH), F32)
    if final:
        in_specs += [pl.BlockSpec((1, width), lambda k, info: (0, 0))] * 2
        args += [g[None] for g in gains]
        out_shape = [
            jax.ShapeDtypeStruct((heads, rows, DH), BF16),
            jax.ShapeDtypeStruct((2, heads, rows, DH), BF16),
        ]
        out_specs = [
            pl.BlockSpec((heads, rows, DH), lambda k, info: (0, 0, 0)),
            pl.BlockSpec((2, heads, rows, DH), lambda k, info: (0, 0, 0, 0)),
        ]
        scratch = [pltpu.VMEM((rows, 3 * width), F32)] + scratch
    else:
        out_shape, out_specs = raw, a_spec
    return pl.pallas_call(
        functools.partial(project_body, pairs, len(after), final),
        grid_spec=pltpu.PrefetchScalarGridSpec(
            num_scalar_prefetch=1,
            grid=(count,),
            in_specs=in_specs,
            out_specs=out_specs,
            scratch_shapes=scratch,
        ),
        out_shape=out_shape,
        compiler_params=pltpu.CompilerParams(vmem_limit_bytes=48 * 2**20),
        cost_estimate=pl.CostEstimate(flops=flops, bytes_accessed=1, transcendentals=0),
        name="project" + ("_end" if final else "_raw"),
    )(info, *args)


def finish_body(info, inner, outer, wq, wk, wv, qg, kg, raw, q_out, kv_out, rows, sem):
    @pl.when(pl.program_id(0) == 0)
    def _():
        for side, source in enumerate((inner, outer)):

            @pl.when(info[0] == side)
            def _(source=source):
                pltpu.make_async_copy(source, rows, sem).start()

        pltpu.make_async_copy(inner, rows, sem).wait()

    weight = jnp.concatenate([wq[...], wk[...], wv[...]], axis=1)
    part = jnp.dot(rows[...], weight, preferred_element_type=F32)
    total = [raw[group, 0] + part[:, group * DH : (group + 1) * DH] for group in range(3)]
    store_head(total, (qg[...], kg[...]), q_out, kv_out, 0)


def finish(raw, inner, outer, info, weights, gains, flops):
    rows, chans = inner.shape
    heads = raw.shape[1]
    w_spec = pl.BlockSpec((chans, DH), lambda h, info: (info[1], h))
    g_spec = pl.BlockSpec((1, DH), lambda h, info: (0, h))
    return pl.pallas_call(
        finish_body,
        grid_spec=pltpu.PrefetchScalarGridSpec(
            num_scalar_prefetch=1,
            grid=(heads,),
            in_specs=[ANY] * 2
            + [w_spec] * 3
            + [g_spec] * 2
            + [pl.BlockSpec((3, 1, rows, DH), lambda h, info: (0, h, 0, 0))],
            out_specs=[
                pl.BlockSpec((1, rows, DH), lambda h, info: (h, 0, 0)),
                pl.BlockSpec((2, 1, rows, DH), lambda h, info: (0, h, 0, 0)),
            ],
            scratch_shapes=[pltpu.VMEM((rows, chans), BF16), pltpu.SemaphoreType.DMA],
        ),
        out_shape=[
            jax.ShapeDtypeStruct((heads, rows, DH), BF16),
            jax.ShapeDtypeStruct((2, heads, rows, DH), BF16),
        ],
        compiler_params=pltpu.CompilerParams(vmem_limit_bytes=48 * 2**20),
        cost_estimate=pl.CostEstimate(flops=flops, bytes_accessed=1, transcendentals=0),
        name="finish",
    )(info, inner, outer, *weights, *(g[None] for g in gains), raw)


def attend_body(row_block, asked, choices, fresh, info, *refs):
    refs = list(refs)
    queries = [refs.pop(0) for _ in range(asked)]
    options = [[[refs.pop(0) for _ in range(n)] for n in counts] for counts in choices]
    if not fresh:
        refs.pop(0)
    out, held, sem = refs
    h = pl.program_id(0)

    def fetch(part, pieces, head):
        row = 0
        for piece in pieces:
            place = held.at[part, :, head, pl.ds(row, piece.shape[2])]
            pltpu.make_async_copy(piece.at[:, head], place, sem.at[part, head]).start()
            row += piece.shape[2]

    @pl.when(h == 0)
    def _():
        for head in range(held.shape[2]):
            for part in range(2):
                for j, source in enumerate(options[part]):

                    @pl.when(info[2 * part] == j)
                    def _(part=part, source=source, head=head):
                        fetch(part, source, head)

    for part in range(2):
        pltpu.make_async_copy(held.at[part, :, h], held.at[part, :, h], sem.at[part, h]).wait()
    factor = 1.4426950408889634 / DH**0.5
    key = jnp.concatenate([held[0, 0, h], held[1, 0, h]], axis=0)
    value = jnp.concatenate([held[0, 1, h], held[1, 1, h]], axis=0)
    value = jnp.concatenate([value, jnp.ones_like(value)], axis=1)
    blocks = [query[0, r : r + row_block, :] for query in queries for r in range(0, query.shape[1], row_block)]

    def score(block):
        return lax.dot_general(block, key, (((1,), (1,)), ((), ())), preferred_element_type=F32)

    ahead = score(blocks[0])
    for r in range(len(blocks)):
        scores = ahead
        if r + 1 < len(blocks):
            ahead = score(blocks[r + 1])
        tops = [scores[:, c : c + DH] for c in range(0, scores.shape[1], DH)]
        top = jnp.max(functools.reduce(jnp.maximum, tops), axis=-1, keepdims=True)
        expo = jnp.exp2((scores - top) * factor).astype(BF16)
        result = jnp.dot(expo, value, preferred_element_type=F32)
        out[0, r * row_block : (r + 1) * row_block, :] = (result[:, :DH] / result[:, DH:]).astype(BF16)


def attend(queries, anchors, anchor, options, choice, frame, partly=None):
    heads = queries[0].shape[0]
    rows = sum(query.shape[1] for query in queries)
    args = list(queries) + [piece for pieces in (*anchors, *options) for piece in pieces]
    counts = [[len(pieces) for pieces in group] for group in (anchors, options)]
    aliases = {}
    if partly is not None:
        aliases = {1 + len(args): 0}
        args.append(partly)
    return pl.pallas_call(
        functools.partial(attend_body, 256, len(queries), counts, partly is None),
        grid_spec=pltpu.PrefetchScalarGridSpec(
            num_scalar_prefetch=1,
            grid=(heads,),
            in_specs=[pl.BlockSpec((1, q.shape[1], DH), lambda h, info: (h, 0, 0)) for q in queries]
            + [ANY] * (len(args) - len(queries)),
            out_specs=pl.BlockSpec((1, rows, DH), lambda h, info: (info[1], 0, h)),
            scratch_shapes=[
                pltpu.VMEM((2, 2, heads, rows, DH), BF16),
                pltpu.SemaphoreType.DMA((2, heads)),
            ],
        ),
        out_shape=jax.ShapeDtypeStruct((2, rows, heads * DH), BF16),
        input_output_aliases=aliases,
        compiler_params=pltpu.CompilerParams(vmem_limit_bytes=32 * 2**20),
        cost_estimate=pl.CostEstimate(
            flops=10 * 8 * heads * rows * rows * DH,
            bytes_accessed=2 * heads * rows * DH * 6,
            transcendentals=2 * heads * rows * rows,
        ),
        name="attend",
    )(jnp.stack([anchor, frame, choice]).astype(jnp.int32), *args)


def broadcast_first(x, axis):
    count = lax.axis_size(axis)
    mine = lax.axis_index(axis)
    held = x
    for to in reversed(range(2, count, 2)):
        held = jnp.where(mine == to, lax.ppermute(x, axis, [(0, to)]), held)
    return held, lax.ppermute(held, axis, [(i, i + 1) for i in range(0, count, 2)])


INWARD = [(0, 1), (3, 2)]
MIDDLE = [(1, 2), (2, 1)]
OUTWARD = [(1, 0), (2, 3)]


def mix(before, centre, after, taps):
    before, centre, after = (v.astype(F32) for v in (before, centre, after))
    return (centre + taps[0] * before + taps[1] * centre + taps[2] * after).astype(BF16)


def split_rows(scales):
    parts, rest = [], scales
    for _ in range(3):
        part = lax.reduce_precision(rest, 8, 7)
        parts.append(part.astype(BF16))
        rest = rest - part
    rows = jnp.concatenate(parts, axis=0)
    return jnp.pad(rows, ((0, 16 - rows.shape[0]), (0, 0)))


def joined_rows(rows, count):
    high, middle, low = (rows[i * count : (i + 1) * count].astype(F32) for i in range(3))
    return high + middle + low


def per_device(frames, taps, w_query, w_key, w_value, q_gain, k_gain):
    count = lax.axis_size("tm")
    pos = lax.axis_index("tm")
    z = lax.axis_index("head").astype(jnp.int32)
    outer = (z == 0) | (z == 3)
    near, far = (z + 2) % 4, 3 - z
    side = outer.astype(jnp.int32)
    pair, second, third = z ^ 1, jnp.where(outer, near, far), jnp.where(outer, far, near)
    info = jnp.stack([side, z, pair, second, third])
    info_raw, info_end = jnp.stack([side, z, pair, second]), jnp.stack([side, third])
    hold = lax.optimization_barrier
    weights = (w_query, w_key, w_value)
    gains = (q_gain, k_gain)
    ups = [(i, i + 1) for i in range(count - 1)]
    downs = [(j, i) for i, j in ups]
    start = pos == 0

    def send(x, pairs):
        return lax.ppermute(x, "head", pairs)

    def mix_first(first, last, following, scales):
        return mix(
            jnp.where(start, jnp.zeros_like(first), first),
            jnp.where(start, first, last),
            jnp.where(start, last, following),
            scales,
        )

    def mix_second(first, last, following, preceding, scales):
        return mix(
            jnp.where(start, first, preceding),
            jnp.where(start, last, first),
            jnp.where(start, following, last),
            scales,
        )

    raw_first = send(frames[0], OUTWARD)
    following = lax.ppermute(frames[0], "tm", downs)
    mixed1 = mix_first(frames[0], frames[1], following, taps)
    last = jnp.concatenate([frames[1], split_rows(taps)], axis=0)
    later, last, mixed1 = hold((frames, last, mixed1))
    inward1, middle1 = send(mixed1, INWARD), send(mixed1, MIDDLE)
    raw_last = send(last, OUTWARD)
    later, raw_first = hold((later[1], raw_first))
    preceding = lax.ppermute(later, "tm", ups)
    mixed2 = mix_second(frames[0], frames[1], following, preceding, taps)
    raw_following = lax.ppermute(raw_first, "tm", downs)
    inward1, middle1 = hold((inward1, middle1))
    cross1, second1 = send(inward1, MIDDLE), send(middle1, OUTWARD)
    outer_taps = joined_rows(raw_last[later.shape[0] :], taps.shape[0])
    raw_last = raw_last[: later.shape[0]]
    raw_preceding = lax.ppermute(raw_last, "tm", ups)
    middle2, inward2 = send(mixed2, MIDDLE), send(mixed2, INWARD)
    level = (cross1, second1, raw_following, raw_preceding)
    cross1, second1, raw_following, raw_preceding = hold(level)
    third1 = send(cross1, OUTWARD)
    first1 = mix_first(raw_first, raw_last, raw_following, outer_taps)
    first2 = mix_second(raw_first, raw_last, raw_following, raw_preceding, outer_taps)
    middle2, first1, first2 = hold((middle2, first1, first2))
    cross2, second2 = send(inward2, MIDDLE), send(middle2, OUTWARD)

    sources1 = [(mixed1,), (inward1, first1), (middle1, second1), (cross1, third1)]
    q1, kv1 = project(sources1, info, weights, gains, after=(inward2, middle2), flops=10**10)
    beside = lax.ppermute(inward2[:16], "tm", [(i, i ^ 1) for i in range(count)])
    kv1, beside = hold((kv1, beside))
    third2 = send(cross2, OUTWARD)
    anchor = broadcast_first(kv1, "tm")
    half = kv1.shape[2] // 2
    halves = hold((kv1[:, :, :half], kv1[:, :, half:], anchor[0]))
    shift1 = [lax.ppermute(x, "tm", [(i, i + 1) for i in range(1, count - 1)]) for x in halves[:2]]
    raw2 = project([(mixed2,), (inward2, first2), (middle2, second2)], info_raw, weights, after=(beside,), flops=10**10)
    q2, kv2 = finish(raw2, cross2, third2, info_end, weights, gains, 10**11)
    shift2 = lax.ppermute(kv2, "tm", [(0, 1)])
    anchor, shift1[0] = hold((anchor, shift1[0]))
    anchors = [[x] for x in anchor]
    late = jnp.where(start, 0, 1)
    odd = pos % 2
    result = attend([q1], anchors, odd, [[kv1], [kv2]], late, late)
    choice = jnp.minimum(pos, 1) + (pos == 1)
    return attend([q2], anchors, odd, [[kv1], shift1, [shift2]], choice, 1 - late, result)


def solution(mesh):
    placed = (
        P("tm", None, "head"),
        P(None, "head"),
        P(None, "head"),
        P(None, "head"),
        P(None, "head"),
        P("head"),
        P("head"),
    )
    return jax.shard_map(
        per_device, mesh=mesh, in_specs=placed, out_specs=P("tm", None, "head"), check_vma=False
    )
```

```python
import functools

import jax
import jax.numpy as jnp
from jax import lax
from jax.experimental import pallas as pl
from jax.experimental.pallas import tpu as pltpu
from jax.sharding import PartitionSpec as P

DH = 128
BF16 = jnp.bfloat16
F32 = jnp.float32
ANY = pl.BlockSpec(memory_space=pl.ANY)


def normalized(part, gain):
    square = part * part
    high = square.astype(BF16)
    low = (square - high.astype(F32)).astype(BF16)
    ones = jnp.ones((2 * DH, DH), BF16)
    total = jnp.dot(jnp.concatenate([high, low], axis=1), ones, preferred_element_type=F32)
    return (part * lax.rsqrt(total * (1.0 / DH) + 1e-06) * gain).astype(BF16)


def store_head(raw, gains, q_out, kv_out, h):
    q_out[h] = normalized(raw[0], gains[0])
    kv_out[0, h] = normalized(raw[1], gains[1])
    kv_out[1, h] = raw[2].astype(BF16)


def project_body(pairs, extra, final, info, *refs):
    refs = list(refs)[extra:]
    count = len(pairs)
    groups = [[refs.pop(0) for _ in range(n)] for n in pairs]
    weights = [refs.pop(0) for _ in range(3)]
    gains = [refs.pop(0) for _ in range(2)] if final else None
    outs = [refs.pop(0) for _ in range(2)] if final else None
    acc, xbuf, sem = refs
    heads = weights[0].shape[1] // DH
    step = pl.program_id(0)

    @pl.when(step == 0)
    def _():
        for i, group in enumerate(groups):
            for j, source in enumerate(group):

                @pl.when((info[0] == j) | (len(group) == 1))
                def _(i=i, source=source):
                    pltpu.make_async_copy(source, xbuf.at[i], sem.at[i]).start()

    for i in range(count):

        @pl.when(step == i)
        def _(i=i):
            pltpu.make_async_copy(groups[i][0], xbuf.at[i], sem.at[i]).wait()
            weight = jnp.concatenate([w[...] for w in weights], axis=1)
            part = jnp.dot(xbuf[i], weight, preferred_element_type=F32)
            if final:
                acc[...] = part if i == 0 else acc[...] + part
            else:
                for group in range(3):
                    for h in range(heads):
                        columns = part[:, (group * heads + h) * DH : (group * heads + h + 1) * DH]
                        acc[group, h] = columns if i == 0 else acc[group, h] + columns

    if final:

        @pl.when(step == count - 1)
        def _():
            for h in range(heads):
                total = [acc[:, (group * heads + h) * DH : (group * heads + h + 1) * DH] for group in range(3)]
                store_head(total, [g[:, h * DH : (h + 1) * DH] for g in gains], *outs, h)


def project(sources, info, weights, gains=None, after=(), flops=1):
    pairs = [len(s) for s in sources]
    count = len(pairs)
    rows, chans = sources[0][0].shape
    width = weights[0].shape[1]
    heads = width // DH
    final = gains is not None
    a_spec = pl.BlockSpec((3, heads, rows, DH), lambda k, info: (0, 0, 0, 0))
    in_specs = [ANY] * (len(after) + sum(pairs)) + [pl.BlockSpec((chans, width), lambda k, info: (info[1 + k], 0))] * 3
    args = list(after) + [x for s in sources for x in s] + list(weights)
    scratch = [pltpu.VMEM((count, rows, chans), BF16), pltpu.SemaphoreType.DMA((count,))]
    raw = jax.ShapeDtypeStruct((3, heads, rows, DH), F32)
    if final:
        in_specs += [pl.BlockSpec((1, width), lambda k, info: (0, 0))] * 2
        args += [g[None] for g in gains]
        out_shape = [
            jax.ShapeDtypeStruct((heads, rows, DH), BF16),
            jax.ShapeDtypeStruct((2, heads, rows, DH), BF16),
        ]
        out_specs = [
            pl.BlockSpec((heads, rows, DH), lambda k, info: (0, 0, 0)),
            pl.BlockSpec((2, heads, rows, DH), lambda k, info: (0, 0, 0, 0)),
        ]
        scratch = [pltpu.VMEM((rows, 3 * width), F32)] + scratch
    else:
        out_shape, out_specs = raw, a_spec
    return pl.pallas_call(
        functools.partial(project_body, pairs, len(after), final),
        grid_spec=pltpu.PrefetchScalarGridSpec(
            num_scalar_prefetch=1,
            grid=(count,),
            in_specs=in_specs,
            out_specs=out_specs,
            scratch_shapes=scratch,
        ),
        out_shape=out_shape,
        compiler_params=pltpu.CompilerParams(vmem_limit_bytes=48 * 2**20),
        cost_estimate=pl.CostEstimate(flops=flops, bytes_accessed=1, transcendentals=0),
        name="project" + ("_end" if final else "_raw"),
    )(info, *args)


def finish_body(info, inner, outer, wq, wk, wv, qg, kg, raw, q_out, kv_out, rows, sem):
    @pl.when(pl.program_id(0) == 0)
    def _():
        for side, source in enumerate((inner, outer)):

            @pl.when(info[0] == side)
            def _(source=source):
                pltpu.make_async_copy(source, rows, sem).start()

        pltpu.make_async_copy(inner, rows, sem).wait()

    weight = jnp.concatenate([wq[...], wk[...], wv[...]], axis=1)
    part = jnp.dot(rows[...], weight, preferred_element_type=F32)
    total = [raw[group, 0] + part[:, group * DH : (group + 1) * DH] for group in range(3)]
    store_head(total, (qg[...], kg[...]), q_out, kv_out, 0)


def finish(raw, inner, outer, info, weights, gains, flops):
    rows, chans = inner.shape
    heads = raw.shape[1]
    w_spec = pl.BlockSpec((chans, DH), lambda h, info: (info[1], h))
    g_spec = pl.BlockSpec((1, DH), lambda h, info: (0, h))
    return pl.pallas_call(
        finish_body,
        grid_spec=pltpu.PrefetchScalarGridSpec(
            num_scalar_prefetch=1,
            grid=(heads,),
            in_specs=[ANY] * 2
            + [w_spec] * 3
            + [g_spec] * 2
            + [pl.BlockSpec((3, 1, rows, DH), lambda h, info: (0, h, 0, 0))],
            out_specs=[
                pl.BlockSpec((1, rows, DH), lambda h, info: (h, 0, 0)),
                pl.BlockSpec((2, 1, rows, DH), lambda h, info: (0, h, 0, 0)),
            ],
            scratch_shapes=[pltpu.VMEM((rows, chans), BF16), pltpu.SemaphoreType.DMA],
        ),
        out_shape=[
            jax.ShapeDtypeStruct((heads, rows, DH), BF16),
            jax.ShapeDtypeStruct((2, heads, rows, DH), BF16),
        ],
        compiler_params=pltpu.CompilerParams(vmem_limit_bytes=48 * 2**20),
        cost_estimate=pl.CostEstimate(flops=flops, bytes_accessed=1, transcendentals=0),
        name="finish",
    )(info, inner, outer, *weights, *(g[None] for g in gains), raw)


def attend_body(row_block, asked, choices, fresh, info, *refs):
    refs = list(refs)
    queries = [refs.pop(0) for _ in range(asked)]
    options = [[[refs.pop(0) for _ in range(n)] for n in counts] for counts in choices]
    if not fresh:
        refs.pop(0)
    out, held, sem = refs
    h = pl.program_id(0)

    def fetch(part, pieces, head):
        row = 0
        for piece in pieces:
            place = held.at[part, :, head, pl.ds(row, piece.shape[2])]
            pltpu.make_async_copy(piece.at[:, head], place, sem.at[part, head]).start()
            row += piece.shape[2]

    @pl.when(h == 0)
    def _():
        for head in range(held.shape[2]):
            for part in range(2):
                for j, source in enumerate(options[part]):

                    @pl.when(info[2 * part] == j)
                    def _(part=part, source=source, head=head):
                        fetch(part, source, head)

    for part in range(2):
        pltpu.make_async_copy(held.at[part, :, h], held.at[part, :, h], sem.at[part, h]).wait()
    factor = 1.4426950408889634 / DH**0.5
    key = jnp.concatenate([held[0, 0, h], held[1, 0, h]], axis=0)
    value = jnp.concatenate([held[0, 1, h], held[1, 1, h]], axis=0)
    value = jnp.concatenate([value, jnp.ones_like(value)], axis=1)
    blocks = [query[0, r : r + row_block, :] for query in queries for r in range(0, query.shape[1], row_block)]

    def score(block):
        return lax.dot_general(block, key, (((1,), (1,)), ((), ())), preferred_element_type=F32)

    ahead = score(blocks[0])
    for r in range(len(blocks)):
        scores = ahead
        if r + 1 < len(blocks):
            ahead = score(blocks[r + 1])
        tops = [scores[:, c : c + DH] for c in range(0, scores.shape[1], DH)]
        top = jnp.max(functools.reduce(jnp.maximum, tops), axis=-1, keepdims=True)
        expo = jnp.exp2((scores - top) * factor).astype(BF16)
        result = jnp.dot(expo, value, preferred_element_type=F32)
        out[0, r * row_block : (r + 1) * row_block, :] = (result[:, :DH] / result[:, DH:]).astype(BF16)


def attend(queries, anchors, anchor, options, choice, frame, partly=None):
    heads = queries[0].shape[0]
    rows = sum(query.shape[1] for query in queries)
    args = list(queries) + [piece for pieces in (*anchors, *options) for piece in pieces]
    counts = [[len(pieces) for pieces in group] for group in (anchors, options)]
    aliases = {}
    if partly is not None:
        aliases = {1 + len(args): 0}
        args.append(partly)
    return pl.pallas_call(
        functools.partial(attend_body, 256, len(queries), counts, partly is None),
        grid_spec=pltpu.PrefetchScalarGridSpec(
            num_scalar_prefetch=1,
            grid=(heads,),
            in_specs=[pl.BlockSpec((1, q.shape[1], DH), lambda h, info: (h, 0, 0)) for q in queries]
            + [ANY] * (len(args) - len(queries)),
            out_specs=pl.BlockSpec((1, rows, DH), lambda h, info: (info[1], 0, h)),
            scratch_shapes=[
                pltpu.VMEM((2, 2, heads, rows, DH), BF16),
                pltpu.SemaphoreType.DMA((2, heads)),
            ],
        ),
        out_shape=jax.ShapeDtypeStruct((2, rows, heads * DH), BF16),
        input_output_aliases=aliases,
        compiler_params=pltpu.CompilerParams(vmem_limit_bytes=32 * 2**20),
        cost_estimate=pl.CostEstimate(
            flops=10 * 8 * heads * rows * rows * DH,
            bytes_accessed=2 * heads * rows * DH * 6,
            transcendentals=2 * heads * rows * rows,
        ),
        name="attend",
    )(jnp.stack([anchor, frame, choice]).astype(jnp.int32), *args)


def broadcast_first(x, axis):
    count = lax.axis_size(axis)
    mine = lax.axis_index(axis)
    held = x
    for to in reversed(range(2, count, 2)):
        held = jnp.where(mine == to, lax.ppermute(x, axis, [(0, to)]), held)
    return held, lax.ppermute(held, axis, [(i, i + 1) for i in range(0, count, 2)])


INWARD = [(0, 1), (3, 2)]
MIDDLE = [(1, 2), (2, 1)]
OUTWARD = [(1, 0), (2, 3)]


def mix(before, centre, after, taps):
    before, centre, after = (v.astype(F32) for v in (before, centre, after))
    return (centre + taps[0] * before + taps[1] * centre + taps[2] * after).astype(BF16)


def split_rows(scales):
    parts, rest = [], scales
    for _ in range(3):
        part = lax.reduce_precision(rest, 8, 7)
        parts.append(part.astype(BF16))
        rest = rest - part
    rows = jnp.concatenate(parts, axis=0)
    return jnp.pad(rows, ((0, 16 - rows.shape[0]), (0, 0)))


def joined_rows(rows, count):
    high, middle, low = (rows[i * count : (i + 1) * count].astype(F32) for i in range(3))
    return high + middle + low


def per_device(frames, taps, w_query, w_key, w_value, q_gain, k_gain):
    count = lax.axis_size("tm")
    pos = lax.axis_index("tm")
    z = lax.axis_index("head").astype(jnp.int32)
    outer = (z == 0) | (z == 3)
    near, far = (z + 2) % 4, 3 - z
    side = outer.astype(jnp.int32)
    pair, second, third = z ^ 1, jnp.where(outer, near, far), jnp.where(outer, far, near)
    info = jnp.stack([side, z, pair, second, third])
    info_raw, info_end = jnp.stack([side, z, pair, second]), jnp.stack([side, third])
    hold = lax.optimization_barrier
    weights = (w_query, w_key, w_value)
    gains = (q_gain, k_gain)
    ups = [(i, i + 1) for i in range(count - 1)]
    downs = [(j, i) for i, j in ups]
    start = pos == 0

    def send(x, pairs):
        return lax.ppermute(x, "head", pairs)

    def mix_first(first, last, following, scales):
        return mix(
            jnp.where(start, jnp.zeros_like(first), first),
            jnp.where(start, first, last),
            jnp.where(start, last, following),
            scales,
        )

    def mix_second(first, last, following, preceding, scales):
        return mix(
            jnp.where(start, first, preceding),
            jnp.where(start, last, first),
            jnp.where(start, following, last),
            scales,
        )

    raw_first = send(frames[0], OUTWARD)
    following = lax.ppermute(frames[0], "tm", downs)
    mixed1 = mix_first(frames[0], frames[1], following, taps)
    last = jnp.concatenate([frames[1], split_rows(taps)], axis=0)
    later, last, mixed1 = hold((frames, last, mixed1))
    inward1, middle1 = send(mixed1, INWARD), send(mixed1, MIDDLE)
    raw_last = send(last, OUTWARD)
    later, raw_first = hold((later[1], raw_first))
    preceding = lax.ppermute(later, "tm", ups)
    mixed2 = mix_second(frames[0], frames[1], following, preceding, taps)
    raw_following = lax.ppermute(raw_first, "tm", downs)
    inward1, middle1 = hold((inward1, middle1))
    cross1, second1 = send(inward1, MIDDLE), send(middle1, OUTWARD)
    outer_taps = joined_rows(raw_last[later.shape[0] :], taps.shape[0])
    raw_last = raw_last[: later.shape[0]]
    raw_preceding = lax.ppermute(raw_last, "tm", ups)
    middle2, inward2 = send(mixed2, MIDDLE), send(mixed2, INWARD)
    level = (cross1, second1, raw_following, raw_preceding)
    cross1, second1, raw_following, raw_preceding = hold(level)
    third1 = send(cross1, OUTWARD)
    first1 = mix_first(raw_first, raw_last, raw_following, outer_taps)
    first2 = mix_second(raw_first, raw_last, raw_following, raw_preceding, outer_taps)
    middle2, first1, first2 = hold((middle2, first1, first2))
    cross2, second2 = send(inward2, MIDDLE), send(middle2, OUTWARD)

    sources1 = [(mixed1,), (inward1, first1), (middle1, second1), (cross1, third1)]
    q1, kv1 = project(sources1, info, weights, gains, after=(inward2, middle2), flops=10**10)
    beside = lax.ppermute(inward2[:16], "tm", [(i, i ^ 1) for i in range(count)])
    kv1, beside = hold((kv1, beside))
    third2 = send(cross2, OUTWARD)
    anchor = broadcast_first(kv1, "tm")
    cut = 3 * kv1.shape[2] // 4
    pieces = hold((kv1[:, :, :cut], kv1[:, :, cut:], anchor[0]))
    shift1 = [lax.ppermute(x, "tm", [(i, i + 1) for i in range(1, count - 1)]) for x in pieces[:2]]
    raw2 = project([(mixed2,), (inward2, first2), (middle2, second2)], info_raw, weights, after=(beside,), flops=10**10)
    q2, kv2 = finish(raw2, cross2, third2, info_end, weights, gains, 10**11)
    shift2 = lax.ppermute(kv2, "tm", [(0, 1)])
    anchor, shift1[0] = hold((anchor, shift1[0]))
    anchors = [[x] for x in anchor]
    late = jnp.where(start, 0, 1)
    odd = pos % 2
    result = attend([q1], anchors, odd, [[kv1], [kv2]], late, late)
    choice = jnp.minimum(pos, 1) + (pos == 1)
    return attend([q2], anchors, odd, [[kv1], shift1, [shift2]], choice, 1 - late, result)


def solution(mesh):
    placed = (
        P("tm", None, "head"),
        P(None, "head"),
        P(None, "head"),
        P(None, "head"),
        P(None, "head"),
        P("head"),
        P("head"),
    )
    return jax.shard_map(
        per_device, mesh=mesh, in_specs=placed, out_specs=P("tm", None, "head"), check_vma=False
    )
```

```python
import functools

import jax
import jax.numpy as jnp
from jax import lax
from jax.experimental import pallas as pl
from jax.experimental.pallas import tpu as pltpu
from jax.sharding import PartitionSpec as P

DH = 128
BF16 = jnp.bfloat16
F32 = jnp.float32
ANY = pl.BlockSpec(memory_space=pl.ANY)


def normalized(part, gain):
    square = part * part
    high = square.astype(BF16)
    low = (square - high.astype(F32)).astype(BF16)
    ones = jnp.ones((2 * DH, DH), BF16)
    total = jnp.dot(jnp.concatenate([high, low], axis=1), ones, preferred_element_type=F32)
    return (part * lax.rsqrt(total * (1.0 / DH) + 1e-06) * gain).astype(BF16)


def store_head(raw, gains, q_out, kv_out, h):
    q_out[h] = normalized(raw[0], gains[0])
    kv_out[0, h] = normalized(raw[1], gains[1])
    kv_out[1, h] = raw[2].astype(BF16)


def project_body(pairs, extra, final, info, *refs):
    refs = list(refs)[extra:]
    count = len(pairs)
    groups = [[refs.pop(0) for _ in range(n)] for n in pairs]
    weights = [refs.pop(0) for _ in range(3)]
    gains = [refs.pop(0) for _ in range(2)] if final else None
    outs = [refs.pop(0) for _ in range(2)] if final else None
    acc, xbuf, sem = refs
    heads = weights[0].shape[1] // DH
    step = pl.program_id(0)

    @pl.when(step == 0)
    def _():
        for i, group in enumerate(groups):
            for j, source in enumerate(group):

                @pl.when((info[0] == j) | (len(group) == 1))
                def _(i=i, source=source):
                    pltpu.make_async_copy(source, xbuf.at[i], sem.at[i]).start()

    for i in range(count):

        @pl.when(step == i)
        def _(i=i):
            pltpu.make_async_copy(groups[i][0], xbuf.at[i], sem.at[i]).wait()
            weight = jnp.concatenate([w[...] for w in weights], axis=1)
            part = jnp.dot(xbuf[i], weight, preferred_element_type=F32)
            if final:
                acc[...] = part if i == 0 else acc[...] + part
            else:
                for group in range(3):
                    for h in range(heads):
                        columns = part[:, (group * heads + h) * DH : (group * heads + h + 1) * DH]
                        acc[group, h] = columns if i == 0 else acc[group, h] + columns

    if final:

        @pl.when(step == count - 1)
        def _():
            for h in range(heads):
                total = [acc[:, (group * heads + h) * DH : (group * heads + h + 1) * DH] for group in range(3)]
                store_head(total, [g[:, h * DH : (h + 1) * DH] for g in gains], *outs, h)


def project(sources, info, weights, gains=None, after=(), flops=1):
    pairs = [len(s) for s in sources]
    count = len(pairs)
    rows, chans = sources[0][0].shape
    width = weights[0].shape[1]
    heads = width // DH
    final = gains is not None
    a_spec = pl.BlockSpec((3, heads, rows, DH), lambda k, info: (0, 0, 0, 0))
    in_specs = [ANY] * (len(after) + sum(pairs)) + [pl.BlockSpec((chans, width), lambda k, info: (info[1 + k], 0))] * 3
    args = list(after) + [x for s in sources for x in s] + list(weights)
    scratch = [pltpu.VMEM((count, rows, chans), BF16), pltpu.SemaphoreType.DMA((count,))]
    raw = jax.ShapeDtypeStruct((3, heads, rows, DH), F32)
    if final:
        in_specs += [pl.BlockSpec((1, width), lambda k, info: (0, 0))] * 2
        args += [g[None] for g in gains]
        out_shape = [
            jax.ShapeDtypeStruct((heads, rows, DH), BF16),
            jax.ShapeDtypeStruct((2, heads, rows, DH), BF16),
        ]
        out_specs = [
            pl.BlockSpec((heads, rows, DH), lambda k, info: (0, 0, 0)),
            pl.BlockSpec((2, heads, rows, DH), lambda k, info: (0, 0, 0, 0)),
        ]
        scratch = [pltpu.VMEM((rows, 3 * width), F32)] + scratch
    else:
        out_shape, out_specs = raw, a_spec
    return pl.pallas_call(
        functools.partial(project_body, pairs, len(after), final),
        grid_spec=pltpu.PrefetchScalarGridSpec(
            num_scalar_prefetch=1,
            grid=(count,),
            in_specs=in_specs,
            out_specs=out_specs,
            scratch_shapes=scratch,
        ),
        out_shape=out_shape,
        compiler_params=pltpu.CompilerParams(vmem_limit_bytes=48 * 2**20),
        cost_estimate=pl.CostEstimate(flops=flops, bytes_accessed=1, transcendentals=0),
        name="project" + ("_end" if final else "_raw"),
    )(info, *args)


def finish_body(info, inner, outer, wq, wk, wv, qg, kg, raw, q_out, kv_out, rows, sem):
    @pl.when(pl.program_id(0) == 0)
    def _():
        for side, source in enumerate((inner, outer)):

            @pl.when(info[0] == side)
            def _(source=source):
                pltpu.make_async_copy(source, rows, sem).start()

        pltpu.make_async_copy(inner, rows, sem).wait()

    weight = jnp.concatenate([wq[...], wk[...], wv[...]], axis=1)
    part = jnp.dot(rows[...], weight, preferred_element_type=F32)
    total = [raw[group, 0] + part[:, group * DH : (group + 1) * DH] for group in range(3)]
    store_head(total, (qg[...], kg[...]), q_out, kv_out, 0)


def finish(raw, inner, outer, info, weights, gains, flops):
    rows, chans = inner.shape
    heads = raw.shape[1]
    w_spec = pl.BlockSpec((chans, DH), lambda h, info: (info[1], h))
    g_spec = pl.BlockSpec((1, DH), lambda h, info: (0, h))
    return pl.pallas_call(
        finish_body,
        grid_spec=pltpu.PrefetchScalarGridSpec(
            num_scalar_prefetch=1,
            grid=(heads,),
            in_specs=[ANY] * 2
            + [w_spec] * 3
            + [g_spec] * 2
            + [pl.BlockSpec((3, 1, rows, DH), lambda h, info: (0, h, 0, 0))],
            out_specs=[
                pl.BlockSpec((1, rows, DH), lambda h, info: (h, 0, 0)),
                pl.BlockSpec((2, 1, rows, DH), lambda h, info: (0, h, 0, 0)),
            ],
            scratch_shapes=[pltpu.VMEM((rows, chans), BF16), pltpu.SemaphoreType.DMA],
        ),
        out_shape=[
            jax.ShapeDtypeStruct((heads, rows, DH), BF16),
            jax.ShapeDtypeStruct((2, heads, rows, DH), BF16),
        ],
        compiler_params=pltpu.CompilerParams(vmem_limit_bytes=48 * 2**20),
        cost_estimate=pl.CostEstimate(flops=flops, bytes_accessed=1, transcendentals=0),
        name="finish",
    )(info, inner, outer, *weights, *(g[None] for g in gains), raw)


def attend_body(row_block, asked, choices, fresh, info, *refs):
    refs = list(refs)
    queries = [refs.pop(0) for _ in range(asked)]
    options = [[[refs.pop(0) for _ in range(n)] for n in counts] for counts in choices]
    if not fresh:
        refs.pop(0)
    out, held, sem = refs
    h = pl.program_id(0)

    def fetch(part, pieces, head):
        row = 0
        for piece in pieces:
            place = held.at[part, :, head, pl.ds(row, piece.shape[2])]
            pltpu.make_async_copy(piece.at[:, head], place, sem.at[part, head]).start()
            row += piece.shape[2]

    @pl.when(h == 0)
    def _():
        for head in range(held.shape[2]):
            for part in range(2):
                for j, source in enumerate(options[part]):

                    @pl.when(info[2 * part] == j)
                    def _(part=part, source=source, head=head):
                        fetch(part, source, head)

    for part in range(2):
        pltpu.make_async_copy(held.at[part, :, h], held.at[part, :, h], sem.at[part, h]).wait()
    factor = 1.4426950408889634 / DH**0.5
    key = jnp.concatenate([held[0, 0, h], held[1, 0, h]], axis=0)
    value = jnp.concatenate([held[0, 1, h], held[1, 1, h]], axis=0)
    value = jnp.concatenate([value, jnp.ones_like(value)], axis=1)
    blocks = [query[0, r : r + row_block, :] for query in queries for r in range(0, query.shape[1], row_block)]

    def score(block):
        return lax.dot_general(block, key, (((1,), (1,)), ((), ())), preferred_element_type=F32)

    ahead = score(blocks[0])
    for r in range(len(blocks)):
        scores = ahead
        if r + 1 < len(blocks):
            ahead = score(blocks[r + 1])
        tops = [scores[:, c : c + DH] for c in range(0, scores.shape[1], DH)]
        top = jnp.max(functools.reduce(jnp.maximum, tops), axis=-1, keepdims=True)
        expo = jnp.exp2((scores - top) * factor).astype(BF16)
        result = jnp.dot(expo, value, preferred_element_type=F32)
        out[0, r * row_block : (r + 1) * row_block, :] = (result[:, :DH] / result[:, DH:]).astype(BF16)


def attend(queries, anchors, anchor, options, choice, frame, partly=None):
    heads = queries[0].shape[0]
    rows = sum(query.shape[1] for query in queries)
    args = list(queries) + [piece for pieces in (*anchors, *options) for piece in pieces]
    counts = [[len(pieces) for pieces in group] for group in (anchors, options)]
    aliases = {}
    if partly is not None:
        aliases = {1 + len(args): 0}
        args.append(partly)
    return pl.pallas_call(
        functools.partial(attend_body, 256, len(queries), counts, partly is None),
        grid_spec=pltpu.PrefetchScalarGridSpec(
            num_scalar_prefetch=1,
            grid=(heads,),
            in_specs=[pl.BlockSpec((1, q.shape[1], DH), lambda h, info: (h, 0, 0)) for q in queries]
            + [ANY] * (len(args) - len(queries)),
            out_specs=pl.BlockSpec((1, rows, DH), lambda h, info: (info[1], 0, h)),
            scratch_shapes=[
                pltpu.VMEM((2, 2, heads, rows, DH), BF16),
                pltpu.SemaphoreType.DMA((2, heads)),
            ],
        ),
        out_shape=jax.ShapeDtypeStruct((2, rows, heads * DH), BF16),
        input_output_aliases=aliases,
        compiler_params=pltpu.CompilerParams(vmem_limit_bytes=32 * 2**20),
        cost_estimate=pl.CostEstimate(
            flops=10 * 8 * heads * rows * rows * DH,
            bytes_accessed=2 * heads * rows * DH * 6,
            transcendentals=2 * heads * rows * rows,
        ),
        name="attend",
    )(jnp.stack([anchor, frame, choice]).astype(jnp.int32), *args)


def broadcast_first(x, axis):
    count = lax.axis_size(axis)
    mine = lax.axis_index(axis)
    held = x
    for to in reversed(range(2, count, 2)):
        held = jnp.where(mine == to, lax.ppermute(x, axis, [(0, to)]), held)
    return held, lax.ppermute(held, axis, [(i, i + 1) for i in range(0, count, 2)])


INWARD = [(0, 1), (3, 2)]
MIDDLE = [(1, 2), (2, 1)]
OUTWARD = [(1, 0), (2, 3)]


def mix(before, centre, after, taps):
    before, centre, after = (v.astype(F32) for v in (before, centre, after))
    return (centre + taps[0] * before + taps[1] * centre + taps[2] * after).astype(BF16)


def split_rows(scales):
    parts, rest = [], scales
    for _ in range(3):
        part = lax.reduce_precision(rest, 8, 7)
        parts.append(part.astype(BF16))
        rest = rest - part
    rows = jnp.concatenate(parts, axis=0)
    return jnp.pad(rows, ((0, 16 - rows.shape[0]), (0, 0)))


def joined_rows(rows, count):
    high, middle, low = (rows[i * count : (i + 1) * count].astype(F32) for i in range(3))
    return high + middle + low


def per_device(frames, taps, w_query, w_key, w_value, q_gain, k_gain):
    count = lax.axis_size("tm")
    pos = lax.axis_index("tm")
    z = lax.axis_index("head").astype(jnp.int32)
    outer = (z == 0) | (z == 3)
    near, far = (z + 2) % 4, 3 - z
    side = outer.astype(jnp.int32)
    pair, second, third = z ^ 1, jnp.where(outer, near, far), jnp.where(outer, far, near)
    info = jnp.stack([side, z, pair, second, third])
    info_raw, info_end = jnp.stack([side, z, pair, second]), jnp.stack([side, third])
    hold = lax.optimization_barrier
    weights = (w_query, w_key, w_value)
    gains = (q_gain, k_gain)
    ups = [(i, i + 1) for i in range(count - 1)]
    downs = [(j, i) for i, j in ups]
    start = pos == 0

    def send(x, pairs):
        return lax.ppermute(x, "head", pairs)

    def mix_first(first, last, following, scales):
        return mix(
            jnp.where(start, jnp.zeros_like(first), first),
            jnp.where(start, first, last),
            jnp.where(start, last, following),
            scales,
        )

    def mix_second(first, last, following, preceding, scales):
        return mix(
            jnp.where(start, first, preceding),
            jnp.where(start, last, first),
            jnp.where(start, following, last),
            scales,
        )

    raw_first = send(frames[0], OUTWARD)
    following = lax.ppermute(frames[0], "tm", downs)
    mixed1 = mix_first(frames[0], frames[1], following, taps)
    last = jnp.concatenate([frames[1], split_rows(taps)], axis=0)
    later, last, mixed1 = hold((frames, last, mixed1))
    inward1, middle1 = send(mixed1, INWARD), send(mixed1, MIDDLE)
    raw_last = send(last, OUTWARD)
    later, raw_first = hold((later[1], raw_first))
    preceding = lax.ppermute(later, "tm", ups)
    mixed2 = mix_second(frames[0], frames[1], following, preceding, taps)
    raw_following = lax.ppermute(raw_first, "tm", downs)
    inward1, middle1 = hold((inward1, middle1))
    cross1, second1 = send(inward1, MIDDLE), send(middle1, OUTWARD)
    outer_taps = joined_rows(raw_last[later.shape[0] :], taps.shape[0])
    raw_last = raw_last[: later.shape[0]]
    raw_preceding = lax.ppermute(raw_last, "tm", ups)
    middle2, inward2 = send(mixed2, MIDDLE), send(mixed2, INWARD)
    level = (cross1, second1, raw_following, raw_preceding)
    cross1, second1, raw_following, raw_preceding = hold(level)
    third1 = send(cross1, OUTWARD)
    first1 = mix_first(raw_first, raw_last, raw_following, outer_taps)
    first2 = mix_second(raw_first, raw_last, raw_following, raw_preceding, outer_taps)
    middle2, first1, first2 = hold((middle2, first1, first2))
    cross2, second2 = send(inward2, MIDDLE), send(middle2, OUTWARD)

    sources1 = [(mixed1,), (inward1, first1), (middle1, second1), (cross1, third1)]
    q1, kv1 = project(sources1, info, weights, gains, after=(inward2, middle2), flops=10**10)
    beside = lax.ppermute(inward2[:16], "tm", [(i, i ^ 1) for i in range(count)])
    kv1, beside = hold((kv1, beside))
    third2 = send(cross2, OUTWARD)
    anchor = broadcast_first(kv1, "tm")
    cut = 5 * kv1.shape[2] // 8
    pieces = hold((kv1[:, :, :cut], kv1[:, :, cut:], anchor[0]))
    shift1 = [lax.ppermute(x, "tm", [(i, i + 1) for i in range(1, count - 1)]) for x in pieces[:2]]
    raw2 = project([(mixed2,), (inward2, first2), (middle2, second2)], info_raw, weights, after=(beside,), flops=10**10)
    q2, kv2 = finish(raw2, cross2, third2, info_end, weights, gains, 10**11)
    shift2 = lax.ppermute(kv2, "tm", [(0, 1)])
    anchor, shift1[0] = hold((anchor, shift1[0]))
    anchors = [[x] for x in anchor]
    late = jnp.where(start, 0, 1)
    odd = pos % 2
    result = attend([q1], anchors, odd, [[kv1], [kv2]], late, late)
    choice = jnp.minimum(pos, 1) + (pos == 1)
    return attend([q2], anchors, odd, [[kv1], shift1, [shift2]], choice, 1 - late, result)


def solution(mesh):
    placed = (
        P("tm", None, "head"),
        P(None, "head"),
        P(None, "head"),
        P(None, "head"),
        P(None, "head"),
        P("head"),
        P("head"),
    )
    return jax.shard_map(
        per_device, mesh=mesh, in_specs=placed, out_specs=P("tm", None, "head"), check_vma=False
    )
```

```python
import functools

import jax
import jax.numpy as jnp
from jax import lax
from jax.experimental import pallas as pl
from jax.experimental.pallas import tpu as pltpu
from jax.sharding import PartitionSpec as P

DH = 128
BF16 = jnp.bfloat16
F32 = jnp.float32
ANY = pl.BlockSpec(memory_space=pl.ANY)


def normalized(part, gain):
    square = part * part
    high = square.astype(BF16)
    low = (square - high.astype(F32)).astype(BF16)
    ones = jnp.ones((2 * DH, DH), BF16)
    total = jnp.dot(jnp.concatenate([high, low], axis=1), ones, preferred_element_type=F32)
    return (part * lax.rsqrt(total * (1.0 / DH) + 1e-06) * gain).astype(BF16)


def store_head(raw, gains, q_out, kv_out, h):
    q_out[h] = normalized(raw[0], gains[0])
    kv_out[0, h] = normalized(raw[1], gains[1])
    kv_out[1, h] = raw[2].astype(BF16)


def project_body(pairs, extra, wide, final, info, *refs):
    refs = list(refs)[extra:]
    count = len(pairs)
    groups = [[refs.pop(0) for _ in range(n)] for n in pairs]
    weights = [refs.pop(0) for _ in range(wide)]
    gain = refs.pop(0) if final else None
    out = refs.pop(0) if final else None
    acc, xbuf, sem = refs
    heads = weights[0].shape[1] // DH
    step = pl.program_id(0)

    @pl.when(step == 0)
    def _():
        for i, group in enumerate(groups):
            for j, source in enumerate(group):

                @pl.when((info[0] == j) | (len(group) == 1))
                def _(i=i, source=source):
                    pltpu.make_async_copy(source, xbuf.at[i], sem.at[i]).start()

    for i in range(count):

        @pl.when(step == i)
        def _(i=i):
            pltpu.make_async_copy(groups[i][0], xbuf.at[i], sem.at[i]).wait()
            weight = jnp.concatenate([w[...] for w in weights], axis=1)
            part = jnp.dot(xbuf[i], weight, preferred_element_type=F32)
            if final:
                acc[...] = part if i == 0 else acc[...] + part
            else:
                for group in range(3):
                    for h in range(heads):
                        columns = part[:, (group * heads + h) * DH : (group * heads + h + 1) * DH]
                        acc[group, h] = columns if i == 0 else acc[group, h] + columns

    if final:

        @pl.when(step == count - 1)
        def _():
            for h in range(heads):
                span = slice(h * DH, (h + 1) * DH)
                scaled = normalized(acc[:, span], gain[:, span])
                if wide == 1:
                    out[h] = scaled
                else:
                    out[0, h] = scaled
                    out[1, h] = acc[:, (heads + h) * DH : (heads + h + 1) * DH].astype(BF16)


def project(sources, info, weights, gain=None, after=(), flops=1):
    pairs = [len(s) for s in sources]
    count = len(pairs)
    rows, chans = sources[0][0].shape
    width = weights[0].shape[1]
    heads = width // DH
    final, wide = gain is not None, len(weights)
    a_spec = pl.BlockSpec((3, heads, rows, DH), lambda k, info: (0, 0, 0, 0))
    in_specs = [ANY] * (len(after) + sum(pairs)) + [pl.BlockSpec((chans, width), lambda k, info: (info[1 + k], 0))] * wide
    args = list(after) + [x for s in sources for x in s] + list(weights)
    scratch = [pltpu.VMEM((count, rows, chans), BF16), pltpu.SemaphoreType.DMA((count,))]
    raw = jax.ShapeDtypeStruct((3, heads, rows, DH), F32)
    if final:
        in_specs += [pl.BlockSpec((1, width), lambda k, info: (0, 0))]
        args += [gain[None]]
        shape = (heads, rows, DH) if wide == 1 else (2, heads, rows, DH)
        out_shape = jax.ShapeDtypeStruct(shape, BF16)
        out_specs = pl.BlockSpec(shape, lambda k, info: (0,) * len(shape))
        scratch = [pltpu.VMEM((rows, wide * width), F32)] + scratch
    else:
        out_shape, out_specs = raw, a_spec
    return pl.pallas_call(
        functools.partial(project_body, pairs, len(after), wide, final),
        grid_spec=pltpu.PrefetchScalarGridSpec(
            num_scalar_prefetch=1,
            grid=(count,),
            in_specs=in_specs,
            out_specs=out_specs,
            scratch_shapes=scratch,
        ),
        out_shape=out_shape,
        compiler_params=pltpu.CompilerParams(vmem_limit_bytes=48 * 2**20),
        cost_estimate=pl.CostEstimate(flops=flops, bytes_accessed=1, transcendentals=0),
        name="project" + ("_end" if final else "_raw"),
    )(info, *args)


def finish_body(info, inner, outer, wq, wk, wv, qg, kg, raw, q_out, kv_out, rows, sem):
    @pl.when(pl.program_id(0) == 0)
    def _():
        for side, source in enumerate((inner, outer)):

            @pl.when(info[0] == side)
            def _(source=source):
                pltpu.make_async_copy(source, rows, sem).start()

        pltpu.make_async_copy(inner, rows, sem).wait()

    weight = jnp.concatenate([wq[...], wk[...], wv[...]], axis=1)
    part = jnp.dot(rows[...], weight, preferred_element_type=F32)
    total = [raw[group, 0] + part[:, group * DH : (group + 1) * DH] for group in range(3)]
    store_head(total, (qg[...], kg[...]), q_out, kv_out, 0)


def finish(raw, inner, outer, info, weights, gains, flops):
    rows, chans = inner.shape
    heads = raw.shape[1]
    w_spec = pl.BlockSpec((chans, DH), lambda h, info: (info[1], h))
    g_spec = pl.BlockSpec((1, DH), lambda h, info: (0, h))
    return pl.pallas_call(
        finish_body,
        grid_spec=pltpu.PrefetchScalarGridSpec(
            num_scalar_prefetch=1,
            grid=(heads,),
            in_specs=[ANY] * 2
            + [w_spec] * 3
            + [g_spec] * 2
            + [pl.BlockSpec((3, 1, rows, DH), lambda h, info: (0, h, 0, 0))],
            out_specs=[
                pl.BlockSpec((1, rows, DH), lambda h, info: (h, 0, 0)),
                pl.BlockSpec((2, 1, rows, DH), lambda h, info: (0, h, 0, 0)),
            ],
            scratch_shapes=[pltpu.VMEM((rows, chans), BF16), pltpu.SemaphoreType.DMA],
        ),
        out_shape=[
            jax.ShapeDtypeStruct((heads, rows, DH), BF16),
            jax.ShapeDtypeStruct((2, heads, rows, DH), BF16),
        ],
        compiler_params=pltpu.CompilerParams(vmem_limit_bytes=48 * 2**20),
        cost_estimate=pl.CostEstimate(flops=flops, bytes_accessed=1, transcendentals=0),
        name="finish",
    )(info, inner, outer, *weights, *(g[None] for g in gains), raw)


def attend_body(row_block, asked, choices, fresh, info, *refs):
    refs = list(refs)
    queries = [refs.pop(0) for _ in range(asked)]
    options = [[[refs.pop(0) for _ in range(n)] for n in counts] for counts in choices]
    if not fresh:
        refs.pop(0)
    out, held, sem = refs
    h = pl.program_id(0)

    def fetch(part, pieces, head):
        row = 0
        for piece in pieces:
            place = held.at[part, :, head, pl.ds(row, piece.shape[2])]
            pltpu.make_async_copy(piece.at[:, head], place, sem.at[part, head]).start()
            row += piece.shape[2]

    @pl.when(h == 0)
    def _():
        for head in range(held.shape[2]):
            for part in range(2):
                for j, source in enumerate(options[part]):

                    @pl.when(info[2 * part] == j)
                    def _(part=part, source=source, head=head):
                        fetch(part, source, head)

    for part in range(2):
        pltpu.make_async_copy(held.at[part, :, h], held.at[part, :, h], sem.at[part, h]).wait()
    factor = 1.4426950408889634 / DH**0.5
    key = jnp.concatenate([held[0, 0, h], held[1, 0, h]], axis=0)
    value = jnp.concatenate([held[0, 1, h], held[1, 1, h]], axis=0)
    value = jnp.concatenate([value, jnp.ones_like(value)], axis=1)
    blocks = [query[0, r : r + row_block, :] for query in queries for r in range(0, query.shape[1], row_block)]

    def score(block):
        return lax.dot_general(block, key, (((1,), (1,)), ((), ())), preferred_element_type=F32)

    ahead = score(blocks[0])
    for r in range(len(blocks)):
        scores = ahead
        if r + 1 < len(blocks):
            ahead = score(blocks[r + 1])
        tops = [scores[:, c : c + DH] for c in range(0, scores.shape[1], DH)]
        top = jnp.max(functools.reduce(jnp.maximum, tops), axis=-1, keepdims=True)
        expo = jnp.exp2((scores - top) * factor).astype(BF16)
        result = jnp.dot(expo, value, preferred_element_type=F32)
        out[0, r * row_block : (r + 1) * row_block, :] = (result[:, :DH] / result[:, DH:]).astype(BF16)


def attend(queries, anchors, anchor, options, choice, frame, partly=None):
    heads = queries[0].shape[0]
    rows = sum(query.shape[1] for query in queries)
    args = list(queries) + [piece for pieces in (*anchors, *options) for piece in pieces]
    counts = [[len(pieces) for pieces in group] for group in (anchors, options)]
    aliases = {}
    if partly is not None:
        aliases = {1 + len(args): 0}
        args.append(partly)
    return pl.pallas_call(
        functools.partial(attend_body, 256, len(queries), counts, partly is None),
        grid_spec=pltpu.PrefetchScalarGridSpec(
            num_scalar_prefetch=1,
            grid=(heads,),
            in_specs=[pl.BlockSpec((1, q.shape[1], DH), lambda h, info: (h, 0, 0)) for q in queries]
            + [ANY] * (len(args) - len(queries)),
            out_specs=pl.BlockSpec((1, rows, DH), lambda h, info: (info[1], 0, h)),
            scratch_shapes=[
                pltpu.VMEM((2, 2, heads, rows, DH), BF16),
                pltpu.SemaphoreType.DMA((2, heads)),
            ],
        ),
        out_shape=jax.ShapeDtypeStruct((2, rows, heads * DH), BF16),
        input_output_aliases=aliases,
        compiler_params=pltpu.CompilerParams(vmem_limit_bytes=32 * 2**20),
        cost_estimate=pl.CostEstimate(
            flops=10 * 8 * heads * rows * rows * DH,
            bytes_accessed=2 * heads * rows * DH * 6,
            transcendentals=2 * heads * rows * rows,
        ),
        name="attend",
    )(jnp.stack([anchor, frame, choice]).astype(jnp.int32), *args)


def broadcast_first(x, axis):
    count = lax.axis_size(axis)
    mine = lax.axis_index(axis)
    held = x
    for to in reversed(range(2, count, 2)):
        held = jnp.where(mine == to, lax.ppermute(x, axis, [(0, to)]), held)
    return held, lax.ppermute(held, axis, [(i, i + 1) for i in range(0, count, 2)])


INWARD = [(0, 1), (3, 2)]
MIDDLE = [(1, 2), (2, 1)]
OUTWARD = [(1, 0), (2, 3)]


def mix(before, centre, after, taps):
    before, centre, after = (v.astype(F32) for v in (before, centre, after))
    return (centre + taps[0] * before + taps[1] * centre + taps[2] * after).astype(BF16)


def split_rows(scales):
    parts, rest = [], scales
    for _ in range(3):
        part = lax.reduce_precision(rest, 8, 7)
        parts.append(part.astype(BF16))
        rest = rest - part
    rows = jnp.concatenate(parts, axis=0)
    return jnp.pad(rows, ((0, 16 - rows.shape[0]), (0, 0)))


def joined_rows(rows, count):
    high, middle, low = (rows[i * count : (i + 1) * count].astype(F32) for i in range(3))
    return high + middle + low


def per_device(frames, taps, w_query, w_key, w_value, q_gain, k_gain):
    count = lax.axis_size("tm")
    pos = lax.axis_index("tm")
    z = lax.axis_index("head").astype(jnp.int32)
    outer = (z == 0) | (z == 3)
    near, far = (z + 2) % 4, 3 - z
    side = outer.astype(jnp.int32)
    pair, second, third = z ^ 1, jnp.where(outer, near, far), jnp.where(outer, far, near)
    info = jnp.stack([side, z, pair, second, third])
    info_raw, info_end = jnp.stack([side, z, pair, second]), jnp.stack([side, third])
    hold = lax.optimization_barrier
    weights = (w_query, w_key, w_value)
    gains = (q_gain, k_gain)
    ups = [(i, i + 1) for i in range(count - 1)]
    downs = [(j, i) for i, j in ups]
    start = pos == 0

    def send(x, pairs):
        return lax.ppermute(x, "head", pairs)

    def mix_first(first, last, following, scales):
        return mix(
            jnp.where(start, jnp.zeros_like(first), first),
            jnp.where(start, first, last),
            jnp.where(start, last, following),
            scales,
        )

    def mix_second(first, last, following, preceding, scales):
        return mix(
            jnp.where(start, first, preceding),
            jnp.where(start, last, first),
            jnp.where(start, following, last),
            scales,
        )

    raw_first = send(frames[0], OUTWARD)
    following = lax.ppermute(frames[0], "tm", downs)
    mixed1 = mix_first(frames[0], frames[1], following, taps)
    last = jnp.concatenate([frames[1], split_rows(taps)], axis=0)
    later, last, mixed1 = hold((frames, last, mixed1))
    inward1, middle1 = send(mixed1, INWARD), send(mixed1, MIDDLE)
    raw_last = send(last, OUTWARD)
    later, raw_first = hold((later[1], raw_first))
    preceding = lax.ppermute(later, "tm", ups)
    mixed2 = mix_second(frames[0], frames[1], following, preceding, taps)
    raw_following = lax.ppermute(raw_first, "tm", downs)
    inward1, middle1 = hold((inward1, middle1))
    cross1, second1 = send(inward1, MIDDLE), send(middle1, OUTWARD)
    outer_taps = joined_rows(raw_last[later.shape[0] :], taps.shape[0])
    raw_last = raw_last[: later.shape[0]]
    raw_preceding = lax.ppermute(raw_last, "tm", ups)
    middle2, inward2 = send(mixed2, MIDDLE), send(mixed2, INWARD)
    level = (cross1, second1, raw_following, raw_preceding)
    cross1, second1, raw_following, raw_preceding = hold(level)
    third1 = send(cross1, OUTWARD)
    first1 = mix_first(raw_first, raw_last, raw_following, outer_taps)
    first2 = mix_second(raw_first, raw_last, raw_following, raw_preceding, outer_taps)
    middle2, first1, first2 = hold((middle2, first1, first2))
    cross2, second2 = send(inward2, MIDDLE), send(middle2, OUTWARD)

    sources1 = [(mixed1,), (inward1, first1), (middle1, second1), (cross1, third1)]
    kv1 = project(sources1, info, weights[1:], k_gain, after=(inward2, middle2), flops=10**10)
    q1 = project(sources1, info, weights[:1], q_gain, after=(kv1,), flops=10**9)
    beside = lax.ppermute(inward2[:16], "tm", [(i, i ^ 1) for i in range(count)])
    kv1, beside = hold((kv1, beside))
    third2 = send(cross2, OUTWARD)
    anchor = broadcast_first(kv1, "tm")
    cut = 3 * kv1.shape[2] // 4
    pieces = hold((kv1[:, :, :cut], kv1[:, :, cut:], anchor[0]))
    shift1 = [lax.ppermute(x, "tm", [(i, i + 1) for i in range(1, count - 1)]) for x in pieces[:2]]
    raw2 = project([(mixed2,), (inward2, first2), (middle2, second2)], info_raw, weights, after=(beside, q1), flops=10**10)
    q2, kv2 = finish(raw2, cross2, third2, info_end, weights, gains, 10**11)
    shift2 = lax.ppermute(kv2, "tm", [(0, 1)])
    anchor, shift1[0] = hold((anchor, shift1[0]))
    anchors = [[x] for x in anchor]
    late = jnp.where(start, 0, 1)
    odd = pos % 2
    result = attend([q1], anchors, odd, [[kv1], [kv2]], late, late)
    choice = jnp.minimum(pos, 1) + (pos == 1)
    return attend([q2], anchors, odd, [[kv1], shift1, [shift2]], choice, 1 - late, result)


def solution(mesh):
    placed = (
        P("tm", None, "head"),
        P(None, "head"),
        P(None, "head"),
        P(None, "head"),
        P(None, "head"),
        P("head"),
        P("head"),
    )
    return jax.shard_map(
        per_device, mesh=mesh, in_specs=placed, out_specs=P("tm", None, "head"), check_vma=False
    )
```

```python
import functools

import jax
import jax.numpy as jnp
from jax import lax
from jax.experimental import pallas as pl
from jax.experimental.pallas import tpu as pltpu
from jax.sharding import PartitionSpec as P

DH = 128
BF16 = jnp.bfloat16
F32 = jnp.float32
ANY = pl.BlockSpec(memory_space=pl.ANY)


def normalized(part, gain):
    square = part * part
    high = square.astype(BF16)
    low = (square - high.astype(F32)).astype(BF16)
    ones = jnp.ones((2 * DH, DH), BF16)
    total = jnp.dot(jnp.concatenate([high, low], axis=1), ones, preferred_element_type=F32)
    return (part * lax.rsqrt(total * (1.0 / DH) + 1e-06) * gain).astype(BF16)


def store_head(raw, gains, q_out, kv_out, h):
    q_out[h] = normalized(raw[0], gains[0])
    kv_out[0, h] = normalized(raw[1], gains[1])
    kv_out[1, h] = raw[2].astype(BF16)


def project_body(pairs, extra, wide, final, info, *refs):
    refs = list(refs)[extra:]
    count = len(pairs)
    groups = [[refs.pop(0) for _ in range(n)] for n in pairs]
    weights = [refs.pop(0) for _ in range(wide)]
    gain = refs.pop(0) if final else None
    out = refs.pop(0) if final else None
    acc, xbuf, sem = refs
    heads = weights[0].shape[1] // DH
    step = pl.program_id(0)

    @pl.when(step == 0)
    def _():
        for i, group in enumerate(groups):
            for j, source in enumerate(group):

                @pl.when((info[0] == j) | (len(group) == 1))
                def _(i=i, source=source):
                    pltpu.make_async_copy(source, xbuf.at[i], sem.at[i]).start()

    for i in range(count):

        @pl.when(step == i)
        def _(i=i):
            pltpu.make_async_copy(groups[i][0], xbuf.at[i], sem.at[i]).wait()
            weight = jnp.concatenate([w[...] for w in weights], axis=1)
            part = jnp.dot(xbuf[i], weight, preferred_element_type=F32)
            if final:
                acc[...] = part if i == 0 else acc[...] + part
            else:
                for group in range(3):
                    for h in range(heads):
                        columns = part[:, (group * heads + h) * DH : (group * heads + h + 1) * DH]
                        acc[group, h] = columns if i == 0 else acc[group, h] + columns

    if final:

        @pl.when(step == count - 1)
        def _():
            for h in range(heads):
                span = slice(h * DH, (h + 1) * DH)
                scaled = normalized(acc[:, span], gain[:, span])
                if wide == 1:
                    out[h] = scaled
                else:
                    out[0, h] = scaled
                    out[1, h] = acc[:, (heads + h) * DH : (heads + h + 1) * DH].astype(BF16)


def project(sources, info, weights, gain=None, after=(), flops=1):
    pairs = [len(s) for s in sources]
    count = len(pairs)
    rows, chans = sources[0][0].shape
    width = weights[0].shape[1]
    heads = width // DH
    final, wide = gain is not None, len(weights)
    a_spec = pl.BlockSpec((3, heads, rows, DH), lambda k, info: (0, 0, 0, 0))
    in_specs = [ANY] * (len(after) + sum(pairs)) + [pl.BlockSpec((chans, width), lambda k, info: (info[1 + k], 0))] * wide
    args = list(after) + [x for s in sources for x in s] + list(weights)
    scratch = [pltpu.VMEM((count, rows, chans), BF16), pltpu.SemaphoreType.DMA((count,))]
    raw = jax.ShapeDtypeStruct((3, heads, rows, DH), F32)
    if final:
        in_specs += [pl.BlockSpec((1, width), lambda k, info: (0, 0))]
        args += [gain[None]]
        shape = (heads, rows, DH) if wide == 1 else (2, heads, rows, DH)
        out_shape = jax.ShapeDtypeStruct(shape, BF16)
        out_specs = pl.BlockSpec(shape, lambda k, info: (0,) * len(shape))
        scratch = [pltpu.VMEM((rows, wide * width), F32)] + scratch
    else:
        out_shape, out_specs = raw, a_spec
    return pl.pallas_call(
        functools.partial(project_body, pairs, len(after), wide, final),
        grid_spec=pltpu.PrefetchScalarGridSpec(
            num_scalar_prefetch=1,
            grid=(count,),
            in_specs=in_specs,
            out_specs=out_specs,
            scratch_shapes=scratch,
        ),
        out_shape=out_shape,
        compiler_params=pltpu.CompilerParams(vmem_limit_bytes=48 * 2**20),
        cost_estimate=pl.CostEstimate(flops=flops, bytes_accessed=1, transcendentals=0),
        name="project" + ("_end" if final else "_raw"),
    )(info, *args)


def finish_body(info, inner, outer, wq, wk, wv, qg, kg, raw, q_out, kv_out, rows, sem):
    @pl.when(pl.program_id(0) == 0)
    def _():
        for side, source in enumerate((inner, outer)):

            @pl.when(info[0] == side)
            def _(source=source):
                pltpu.make_async_copy(source, rows, sem).start()

        pltpu.make_async_copy(inner, rows, sem).wait()

    weight = jnp.concatenate([wq[...], wk[...], wv[...]], axis=1)
    part = jnp.dot(rows[...], weight, preferred_element_type=F32)
    total = [raw[group, 0] + part[:, group * DH : (group + 1) * DH] for group in range(3)]
    store_head(total, (qg[...], kg[...]), q_out, kv_out, 0)


def finish(raw, inner, outer, info, weights, gains, flops):
    rows, chans = inner.shape
    heads = raw.shape[1]
    w_spec = pl.BlockSpec((chans, DH), lambda h, info: (info[1], h))
    g_spec = pl.BlockSpec((1, DH), lambda h, info: (0, h))
    return pl.pallas_call(
        finish_body,
        grid_spec=pltpu.PrefetchScalarGridSpec(
            num_scalar_prefetch=1,
            grid=(heads,),
            in_specs=[ANY] * 2
            + [w_spec] * 3
            + [g_spec] * 2
            + [pl.BlockSpec((3, 1, rows, DH), lambda h, info: (0, h, 0, 0))],
            out_specs=[
                pl.BlockSpec((1, rows, DH), lambda h, info: (h, 0, 0)),
                pl.BlockSpec((2, 1, rows, DH), lambda h, info: (0, h, 0, 0)),
            ],
            scratch_shapes=[pltpu.VMEM((rows, chans), BF16), pltpu.SemaphoreType.DMA],
        ),
        out_shape=[
            jax.ShapeDtypeStruct((heads, rows, DH), BF16),
            jax.ShapeDtypeStruct((2, heads, rows, DH), BF16),
        ],
        compiler_params=pltpu.CompilerParams(vmem_limit_bytes=48 * 2**20),
        cost_estimate=pl.CostEstimate(flops=flops, bytes_accessed=1, transcendentals=0),
        name="finish",
    )(info, inner, outer, *weights, *(g[None] for g in gains), raw)


def attend_body(row_block, asked, choices, fresh, info, *refs):
    refs = list(refs)
    queries = [refs.pop(0) for _ in range(asked)]
    options = [[[refs.pop(0) for _ in range(n)] for n in counts] for counts in choices]
    if not fresh:
        refs.pop(0)
    out, held, sem = refs
    h = pl.program_id(0)

    def fetch(part, pieces, head):
        row = 0
        for piece in pieces:
            place = held.at[part, :, head, pl.ds(row, piece.shape[2])]
            pltpu.make_async_copy(piece.at[:, head], place, sem.at[part, head]).start()
            row += piece.shape[2]

    @pl.when(h == 0)
    def _():
        for head in range(held.shape[2]):
            for part in range(2):
                for j, source in enumerate(options[part]):

                    @pl.when(info[2 * part] == j)
                    def _(part=part, source=source, head=head):
                        fetch(part, source, head)

    for part in range(2):
        pltpu.make_async_copy(held.at[part, :, h], held.at[part, :, h], sem.at[part, h]).wait()
    factor = 1.4426950408889634 / DH**0.5
    key = jnp.concatenate([held[0, 0, h], held[1, 0, h]], axis=0)
    value = jnp.concatenate([held[0, 1, h], held[1, 1, h]], axis=0)
    value = jnp.concatenate([value, jnp.ones_like(value)], axis=1)
    blocks = [query[0, r : r + row_block, :] for query in queries for r in range(0, query.shape[1], row_block)]

    def score(block):
        return lax.dot_general(block, key, (((1,), (1,)), ((), ())), preferred_element_type=F32)

    ahead = score(blocks[0])
    for r in range(len(blocks)):
        scores = ahead
        if r + 1 < len(blocks):
            ahead = score(blocks[r + 1])
        tops = [scores[:, c : c + DH] for c in range(0, scores.shape[1], DH)]
        top = jnp.max(functools.reduce(jnp.maximum, tops), axis=-1, keepdims=True)
        expo = jnp.exp2((scores - top) * factor).astype(BF16)
        result = jnp.dot(expo, value, preferred_element_type=F32)
        out[0, r * row_block : (r + 1) * row_block, :] = (result[:, :DH] / result[:, DH:]).astype(BF16)


def attend(queries, anchors, anchor, options, choice, frame, partly=None):
    heads = queries[0].shape[0]
    rows = sum(query.shape[1] for query in queries)
    args = list(queries) + [piece for pieces in (*anchors, *options) for piece in pieces]
    counts = [[len(pieces) for pieces in group] for group in (anchors, options)]
    aliases = {}
    if partly is not None:
        aliases = {1 + len(args): 0}
        args.append(partly)
    return pl.pallas_call(
        functools.partial(attend_body, 256, len(queries), counts, partly is None),
        grid_spec=pltpu.PrefetchScalarGridSpec(
            num_scalar_prefetch=1,
            grid=(heads,),
            in_specs=[pl.BlockSpec((1, q.shape[1], DH), lambda h, info: (h, 0, 0)) for q in queries]
            + [ANY] * (len(args) - len(queries)),
            out_specs=pl.BlockSpec((1, rows, DH), lambda h, info: (info[1], 0, h)),
            scratch_shapes=[
                pltpu.VMEM((2, 2, heads, rows, DH), BF16),
                pltpu.SemaphoreType.DMA((2, heads)),
            ],
        ),
        out_shape=jax.ShapeDtypeStruct((2, rows, heads * DH), BF16),
        input_output_aliases=aliases,
        compiler_params=pltpu.CompilerParams(vmem_limit_bytes=32 * 2**20),
        cost_estimate=pl.CostEstimate(
            flops=10 * 8 * heads * rows * rows * DH,
            bytes_accessed=2 * heads * rows * DH * 6,
            transcendentals=2 * heads * rows * rows,
        ),
        name="attend",
    )(jnp.stack([anchor, frame, choice]).astype(jnp.int32), *args)


def broadcast_first(x, axis):
    count = lax.axis_size(axis)
    mine = lax.axis_index(axis)
    held = x
    for to in reversed(range(2, count, 2)):
        held = jnp.where(mine == to, lax.ppermute(x, axis, [(0, to)]), held)
    return held, lax.ppermute(held, axis, [(i, i + 1) for i in range(0, count, 2)])


INWARD = [(0, 1), (3, 2)]
MIDDLE = [(1, 2), (2, 1)]
OUTWARD = [(1, 0), (2, 3)]


def mix(before, centre, after, taps):
    before, centre, after = (v.astype(F32) for v in (before, centre, after))
    return (centre + taps[0] * before + taps[1] * centre + taps[2] * after).astype(BF16)


def split_rows(scales):
    parts, rest = [], scales
    for _ in range(3):
        part = lax.reduce_precision(rest, 8, 7)
        parts.append(part.astype(BF16))
        rest = rest - part
    rows = jnp.concatenate(parts, axis=0)
    return jnp.pad(rows, ((0, 16 - rows.shape[0]), (0, 0)))


def joined_rows(rows, count):
    high, middle, low = (rows[i * count : (i + 1) * count].astype(F32) for i in range(3))
    return high + middle + low


def per_device(frames, taps, w_query, w_key, w_value, q_gain, k_gain):
    count = lax.axis_size("tm")
    pos = lax.axis_index("tm")
    z = lax.axis_index("head").astype(jnp.int32)
    outer = (z == 0) | (z == 3)
    near, far = (z + 2) % 4, 3 - z
    side = outer.astype(jnp.int32)
    pair, second, third = z ^ 1, jnp.where(outer, near, far), jnp.where(outer, far, near)
    info = jnp.stack([side, z, pair, second, third])
    info_raw, info_end = jnp.stack([side, z, pair, second]), jnp.stack([side, third])
    hold = lax.optimization_barrier
    weights = (w_query, w_key, w_value)
    gains = (q_gain, k_gain)
    ups = [(i, i + 1) for i in range(count - 1)]
    downs = [(j, i) for i, j in ups]
    start = pos == 0

    def send(x, pairs):
        return lax.ppermute(x, "head", pairs)

    def mix_first(first, last, following, scales):
        return mix(
            jnp.where(start, jnp.zeros_like(first), first),
            jnp.where(start, first, last),
            jnp.where(start, last, following),
            scales,
        )

    def mix_second(first, last, following, preceding, scales):
        return mix(
            jnp.where(start, first, preceding),
            jnp.where(start, last, first),
            jnp.where(start, following, last),
            scales,
        )

    raw_first = send(frames[0], OUTWARD)
    following = lax.ppermute(frames[0], "tm", downs)
    mixed1 = mix_first(frames[0], frames[1], following, taps)
    last = jnp.concatenate([frames[1], split_rows(taps)], axis=0)
    later, last, mixed1 = hold((frames, last, mixed1))
    inward1, middle1 = send(mixed1, INWARD), send(mixed1, MIDDLE)
    raw_last = send(last, OUTWARD)
    later, raw_first = hold((later[1], raw_first))
    preceding = lax.ppermute(later, "tm", ups)
    mixed2 = mix_second(frames[0], frames[1], following, preceding, taps)
    raw_following = lax.ppermute(raw_first, "tm", downs)
    inward1, middle1 = hold((inward1, middle1))
    cross1, second1 = send(inward1, MIDDLE), send(middle1, OUTWARD)
    outer_taps = joined_rows(raw_last[later.shape[0] :], taps.shape[0])
    raw_last = raw_last[: later.shape[0]]
    raw_preceding = lax.ppermute(raw_last, "tm", ups)
    middle2, inward2 = send(mixed2, MIDDLE), send(mixed2, INWARD)
    level = (cross1, second1, raw_following, raw_preceding)
    cross1, second1, raw_following, raw_preceding = hold(level)
    third1 = send(cross1, OUTWARD)
    first1 = mix_first(raw_first, raw_last, raw_following, outer_taps)
    first2 = mix_second(raw_first, raw_last, raw_following, raw_preceding, outer_taps)
    middle2, first1, first2 = hold((middle2, first1, first2))
    cross2, second2 = send(inward2, MIDDLE), send(middle2, OUTWARD)

    sources1 = [(mixed1,), (inward1, first1), (middle1, second1), (cross1, third1)]
    kv1 = project(sources1, info, weights[1:], k_gain, after=(inward2, middle2), flops=10**10)
    q1 = project(sources1, info, weights[:1], q_gain, after=(kv1,), flops=10**9)
    beside = lax.ppermute(inward2[:16], "tm", [(i, i ^ 1) for i in range(count)])
    kv1, beside = hold((kv1, beside))
    third2 = send(cross2, OUTWARD)
    anchor = broadcast_first(kv1, "tm")
    cut = 5 * kv1.shape[2] // 8
    pieces = hold((kv1[:, :, :cut], kv1[:, :, cut:], anchor[0]))
    shift1 = [lax.ppermute(x, "tm", [(i, i + 1) for i in range(1, count - 1)]) for x in pieces[:2]]
    raw2 = project([(mixed2,), (inward2, first2), (middle2, second2)], info_raw, weights, after=(beside, q1), flops=10**10)
    q2, kv2 = finish(raw2, cross2, third2, info_end, weights, gains, 10**11)
    shift2 = lax.ppermute(kv2, "tm", [(0, 1)])
    anchor, shift1[0] = hold((anchor, shift1[0]))
    anchors = [[x] for x in anchor]
    late = jnp.where(start, 0, 1)
    odd = pos % 2
    result = attend([q1], anchors, odd, [[kv1], [kv2]], late, late)
    choice = jnp.minimum(pos, 1) + (pos == 1)
    return attend([q2], anchors, odd, [[kv1], shift1, [shift2]], choice, 1 - late, result)


def solution(mesh):
    placed = (
        P("tm", None, "head"),
        P(None, "head"),
        P(None, "head"),
        P(None, "head"),
        P(None, "head"),
        P("head"),
        P("head"),
    )
    return jax.shard_map(
        per_device, mesh=mesh, in_specs=placed, out_specs=P("tm", None, "head"), check_vma=False
    )
```

```python
import functools

import jax
import jax.numpy as jnp
from jax import lax
from jax.experimental import pallas as pl
from jax.experimental.pallas import tpu as pltpu
from jax.sharding import PartitionSpec as P

DH = 128
BF16 = jnp.bfloat16
F32 = jnp.float32
ANY = pl.BlockSpec(memory_space=pl.ANY)


def normalized(part, gain):
    square = part * part
    high = square.astype(BF16)
    low = (square - high.astype(F32)).astype(BF16)
    ones = jnp.ones((2 * DH, DH), BF16)
    total = jnp.dot(jnp.concatenate([high, low], axis=1), ones, preferred_element_type=F32)
    return (part * lax.rsqrt(total * (1.0 / DH) + 1e-06) * gain).astype(BF16)


def store_head(raw, gains, q_out, kv_out, h):
    q_out[h] = normalized(raw[0], gains[0])
    kv_out[0, h] = normalized(raw[1], gains[1])
    kv_out[1, h] = raw[2].astype(BF16)


def project_body(pairs, extra, wide, final, info, *refs):
    refs = list(refs)[extra:]
    count = len(pairs)
    groups = [[refs.pop(0) for _ in range(n)] for n in pairs]
    weights = [refs.pop(0) for _ in range(wide)]
    gain = refs.pop(0) if final else None
    out = refs.pop(0) if final else None
    acc, xbuf, sem = refs
    heads = weights[0].shape[1] // DH
    step = pl.program_id(0)

    @pl.when(step == 0)
    def _():
        for i, group in enumerate(groups):
            for j, source in enumerate(group):

                @pl.when((info[0] == j) | (len(group) == 1))
                def _(i=i, source=source):
                    pltpu.make_async_copy(source, xbuf.at[i], sem.at[i]).start()

    for i in range(count):

        @pl.when(step == i)
        def _(i=i):
            pltpu.make_async_copy(groups[i][0], xbuf.at[i], sem.at[i]).wait()
            weight = jnp.concatenate([w[...] for w in weights], axis=1)
            part = jnp.dot(xbuf[i], weight, preferred_element_type=F32)
            if final:
                acc[...] = part if i == 0 else acc[...] + part
            else:
                for group in range(3):
                    for h in range(heads):
                        columns = part[:, (group * heads + h) * DH : (group * heads + h + 1) * DH]
                        acc[group, h] = columns if i == 0 else acc[group, h] + columns

    if final:

        @pl.when(step == count - 1)
        def _():
            for h in range(heads):
                span = slice(h * DH, (h + 1) * DH)
                scaled = normalized(acc[:, span], gain[:, span])
                if wide == 1:
                    out[h] = scaled
                else:
                    out[0, h] = scaled
                    out[1, h] = acc[:, (heads + h) * DH : (heads + h + 1) * DH].astype(BF16)


def project(sources, info, weights, gain=None, after=(), flops=1):
    pairs = [len(s) for s in sources]
    count = len(pairs)
    rows, chans = sources[0][0].shape
    width = weights[0].shape[1]
    heads = width // DH
    final, wide = gain is not None, len(weights)
    a_spec = pl.BlockSpec((3, heads, rows, DH), lambda k, info: (0, 0, 0, 0))
    in_specs = [ANY] * (len(after) + sum(pairs)) + [pl.BlockSpec((chans, width), lambda k, info: (info[1 + k], 0))] * wide
    args = list(after) + [x for s in sources for x in s] + list(weights)
    scratch = [pltpu.VMEM((count, rows, chans), BF16), pltpu.SemaphoreType.DMA((count,))]
    raw = jax.ShapeDtypeStruct((3, heads, rows, DH), F32)
    if final:
        in_specs += [pl.BlockSpec((1, width), lambda k, info: (0, 0))]
        args += [gain[None]]
        shape = (heads, rows, DH) if wide == 1 else (2, heads, rows, DH)
        out_shape = jax.ShapeDtypeStruct(shape, BF16)
        out_specs = pl.BlockSpec(shape, lambda k, info: (0,) * len(shape))
        scratch = [pltpu.VMEM((rows, wide * width), F32)] + scratch
    else:
        out_shape, out_specs = raw, a_spec
    return pl.pallas_call(
        functools.partial(project_body, pairs, len(after), wide, final),
        grid_spec=pltpu.PrefetchScalarGridSpec(
            num_scalar_prefetch=1,
            grid=(count,),
            in_specs=in_specs,
            out_specs=out_specs,
            scratch_shapes=scratch,
        ),
        out_shape=out_shape,
        compiler_params=pltpu.CompilerParams(vmem_limit_bytes=48 * 2**20),
        cost_estimate=pl.CostEstimate(flops=flops, bytes_accessed=1, transcendentals=0),
        name="project" + ("_end" if final else "_raw"),
    )(info, *args)


def finish_body(info, inner, outer, wq, wk, wv, qg, kg, raw, q_out, kv_out, rows, sem):
    @pl.when(pl.program_id(0) == 0)
    def _():
        for side, source in enumerate((inner, outer)):

            @pl.when(info[0] == side)
            def _(source=source):
                pltpu.make_async_copy(source, rows, sem).start()

        pltpu.make_async_copy(inner, rows, sem).wait()

    weight = jnp.concatenate([wq[...], wk[...], wv[...]], axis=1)
    part = jnp.dot(rows[...], weight, preferred_element_type=F32)
    total = [raw[group, 0] + part[:, group * DH : (group + 1) * DH] for group in range(3)]
    store_head(total, (qg[...], kg[...]), q_out, kv_out, 0)


def finish(raw, inner, outer, info, weights, gains, flops):
    rows, chans = inner.shape
    heads = raw.shape[1]
    w_spec = pl.BlockSpec((chans, DH), lambda h, info: (info[1], h))
    g_spec = pl.BlockSpec((1, DH), lambda h, info: (0, h))
    return pl.pallas_call(
        finish_body,
        grid_spec=pltpu.PrefetchScalarGridSpec(
            num_scalar_prefetch=1,
            grid=(heads,),
            in_specs=[ANY] * 2
            + [w_spec] * 3
            + [g_spec] * 2
            + [pl.BlockSpec((3, 1, rows, DH), lambda h, info: (0, h, 0, 0))],
            out_specs=[
                pl.BlockSpec((1, rows, DH), lambda h, info: (h, 0, 0)),
                pl.BlockSpec((2, 1, rows, DH), lambda h, info: (0, h, 0, 0)),
            ],
            scratch_shapes=[pltpu.VMEM((rows, chans), BF16), pltpu.SemaphoreType.DMA],
        ),
        out_shape=[
            jax.ShapeDtypeStruct((heads, rows, DH), BF16),
            jax.ShapeDtypeStruct((2, heads, rows, DH), BF16),
        ],
        compiler_params=pltpu.CompilerParams(vmem_limit_bytes=48 * 2**20),
        cost_estimate=pl.CostEstimate(flops=flops, bytes_accessed=1, transcendentals=0),
        name="finish",
    )(info, inner, outer, *weights, *(g[None] for g in gains), raw)


def attend_body(row_block, asked, choices, fresh, info, *refs):
    refs = list(refs)
    queries = [refs.pop(0) for _ in range(asked)]
    options = [[[refs.pop(0) for _ in range(n)] for n in counts] for counts in choices]
    if not fresh:
        refs.pop(0)
    out, held, sem = refs
    h = pl.program_id(0)

    def fetch(part, pieces, head):
        row = 0
        for piece in pieces:
            place = held.at[part, :, head, pl.ds(row, piece.shape[2])]
            pltpu.make_async_copy(piece.at[:, head], place, sem.at[part, head]).start()
            row += piece.shape[2]

    @pl.when(h == 0)
    def _():
        for head in range(held.shape[2]):
            for part in range(2):
                for j, source in enumerate(options[part]):

                    @pl.when(info[2 * part] == j)
                    def _(part=part, source=source, head=head):
                        fetch(part, source, head)

    for part in range(2):
        pltpu.make_async_copy(held.at[part, :, h], held.at[part, :, h], sem.at[part, h]).wait()
    factor = 1.4426950408889634 / DH**0.5
    key = jnp.concatenate([held[0, 0, h], held[1, 0, h]], axis=0)
    value = jnp.concatenate([held[0, 1, h], held[1, 1, h]], axis=0)
    value = jnp.concatenate([value, jnp.ones_like(value)], axis=1)
    blocks = [query[0, r : r + row_block, :] for query in queries for r in range(0, query.shape[1], row_block)]

    def score(block):
        return lax.dot_general(block, key, (((1,), (1,)), ((), ())), preferred_element_type=F32)

    ahead = score(blocks[0])
    for r in range(len(blocks)):
        scores = ahead
        if r + 1 < len(blocks):
            ahead = score(blocks[r + 1])
        tops = [scores[:, c : c + DH] for c in range(0, scores.shape[1], DH)]
        top = jnp.max(functools.reduce(jnp.maximum, tops), axis=-1, keepdims=True)
        expo = jnp.exp2((scores - top) * factor).astype(BF16)
        result = jnp.dot(expo, value, preferred_element_type=F32)
        out[0, r * row_block : (r + 1) * row_block, :] = (result[:, :DH] / result[:, DH:]).astype(BF16)


def attend(queries, anchors, anchor, options, choice, frame, partly=None):
    heads = queries[0].shape[0]
    rows = sum(query.shape[1] for query in queries)
    args = list(queries) + [piece for pieces in (*anchors, *options) for piece in pieces]
    counts = [[len(pieces) for pieces in group] for group in (anchors, options)]
    aliases = {}
    if partly is not None:
        aliases = {1 + len(args): 0}
        args.append(partly)
    return pl.pallas_call(
        functools.partial(attend_body, 256, len(queries), counts, partly is None),
        grid_spec=pltpu.PrefetchScalarGridSpec(
            num_scalar_prefetch=1,
            grid=(heads,),
            in_specs=[pl.BlockSpec((1, q.shape[1], DH), lambda h, info: (h, 0, 0)) for q in queries]
            + [ANY] * (len(args) - len(queries)),
            out_specs=pl.BlockSpec((1, rows, DH), lambda h, info: (info[1], 0, h)),
            scratch_shapes=[
                pltpu.VMEM((2, 2, heads, rows, DH), BF16),
                pltpu.SemaphoreType.DMA((2, heads)),
            ],
        ),
        out_shape=jax.ShapeDtypeStruct((2, rows, heads * DH), BF16),
        input_output_aliases=aliases,
        compiler_params=pltpu.CompilerParams(vmem_limit_bytes=32 * 2**20),
        cost_estimate=pl.CostEstimate(
            flops=10 * 8 * heads * rows * rows * DH,
            bytes_accessed=2 * heads * rows * DH * 6,
            transcendentals=2 * heads * rows * rows,
        ),
        name="attend",
    )(jnp.stack([anchor, frame, choice]).astype(jnp.int32), *args)


def broadcast_first(x, axis):
    count = lax.axis_size(axis)
    mine = lax.axis_index(axis)
    held = x
    for to in reversed(range(2, count, 2)):
        held = jnp.where(mine == to, lax.ppermute(x, axis, [(0, to)]), held)
    return held, lax.ppermute(held, axis, [(i, i + 1) for i in range(0, count, 2)])


INWARD = [(0, 1), (3, 2)]
MIDDLE = [(1, 2), (2, 1)]
OUTWARD = [(1, 0), (2, 3)]


def mix(before, centre, after, taps):
    before, centre, after = (v.astype(F32) for v in (before, centre, after))
    return (centre + taps[0] * before + taps[1] * centre + taps[2] * after).astype(BF16)


def split_rows(scales):
    parts, rest = [], scales
    for _ in range(3):
        part = lax.reduce_precision(rest, 8, 7)
        parts.append(part.astype(BF16))
        rest = rest - part
    rows = jnp.concatenate(parts, axis=0)
    return jnp.pad(rows, ((0, 16 - rows.shape[0]), (0, 0)))


def joined_rows(rows, count):
    high, middle, low = (rows[i * count : (i + 1) * count].astype(F32) for i in range(3))
    return high + middle + low


def per_device(frames, taps, w_query, w_key, w_value, q_gain, k_gain):
    count = lax.axis_size("tm")
    pos = lax.axis_index("tm")
    z = lax.axis_index("head").astype(jnp.int32)
    outer = (z == 0) | (z == 3)
    near, far = (z + 2) % 4, 3 - z
    side = outer.astype(jnp.int32)
    pair, second, third = z ^ 1, jnp.where(outer, near, far), jnp.where(outer, far, near)
    info = jnp.stack([side, z, pair, second, third])
    info_raw, info_end = jnp.stack([side, z, pair, second]), jnp.stack([side, third])
    hold = lax.optimization_barrier
    weights = (w_query, w_key, w_value)
    gains = (q_gain, k_gain)
    ups = [(i, i + 1) for i in range(count - 1)]
    downs = [(j, i) for i, j in ups]
    start = pos == 0

    def send(x, pairs):
        return lax.ppermute(x, "head", pairs)

    def mix_first(first, last, following, scales):
        return mix(
            jnp.where(start, jnp.zeros_like(first), first),
            jnp.where(start, first, last),
            jnp.where(start, last, following),
            scales,
        )

    def mix_second(first, last, following, preceding, scales):
        return mix(
            jnp.where(start, first, preceding),
            jnp.where(start, last, first),
            jnp.where(start, following, last),
            scales,
        )

    raw_first = send(frames[0], OUTWARD)
    following = lax.ppermute(frames[0], "tm", downs)
    mixed1 = mix_first(frames[0], frames[1], following, taps)
    last = jnp.concatenate([frames[1], split_rows(taps)], axis=0)
    later, last, mixed1 = hold((frames, last, mixed1))
    inward1, middle1 = send(mixed1, INWARD), send(mixed1, MIDDLE)
    raw_last = send(last, OUTWARD)
    later, raw_first = hold((later[1], raw_first))
    preceding = lax.ppermute(later, "tm", ups)
    mixed2 = mix_second(frames[0], frames[1], following, preceding, taps)
    raw_following = lax.ppermute(raw_first, "tm", downs)
    inward1, middle1 = hold((inward1, middle1))
    cross1, second1 = send(inward1, MIDDLE), send(middle1, OUTWARD)
    outer_taps = joined_rows(raw_last[later.shape[0] :], taps.shape[0])
    raw_last = raw_last[: later.shape[0]]
    raw_preceding = lax.ppermute(raw_last, "tm", ups)
    middle2, inward2 = send(mixed2, MIDDLE), send(mixed2, INWARD)
    level = (cross1, second1, raw_following, raw_preceding)
    cross1, second1, raw_following, raw_preceding = hold(level)
    third1 = send(cross1, OUTWARD)
    first1 = mix_first(raw_first, raw_last, raw_following, outer_taps)
    first2 = mix_second(raw_first, raw_last, raw_following, raw_preceding, outer_taps)
    middle2, first1, first2 = hold((middle2, first1, first2))
    cross2, second2 = send(inward2, MIDDLE), send(middle2, OUTWARD)

    sources1 = [(mixed1,), (inward1, first1), (middle1, second1), (cross1, third1)]
    kv1 = project(sources1, info, weights[1:], k_gain, after=(inward2, middle2), flops=10**10)
    q1 = project(sources1, info, weights[:1], q_gain, after=(kv1,), flops=10**9)
    beside = lax.ppermute(inward2[:16], "tm", [(i, i ^ 1) for i in range(count)])
    kv1, beside = hold((kv1, beside))
    third2 = send(cross2, OUTWARD)
    anchor = broadcast_first(kv1, "tm")
    cut = kv1.shape[2] // 2
    pieces = hold((kv1[:, :, :cut], kv1[:, :, cut:], anchor[0]))
    shift1 = [lax.ppermute(x, "tm", [(i, i + 1) for i in range(1, count - 1)]) for x in pieces[:2]]
    raw2 = project([(mixed2,), (inward2, first2), (middle2, second2)], info_raw, weights, after=(beside, q1), flops=10**10)
    q2, kv2 = finish(raw2, cross2, third2, info_end, weights, gains, 10**11)
    shift2 = lax.ppermute(kv2, "tm", [(0, 1)])
    anchor, shift1[0] = hold((anchor, shift1[0]))
    anchors = [[x] for x in anchor]
    late = jnp.where(start, 0, 1)
    odd = pos % 2
    result = attend([q1], anchors, odd, [[kv1], [kv2]], late, late)
    choice = jnp.minimum(pos, 1) + (pos == 1)
    return attend([q2], anchors, odd, [[kv1], shift1, [shift2]], choice, 1 - late, result)


def solution(mesh):
    placed = (
        P("tm", None, "head"),
        P(None, "head"),
        P(None, "head"),
        P(None, "head"),
        P(None, "head"),
        P("head"),
        P("head"),
    )
    return jax.shard_map(
        per_device, mesh=mesh, in_specs=placed, out_specs=P("tm", None, "head"), check_vma=False
    )
```
